32 devices in a mesh: tensor: 4 (over y, x), expert: 4 (over z), dp: 2 (over core).
Axes of the slice: x: 2, y: 2, z: 4, core: 2. Of those that a mesh axis runs over, the one named last changes fastest.
Arguments:
- tokens: bfloat16 [2048, 2048], P(('expert', 'dp')), may hold values from -6 to 6
- grad_output: bfloat16 [2048, 2048], P(('expert', 'dp')), may hold values from -4 to 4
- gate_prob: float32 [2048], P(('expert', 'dp')), may hold values from 0.3 to 1
- expert_index: int32 [2048, 1], P(('expert', 'dp')), may hold values from 0 to 3, as said below
- slot_index: int32 [2048, 1], P(('expert', 'dp')), may hold values from 0 to 127, as said below
- up_weight: bfloat16 [4, 2048, 4096], P('expert', 'dp', 'tensor'), may hold values from -0.125 to 0.125
- down_weight: bfloat16 [4, 2048, 4096], P('expert', 'dp', 'tensor'), may hold values from -0.09375 to 0.09375
Outputs:
- grad_tokens: bfloat16 [2048, 2048], P(('expert', 'dp'), 'tensor')
- grad_up: bfloat16 [4, 2048, 4096], P('expert', 'dp', 'tensor')
- grad_down: bfloat16 [4, 2048, 4096], P('expert', 'dp', 'tensor')
The draws below stay inside these ranges and needn't reach their ends.
Inputs may be any that keep to these rules, and one draw needn't show every extreme that they name: `expert_index`: within each aligned block of 256 rows, at most 128 rows choose one expert; in every block one expert is chosen by exactly 128 rows, and other experts by varying numbers. `slot_index`: slots of rows that choose the same expert within an aligned block of 256 rows are distinct.
All inputs are finite; a program needn't handle non-finite values.
Results may differ from the reference program's by a relative error of at most 0.015.
Values may be sent and summed in bfloat16 or wider, within the bound.
No kernel may reach another device: no remote copies, remote signals or barrier semaphores. Data moves between devices by JAX's collectives and lax.ppermute only.
A program may use at most 128 MiB of HBM per device.

```python
import jax
import jax.numpy as jnp
from jax import lax

D = 2048
H = 4096
TOP = 1
TOK_DEV = 256
EXPERTS = 4
CAP = 128
TOKENS = 2048
N_EXPERT = 4
N_DP = 2


def routing(key):
    busiest = jax.random.randint(jax.random.fold_in(key, 101), (), 0, EXPERTS).astype(jnp.int32)
    block_keys = jax.random.split(jax.random.fold_in(key, 102), TOKENS // TOK_DEV)
    pool = jnp.arange((EXPERTS - 1) * CAP, dtype=jnp.int32)
    own_slots = jnp.arange(CAP, dtype=jnp.int32)
    order = jnp.arange(TOK_DEV, dtype=jnp.int32)

    def per_block(block_key):
        first_key, second_key = jax.random.split(block_key)
        chosen = jax.random.permutation(first_key, pool)[:TOK_DEV - CAP]
        others = chosen // CAP
        others = (others + (others >= busiest).astype(jnp.int32)).astype(jnp.int32)
        expert_list = jnp.concatenate([jnp.zeros((CAP,), jnp.int32) + busiest, others])
        slot_list = jnp.concatenate([own_slots, (chosen % CAP).astype(jnp.int32)])
        shuffle = jax.random.permutation(second_key, order)
        return (expert_list[shuffle], slot_list[shuffle])
    expert_all, slot_all = jax.vmap(per_block)(block_keys)
    return (expert_all.reshape(TOKENS, TOP).astype(jnp.int32), slot_all.reshape(TOKENS, TOP).astype(jnp.int32))


def draw_expert_index(key, part):
    return routing(key)[0]


def draw_slot_index(key, part):
    return routing(key)[1]


def shard_levels(rng, shape, cuts, smallest, top_value):
    def one(position, parts):
        draws = jax.random.uniform(jax.random.fold_in(jax.random.fold_in(rng, 6), position), (parts,), jnp.float32, smallest / len(cuts), top_value / len(cuts))
        return jnp.repeat(jnp.exp(draws), shape[position] // parts).reshape((-1,) + (1,) * (len(shape) - position - 1))

    gain = one(*cuts[0])
    for cut in cuts[1:]:
        gain = gain * one(*cut)
    return gain


def scatter_about(own_key, shape, scale, bound, shards=(), kind=jnp.bfloat16):
    entries = jax.random.normal(own_key, shape, jnp.float32) * scale
    if len(shards) > 0:
        entries = shard_levels(own_key, shape, shards, -0.22, 0.18) * entries
    return jnp.clip(entries, min=-bound, max=bound).astype(kind)


def setup_inputs(seed: int = 0) -> dict:
    splits = jax.random.split(jax.random.key(seed), 8)
    return {
        "tokens": scatter_about(splits[0], (TOKENS, D), 1.0, 6.0, ((0, 8),)),
        "grad_output": scatter_about(splits[1], (TOKENS, D), 0.5, 4.0, ((0, 8),)),
        "gate_prob": jnp.clip(0.3 + 0.7 * jax.random.uniform(splits[2], (TOKENS,), jnp.float32) ** shard_levels(splits[2], (TOKENS,), ((0, 8),), -0.2, 0.2), 0.3, 1.0),
        "expert_index": draw_expert_index(jax.random.fold_in(splits[7], 71), 0),
        "slot_index": draw_slot_index(jax.random.fold_in(splits[7], 71), 0),
        "up_weight": scatter_about(splits[5], (EXPERTS, D, H), D ** -0.5, 0.125, ((0, 4), (1, 2), (2, 4))),
        "down_weight": scatter_about(splits[6], (EXPERTS, D, H), H ** -0.5, 0.09375, ((0, 4), (1, 2), (2, 4))),
    }


def expert_grads(token_rows, grad_rows, up_matrix, down_matrix):
    pre_act = jnp.dot(token_rows, up_matrix, preferred_element_type=jnp.float32)
    hidden = jax.nn.gelu(pre_act).astype(jnp.bfloat16)
    hidden_grad = jnp.dot(grad_rows, down_matrix, preferred_element_type=jnp.float32)
    slope_grad = jax.vjp(jax.nn.gelu, pre_act)[1](hidden_grad)[0].astype(jnp.bfloat16)
    input_part = lax.dot_general(slope_grad, up_matrix, (((1,), (1,)), ((), ())), preferred_element_type=jnp.float32)
    return (hidden, slope_grad, input_part)

def reference(tokens, grad_output, gate_prob, expert_index, slot_index, up_weight, down_weight):
    chosen_expert = expert_index[:, 0].astype(jnp.int32)
    chosen_slot = slot_index[:, 0].astype(jnp.int32)
    block_ids = jnp.arange(TOKENS, dtype=jnp.int32) // TOK_DEV
    source_rank = (block_ids // N_DP).astype(jnp.int32)
    replica = (block_ids % N_DP).astype(jnp.int32)
    scaled = (grad_output.astype(jnp.float32) * gate_prob[:, None]).astype(jnp.bfloat16)
    buf_shape = (EXPERTS, N_DP, N_EXPERT, CAP, D)
    token_buf = jnp.zeros(buf_shape, jnp.bfloat16).at[chosen_expert, replica, source_rank, chosen_slot].set(tokens)
    grad_buf = jnp.zeros(buf_shape, jnp.bfloat16).at[chosen_expert, replica, source_rank, chosen_slot].set(scaled)

    def per_expert(expert_items):
        token_part, grad_part, up_matrix, down_matrix = expert_items
        down_list = []
        up_list = []
        input_list = []
        for replica_id in range(N_DP):
            token_rows = token_part[replica_id].reshape(N_EXPERT * CAP, D)
            grad_rows = grad_part[replica_id].reshape(N_EXPERT * CAP, D)
            hidden, slope_grad, input_part = expert_grads(token_rows, grad_rows, up_matrix, down_matrix)
            down_term = jnp.dot(grad_rows.T, hidden, preferred_element_type=jnp.float32).astype(jnp.bfloat16)
            up_term = jnp.dot(token_rows.T, slope_grad, preferred_element_type=jnp.float32).astype(jnp.bfloat16)
            down_list.append(lax.optimization_barrier(down_term).astype(jnp.float32))
            up_list.append(lax.optimization_barrier(up_term).astype(jnp.float32))
            input_list.append(input_part.astype(jnp.bfloat16).reshape(N_EXPERT, CAP, D))
        return (sum(up_list).astype(jnp.bfloat16), sum(down_list).astype(jnp.bfloat16), jnp.stack(input_list))
    grad_up, grad_down, input_buf = lax.map(per_expert, (token_buf, grad_buf, up_weight, down_weight))
    grad_tokens = input_buf[chosen_expert, replica, source_rank, chosen_slot]
    return (grad_tokens, grad_up, grad_down)
```

```python
import jax
import jax.numpy as jnp
from jax import lax
from jax.sharding import PartitionSpec as P

F32 = jnp.float32
BF16 = jnp.bfloat16


def dot(lhs, rhs, contract):
    return lax.dot_general(lhs, rhs, ((contract[:1], contract[1:]), ((), ())), preferred_element_type=F32)


def xor_order(blocks, shift):
    low = (shift & 1) == 1
    high = (shift & 2) == 2
    once = [jnp.where(low, blocks[i ^ 1], blocks[i]) for i in range(4)]
    return [jnp.where(high, once[i ^ 2], once[i]) for i in range(4)]


def local(tokens, grad_output, gate_prob, expert_index, slot_index, up_weight, down_weight):
    experts = lax.axis_size("expert")
    tensor_size = lax.axis_size("tensor")
    e = lax.axis_index("expert")
    t = lax.axis_index("tensor")
    p = lax.axis_index("dp")
    tok_count, width = tokens.shape
    capacity = 2 * tok_count // experts
    share = width // tensor_size
    half = width // 2
    order = t ^ (2 * p)

    def swap(x):
        return lax.ppermute(x, "dp", [(0, 1), (1, 0)])

    def across(x, j):
        return lax.ppermute(x, "tensor", [(i, i ^ j) for i in range(tensor_size)])

    def shift(x, k):
        return lax.ppermute(x, "expert", [(i, (i + k) % experts) for i in range(experts)])

    up_own, down_own = up_weight[0], down_weight[0]
    up_other, down_other = swap(up_own), swap(down_own)

    position = expert_index[:, 0] * capacity + slot_index[:, 0]
    scaled = (grad_output.astype(F32) * gate_prob[:, None]).astype(BF16)

    def onehot(first, rows):
        ids = lax.broadcasted_iota(jnp.int32, (rows, tok_count), 0) + first
        return (ids == position[None, :]).astype(BF16)

    def place(hot, columns):
        return dot(hot, columns, (1, 0)).astype(BF16)

    def quarter(x):
        return lax.dynamic_slice_in_dim(x, t * share, share, 1)

    def halves(x):
        return (
            lax.dynamic_slice_in_dim(x, p * half, half, 1),
            lax.dynamic_slice_in_dim(x, (1 - p) * half, half, 1),
        )

    def spread(tok, grad):
        tok_x, tok_y = across(tok, 1), across(tok, 2)
        grad_x, grad_y = across(grad, 1), across(grad, 2)
        tok_d, grad_d = across(tok_y, 1), across(grad_x, 2)
        tok_all = xor_order([tok, tok_x, tok_y, tok_d], order)
        grad_all = xor_order([grad, grad_x, grad_y, grad_d], order)
        join = lambda a: (jnp.concatenate(a[:2], 1), jnp.concatenate(a[2:], 1))
        return join(tok_all), join(grad_all)

    def expert_rows(tok, grad):
        pre = dot(tok[0], up_own, (1, 0)) + dot(tok[1], up_other, (1, 0))
        hidden = jax.nn.gelu(pre).astype(BF16)
        hidden_grad = dot(grad[0], down_own, (1, 0)) + dot(grad[1], down_other, (1, 0))
        slope = jax.vjp(jax.nn.gelu, pre)[1](hidden_grad)[0].astype(BF16)
        own = dot(slope, up_own, (1, 1)).astype(BF16)
        other = dot(slope, up_other, (1, 1)).astype(BF16)
        parts = [own[:, :share], own[:, share:], other[:, :share], other[:, share:]]
        sends = xor_order(parts, order)
        total = sends[0].astype(F32)
        for j in (1, 2, 3):
            total = total + across(sends[j], j).astype(F32)
        return hidden, slope, total.astype(BF16)

    tok_q, grad_q = quarter(tokens), quarter(scaled)
    chunks = []
    if experts == 4:
        hots = [onehot(((e + k) % experts) * capacity, capacity) for k in range(experts)]
        rows = []
        for k in (1, 3, 2):
            rows.append((k, shift(place(hots[k], tok_q), k), shift(place(hots[k], grad_q), k)))
        chunks.append(
            (0, tuple(place(hots[0], x) for x in halves(tokens)), tuple(place(hots[0], x) for x in halves(scaled)))
        )
        for k, tok, grad in rows:
            chunks.append((k,) + spread(tok, grad))
    else:
        hots = [onehot(0, experts * capacity)]

        def exchange(x):
            placed = place(hots[0], x).reshape(experts, capacity, share)
            moved = lax.all_to_all(placed, "expert", split_axis=0, concat_axis=0, tiled=True)
            return moved.reshape(experts * capacity, share)

        chunks.append((0,) + spread(exchange(tok_q), exchange(grad_q)))

    grad_tokens = jnp.zeros((tok_count, share), F32)
    hiddens, slopes = [], []
    for k, tok, grad in chunks:
        hidden, slope, total = expert_rows(tok, grad)
        hiddens.append(hidden)
        slopes.append(slope)
        if experts == 4:
            back = shift(total, -k) if k else total
        else:
            back = lax.all_to_all(
                total.reshape(experts, capacity, share), "expert", split_axis=0, concat_axis=0, tiled=True
            ).reshape(experts * capacity, share)
        grad_tokens = grad_tokens + dot(hots[k], back, (0, 0))

    def weight_grad(index, outs):
        own = jnp.concatenate([c[index][0] for c in chunks], 0)
        other = jnp.concatenate([c[index][1] for c in chunks], 0)
        out = jnp.concatenate(outs, 0)
        got = swap(dot(other, out, (0, 0)).astype(BF16))
        mine = dot(own, out, (0, 0)).astype(BF16)
        return (mine.astype(F32) + got.astype(F32)).astype(BF16)[None]

    grad_down = weight_grad(2, hiddens)
    grad_up = weight_grad(1, slopes)
    return grad_tokens.astype(BF16), grad_up, grad_down


def solution(mesh):
    placed = (
        P(("expert", "dp"), None),
        P(("expert", "dp"), None),
        P(("expert", "dp")),
        P(("expert", "dp"), None),
        P(("expert", "dp"), None),
        P("expert", "dp", "tensor"),
        P("expert", "dp", "tensor"),
    )
    return jax.shard_map(
        local,
        mesh=mesh,
        in_specs=placed,
        out_specs=(
            P(("expert", "dp"), "tensor"),
            P("expert", "dp", "tensor"),
            P("expert", "dp", "tensor"),
        ),
        check_vma=False,
    )
```

```python
import functools

import jax
import jax.numpy as jnp
from jax import lax
from jax.experimental import pallas as pl
from jax.experimental.pallas import tpu as pltpu
from jax.sharding import PartitionSpec as P

F32 = jnp.float32
BF16 = jnp.bfloat16
I32 = jnp.int32
ANY = pl.BlockSpec(memory_space=pl.ANY)
VMEM = pl.BlockSpec(memory_space=pltpu.VMEM)
SMEM = pl.BlockSpec(memory_space=pltpu.SMEM)
LIMIT = 44 * 2**20


def dot(lhs, rhs, left=1, right=0):
    return lax.dot_general(lhs, rhs, (((left,), (right,)), ((), ())), preferred_element_type=F32)


def hits(position, first, rows):
    ids = lax.broadcasted_iota(I32, (rows, position.shape[1]), 0) + first
    return ids == position


def gate_of(hit, gate):
    return jnp.sum(jnp.where(hit, gate, 0.0), axis=1, keepdims=True)


def place_kernel(spans, where, position, gate, tok, grad, *outs):
    share = tok.shape[1]
    for k, (rows, out) in enumerate(zip(spans, outs)):
        hit = hits(position[...], where[k], rows)
        hot = hit.astype(BF16)
        out[:, :share] = dot(hot, tok[...]).astype(BF16)
        out[:, share:] = (dot(hot, grad[...]) * gate_of(hit, gate[...])).astype(BF16)


def place(spans, firsts, quarter, position, gate, tokens, grad_output, share):
    count = tokens.shape[0]
    where = jnp.stack(list(firsts) + [quarter]).astype(I32)
    column = lambda i, w: (0, w[len(spans)])
    full = lambda shape: pl.BlockSpec(shape, lambda i, w: (0, 0))
    return pl.pallas_call(
        functools.partial(place_kernel, spans),
        out_shape=[jax.ShapeDtypeStruct((rows, 2 * share), BF16) for rows in spans],
        grid_spec=pltpu.PrefetchScalarGridSpec(
            num_scalar_prefetch=1,
            grid=(1,),
            in_specs=[
                full((1, count)),
                full((1, count)),
                pl.BlockSpec((count, share), column),
                pl.BlockSpec((count, share), column),
            ],
            out_specs=[full((rows, 2 * share)) for rows in spans],
        ),
        compiler_params=pltpu.CompilerParams(vmem_limit_bytes=LIMIT),
        cost_estimate=pl.CostEstimate(
            flops=4 * sum(spans) * count * share, bytes_accessed=4 * (count + sum(spans)) * share, transcendentals=0
        ),
        name="place_rows",
    )(where, position, gate, tokens, grad_output)


def gelu_parts(pre):
    c = 0.7978845608028654
    square = pre * pre
    th = jnp.tanh(c * (pre + 0.044715 * (pre * square)))
    half = 0.5 * (1.0 + th)
    return pre * half, half + 0.5 * pre * (1.0 - th * th) * (c + (3 * 0.044715 * c) * square)


def expert_kernel(own_rows, chunk_rows, base, aliased, where, *refs):
    refs = list(refs)
    take = lambda n: [refs.pop(0) for _ in range(n)]
    if own_rows:
        position, gate, tokens, grad_output = take(4)
    chunks = [take(5) for _ in chunk_rows]
    weights = take(4)
    if aliased:
        take(4)
    tok_out, grad_out, hidden_out, slope_out = take(4)
    blocks = take(4)
    tok, grad, up, down, hidden, slope, back = take(7)
    if own_rows:
        tokens_in, grad_in = take(2)
    (sem,) = take(1)
    rows, width = tok.shape
    half, share = width // 2, width // 4
    order, first, half_start = where[0], where[1], where[2]
    count = [0]

    def copy(src, dst):
        c = pltpu.make_async_copy(src, dst, sem.at[count[0]])
        count[0] += 1
        c.start()
        return c

    waits = []
    if own_rows:
        other_start = half - half_start
        for src, dst in ((tokens, tokens_in), (grad_output, grad_in)):
            for start, place_at in ((half_start, 0), (other_start, half)):
                start = pl.multiple_of(start, half)
                waits.append(copy(src.at[:, pl.ds(start, half)], dst.at[:, pl.ds(place_at, half)]))
    at = own_rows
    for (z, x, y, tok_d, grad_d), n in zip(chunks, chunk_rows):
        tok_slots = [r.at[:, pl.ds(0, share)] for r in (z, x, y)] + [tok_d]
        grad_slots = [r.at[:, pl.ds(share, share)] for r in (z, x, y)] + [grad_d]
        for j in range(4):
            columns = pl.ds(pl.multiple_of((order ^ j) * share, share), share)
            waits.append(copy(tok_slots[j], tok.at[pl.ds(at, n), columns]))
            waits.append(copy(grad_slots[j], grad.at[pl.ds(at, n), columns]))
        at += n
    up_own, up_other, down_own, down_other = weights
    up_waits = [copy(up_own, up.at[pl.ds(0, half), :]), copy(up_other, up.at[pl.ds(half, half), :])]
    down_waits = [copy(down_own, down.at[pl.ds(0, half), :]), copy(down_other, down.at[pl.ds(half, half), :])]
    for w in waits:
        w.wait()
    if own_rows:
        hit = hits(position[...], first, own_rows)
        hot = hit.astype(BF16)
        tok[:own_rows, :] = dot(hot, tokens_in[...]).astype(BF16)
        grad[:own_rows, :] = (dot(hot, grad_in[...]) * gate_of(hit, gate[...])).astype(BF16)
    outs = [copy(tok, tok_out.at[pl.ds(base, rows), :]), copy(grad, grad_out.at[pl.ds(base, rows), :])]
    for w in up_waits + down_waits:
        w.wait()
    hid = hidden.shape[1]
    step = 256
    for n in range(0, hid, step):
        pre = dot(tok[...], up[:, n : n + step])
        hidden_grad = dot(grad[...], down[:, n : n + step])
        act, deriv = gelu_parts(pre)
        hidden[:, n : n + step] = act.astype(BF16)
        slope[:, n : n + step] = (hidden_grad * deriv).astype(BF16)
    outs.append(copy(hidden, hidden_out.at[pl.ds(base, rows), :]))
    outs.append(copy(slope, slope_out.at[pl.ds(base, rows), :]))
    for n in range(4):
        back[n] = dot(slope[...], up[pl.ds(n * share, share), :], 1, 1).astype(BF16)
    for j in range(4):
        outs.append(copy(back.at[order ^ j], blocks[j]))
    for w in outs:
        w.wait()


def expert_rows(where, own, chunks, weights, total_rows, base, previous):
    own_rows = own[0] if own else 0
    chunk_rows = [c[0].shape[0] for c in chunks]
    rows = own_rows + sum(chunk_rows)
    half, hid = weights[0].shape
    width, share = 2 * half, half // 2
    operands = [where]
    specs = [SMEM]
    if own:
        operands += own[1:]
        specs += [VMEM, VMEM, ANY, ANY]
    for c in chunks:
        operands += c
        specs += [ANY] * 5
    operands += weights
    specs += [ANY] * 4
    aliases = {}
    if previous:
        aliases = {len(operands) + i: i for i in range(4)}
        operands += previous
        specs += [ANY] * 4
    shape = lambda *s: jax.ShapeDtypeStruct(s, BF16)
    buf = lambda *s: pltpu.VMEM(s, BF16)
    scratch = [
        buf(rows, width), buf(rows, width), buf(width, hid), buf(width, hid),
        buf(rows, hid), buf(rows, hid), buf(4, rows, share),
    ]
    copies = 4 + 8 * len(chunks) + 8
    if own:
        count = own[3].shape[0]
        scratch += [buf(count, width), buf(count, width)]
        copies += 4
    scratch.append(pltpu.SemaphoreType.DMA((copies,)))
    out = pl.pallas_call(
        functools.partial(expert_kernel, own_rows, chunk_rows, base, bool(previous)),
        out_shape=[shape(total_rows, width)] * 2 + [shape(total_rows, hid)] * 2 + [shape(rows, share)] * 4,
        in_specs=specs,
        out_specs=[ANY] * 8,
        scratch_shapes=scratch,
        input_output_aliases=aliases,
        compiler_params=pltpu.CompilerParams(vmem_limit_bytes=LIMIT),
        cost_estimate=pl.CostEstimate(
            flops=6 * rows * width * hid, bytes_accessed=4 * width * hid + 8 * rows * width, transcendentals=rows * hid
        ),
        name="expert_rows",
    )(*operands)
    return list(out[:4]), list(out[4:])


def unplace_kernel(spans, where, position, *refs):
    out = refs[-1]
    total = None
    for k, (rows, back) in enumerate(zip(spans, refs[:-1])):
        hot = hits(position[...], where[k], rows).astype(BF16)
        part = dot(hot, back[...], 0, 0)
        total = part if total is None else total + part
    out[...] = total.astype(BF16)


def unplace(firsts, position, backs):
    spans = [b.shape[0] for b in backs]
    count, share = position.shape[1], backs[0].shape[1]
    return pl.pallas_call(
        functools.partial(unplace_kernel, spans),
        out_shape=jax.ShapeDtypeStruct((count, share), BF16),
        in_specs=[SMEM] + [VMEM] * (1 + len(backs)),
        out_specs=VMEM,
        compiler_params=pltpu.CompilerParams(vmem_limit_bytes=LIMIT),
        cost_estimate=pl.CostEstimate(
            flops=2 * sum(spans) * count * share, bytes_accessed=2 * (count + sum(spans)) * share, transcendentals=0
        ),
        name="unplace_rows",
    )(jnp.stack(firsts).astype(I32), position, *backs)


def local(tokens, grad_output, gate_prob, expert_index, slot_index, up_weight, down_weight):
    experts = lax.axis_size("expert")
    tensor_size = lax.axis_size("tensor")
    e = lax.axis_index("expert")
    t = lax.axis_index("tensor")
    p = lax.axis_index("dp")
    tok_count, width = tokens.shape
    capacity = 2 * tok_count // experts
    share = width // tensor_size
    half = width // 2
    where = jnp.stack([t ^ (2 * p), e * capacity, p * half]).astype(I32)

    def swap(x):
        return lax.ppermute(x, "dp", [(0, 1), (1, 0)])

    def across(x, j):
        return lax.ppermute(x, "tensor", [(i, i ^ j) for i in range(tensor_size)])

    def shift(x, k):
        return lax.ppermute(x, "expert", [(i, (i + k) % experts) for i in range(experts)])

    def spread(rows):
        x, y = across(rows, 1), across(rows, 2)
        return [rows, x, y, across(y[:, :share], 1), across(x[:, share:], 2)]

    def collect(blocks):
        got = [across(blocks[j], j) for j in (1, 2, 3)]

        def total(lo, hi):
            terms = [b[lo:hi].astype(F32) for b in [blocks[0]] + got]
            return (terms[0] + terms[1] + (terms[2] + terms[3])).astype(BF16)

        return total

    up_own, down_own = up_weight[0], down_weight[0]
    weights = [up_own, swap(up_own), down_own, swap(down_own)]
    position = (expert_index * capacity + slot_index).reshape(1, tok_count)
    gate = gate_prob.reshape(1, tok_count)

    if experts == 4:
        shifts = (1, 3, 2)
        firsts = [((e + k) % experts) * capacity for k in shifts]
        sends = place([capacity] * 3, firsts, t, position, gate, tokens, grad_output, share)
        chunks = [spread(shift(rows, k)) for rows, k in zip(sends, shifts)]
        own = [capacity, position, gate, tokens, grad_output]
        kept, blocks = expert_rows(where, own, chunks[:2], weights, 4 * capacity, 0, None)
        total = collect(blocks)
        backs = [total(0, capacity)]
        backs += [shift(total(i * capacity, (i + 1) * capacity), -k) for i, k in ((1, 1), (2, 3))]
        kept, blocks = expert_rows(where, None, chunks[2:], weights, 4 * capacity, 3 * capacity, kept)
        backs.append(shift(collect(blocks)(0, capacity), -2))
        places = [e * capacity] + firsts
    else:
        rows = experts * capacity

        def exchange(x):
            moved = lax.all_to_all(
                x.reshape(experts, capacity, x.shape[1]), "expert", split_axis=0, concat_axis=0, tiled=True
            )
            return moved.reshape(rows, x.shape[1])

        (send,) = place([rows], [jnp.int32(0)], t, position, gate, tokens, grad_output, share)
        kept, blocks = expert_rows(where, None, [spread(exchange(send))], weights, rows, 0, None)
        backs = [exchange(collect(blocks)(0, rows))]
        places = [jnp.int32(0)]

    grad_tokens = unplace(places, position, backs)
    tok_rows, grad_rows, hidden, slope = kept

    def weight_grad(rows, out):
        got = swap(dot(rows[:, half:], out, 0, 0).astype(BF16))
        mine = dot(rows[:, :half], out, 0, 0).astype(BF16)
        return (mine.astype(F32) + got.astype(F32)).astype(BF16)[None]

    return grad_tokens, weight_grad(tok_rows, slope), weight_grad(grad_rows, hidden)


def solution(mesh):
    placed = (
        P(("expert", "dp"), None),
        P(("expert", "dp"), None),
        P(("expert", "dp")),
        P(("expert", "dp"), None),
        P(("expert", "dp"), None),
        P("expert", "dp", "tensor"),
        P("expert", "dp", "tensor"),
    )
    return jax.shard_map(
        local,
        mesh=mesh,
        in_specs=placed,
        out_specs=(
            P(("expert", "dp"), "tensor"),
            P("expert", "dp", "tensor"),
            P("expert", "dp", "tensor"),
        ),
        check_vma=False,
    )
```

```python
import functools

import jax
import jax.numpy as jnp
from jax import lax
from jax.experimental import pallas as pl
from jax.experimental.pallas import tpu as pltpu
from jax.sharding import PartitionSpec as P

F32 = jnp.float32
BF16 = jnp.bfloat16
I32 = jnp.int32
ANY = pl.BlockSpec(memory_space=pl.ANY)
VMEM = pl.BlockSpec(memory_space=pltpu.VMEM)
SMEM = pl.BlockSpec(memory_space=pltpu.SMEM)
HBM = pl.BlockSpec(memory_space=pltpu.HBM)
LIMIT = 22 * 2**20


def dot(lhs, rhs, left=1, right=0):
    return lax.dot_general(lhs, rhs, (((left,), (right,)), ((), ())), preferred_element_type=F32)


def hits(position, first, rows):
    ids = lax.broadcasted_iota(I32, (rows, position.shape[1]), 0) + first
    return ids == position


def gate_of(hit, gate):
    return jnp.sum(jnp.where(hit, gate, 0.0), axis=1, keepdims=True)


def place_kernel(spans, where, position, gate, tokens, grad_output, *refs):
    outs, (tok, grad, sem) = refs[: len(spans)], refs[len(spans) :]
    share = tok.shape[1]
    columns = pl.ds(pl.multiple_of(where[len(spans)] * share, share), share)
    first = pltpu.make_async_copy(tokens.at[:, columns], tok, sem.at[0])
    second = pltpu.make_async_copy(grad_output.at[:, columns], grad, sem.at[1])
    first.start()
    second.start()
    found = [hits(position[...], where[k], rows) for k, rows in enumerate(spans)]
    first.wait()
    second.wait()
    for hit, out in zip(found, outs):
        hot = hit.astype(BF16)
        out[:, :share] = dot(hot, tok[...]).astype(BF16)
        out[:, share:] = (dot(hot, grad[...]) * gate_of(hit, gate[...])).astype(BF16)


def place(spans, firsts, quarter, position, gate, tokens, grad_output, share):
    count = tokens.shape[0]
    where = jnp.stack(list(firsts) + [quarter]).astype(I32)
    return pl.pallas_call(
        functools.partial(place_kernel, spans),
        out_shape=[jax.ShapeDtypeStruct((rows, 2 * share), BF16) for rows in spans],
        in_specs=[SMEM, VMEM, VMEM, HBM, HBM],
        out_specs=[VMEM] * len(spans),
        scratch_shapes=[
            pltpu.VMEM((count, share), BF16), pltpu.VMEM((count, share), BF16), pltpu.SemaphoreType.DMA((2,))
        ],
        compiler_params=pltpu.CompilerParams(vmem_limit_bytes=54 * 2**20),
        cost_estimate=pl.CostEstimate(
            flops=4 * sum(spans) * count * share, bytes_accessed=4 * (count + sum(spans)) * share, transcendentals=0
        ),
        name="place_rows",
    )(where, position, gate, tokens, grad_output)


def gelu_parts(pre):
    c = 0.7978845608028654
    square = pre * pre
    th = jnp.tanh(c * (pre + 0.044715 * (pre * square)))
    half = 0.5 * (1.0 + th)
    return pre * half, half + 0.5 * pre * (1.0 - th * th) * (c + (3 * 0.044715 * c) * square)


def expert_kernel(own_rows, chunk_rows, base, block_base, aliased, where, *refs):
    refs = list(refs)
    take = lambda n: [refs.pop(0) for _ in range(n)]
    if own_rows:
        position, gate, tokens, grad_output = take(4)
    chunks = [take(5) for _ in chunk_rows]
    up_own, up_other, down_own, down_other = take(4)
    take(aliased)
    tok_out, grad_out, hidden_out, slope_out = take(4)
    blocks = take(4)
    tok, grad, hidden, slope, back = take(5)
    if own_rows:
        tokens_in, grad_in = take(2)
    (sem,) = take(1)
    rows, width = tok.shape
    half, share = width // 2, width // 4
    order, first, half_start = where[0], where[1], where[2]
    count = [0]

    def copy(src, dst):
        c = pltpu.make_async_copy(src, dst, sem.at[count[0]])
        count[0] += 1
        c.start()
        return c

    if own_rows:
        waits = []
        other_start = half - half_start
        for src, dst in ((tokens, tokens_in), (grad_output, grad_in)):
            for start, place_at in ((half_start, 0), (other_start, half)):
                start = pl.multiple_of(start, half)
                waits.append(copy(src.at[:, pl.ds(start, half)], dst.at[:, pl.ds(place_at, half)]))
        hit = hits(position[...], first, own_rows)
        hot = hit.astype(BF16)
        for w in waits:
            w.wait()
        tok[:own_rows, :] = dot(hot, tokens_in[...]).astype(BF16)
        grad[:own_rows, :] = (dot(hot, grad_in[...]) * gate_of(hit, gate[...])).astype(BF16)
    at = own_rows
    for (z, x, y, tok_d, grad_d), n in zip(chunks, chunk_rows):
        for j in range(4):
            columns = pl.ds(pl.multiple_of((order ^ j) * share, share), share)
            tok[at : at + n, columns] = (z, x, y)[j][:, :share] if j < 3 else tok_d[...]
            grad[at : at + n, columns] = (z, x, y)[j][:, share:] if j < 3 else grad_d[...]
        at += n
    outs = [copy(tok, tok_out.at[pl.ds(base, rows), :]), copy(grad, grad_out.at[pl.ds(base, rows), :])]
    hid = hidden.shape[1]
    step = 256
    for n in range(0, hid, step):
        cols = slice(n, n + step)
        pre = dot(tok[:, :half], up_own[:, cols]) + dot(tok[:, half:], up_other[:, cols])
        hidden_grad = dot(grad[:, :half], down_own[:, cols]) + dot(grad[:, half:], down_other[:, cols])
        act, deriv = gelu_parts(pre)
        hidden[:, cols] = act.astype(BF16)
        slope[:, cols] = (hidden_grad * deriv).astype(BF16)
    outs.append(copy(hidden, hidden_out.at[pl.ds(base, rows), :]))
    outs.append(copy(slope, slope_out.at[pl.ds(base, rows), :]))
    for n in range(4):
        source = (up_own, up_other)[n // 2]
        lo = (n % 2) * share
        back[n] = dot(slope[...], source[lo : lo + share, :], 1, 1).astype(BF16)
    for j in range(4):
        outs.append(copy(back.at[order ^ j], blocks[j].at[pl.ds(block_base, rows), :]))
    for w in outs:
        w.wait()


def expert_rows(where, own, chunks, weights, total_rows, base, block_rows, block_base, kept, blocks):
    own_rows = own[0] if own else 0
    chunk_rows = [c[0].shape[0] for c in chunks]
    rows = own_rows + sum(chunk_rows)
    half, hid = weights[0].shape
    width, share = 2 * half, half // 2
    operands = [where]
    specs = [SMEM]
    if own:
        operands += own[1:]
        specs += [VMEM, VMEM, HBM, HBM]
    for c in chunks:
        operands += c
        specs += [VMEM] * 5
    operands += weights
    specs += [VMEM] * 4
    aliases = {}
    for first, previous in ((0, kept), (4, blocks)):
        if previous:
            aliases.update({len(operands) + i: first + i for i in range(4)})
            operands += previous
            specs += [ANY] * 4
    shape = lambda *s: jax.ShapeDtypeStruct(s, BF16)
    buf = lambda *s: pltpu.VMEM(s, BF16)
    scratch = [buf(rows, width), buf(rows, width), buf(rows, hid), buf(rows, hid), buf(4, rows, share)]
    copies = 8
    if own:
        count = own[3].shape[0]
        scratch += [buf(count, width), buf(count, width)]
        copies += 4
    scratch.append(pltpu.SemaphoreType.DMA((copies,)))
    out = pl.pallas_call(
        functools.partial(expert_kernel, own_rows, chunk_rows, base, block_base, len(aliases)),
        out_shape=[shape(total_rows, width)] * 2 + [shape(total_rows, hid)] * 2 + [shape(block_rows, share)] * 4,
        in_specs=specs,
        out_specs=[ANY] * 8,
        scratch_shapes=scratch,
        input_output_aliases=aliases,
        compiler_params=pltpu.CompilerParams(vmem_limit_bytes=LIMIT + rows * 2**15),
        cost_estimate=pl.CostEstimate(
            flops=6 * rows * width * hid, bytes_accessed=4 * width * hid + 8 * rows * width, transcendentals=rows * hid
        ),
        name="expert_rows",
    )(*operands)
    return list(out[:4]), list(out[4:])


def unplace_kernel(spans, where, position, *refs):
    out = refs[-1]
    total = None
    for k, (rows, back) in enumerate(zip(spans, refs[:-1])):
        hot = hits(position[...], where[k], rows).astype(BF16)
        part = dot(hot, back[...], 0, 0)
        total = part if total is None else total + part
    out[...] = total.astype(BF16)


def unplace(firsts, position, backs):
    spans = [b.shape[0] for b in backs]
    count, share = position.shape[1], backs[0].shape[1]
    return pl.pallas_call(
        functools.partial(unplace_kernel, spans),
        out_shape=jax.ShapeDtypeStruct((count, share), BF16),
        in_specs=[SMEM] + [VMEM] * (1 + len(backs)),
        out_specs=VMEM,
        compiler_params=pltpu.CompilerParams(vmem_limit_bytes=LIMIT),
        cost_estimate=pl.CostEstimate(
            flops=2 * sum(spans) * count * share, bytes_accessed=2 * (count + sum(spans)) * share, transcendentals=0
        ),
        name="unplace_rows",
    )(jnp.stack(firsts).astype(I32), position, *backs)


def outer_kernel(rows, out, *refs):
    total = dot(rows[...], out[...], 0, 0).astype(BF16)
    if len(refs) > 1:
        total = (total.astype(F32) + refs[0][...].astype(F32)).astype(BF16)
    refs[-1][...] = total


def outer(rows, out, which, got):
    count, width = rows.shape
    hid = out.shape[1]
    half, block = width // 2, width // 8
    steps = half // block
    tile = pl.BlockSpec((block, hid), lambda i: (i, 0))
    operands = [rows, out] + ([] if got is None else [got])
    return pl.pallas_call(
        outer_kernel,
        out_shape=jax.ShapeDtypeStruct((half, hid), BF16),
        grid=(steps,),
        in_specs=[
            pl.BlockSpec((count, block), lambda i: (0, which * steps + i)),
            pl.BlockSpec((count, hid), lambda i: (0, 0)),
        ]
        + [tile] * (len(operands) - 2),
        out_specs=tile,
        compiler_params=pltpu.CompilerParams(vmem_limit_bytes=LIMIT),
        cost_estimate=pl.CostEstimate(
            flops=2 * count * half * hid, bytes_accessed=2 * (count * (half + hid) + half * hid), transcendentals=0
        ),
        name="weight_grad",
    )(*operands)


def local(tokens, grad_output, gate_prob, expert_index, slot_index, up_weight, down_weight):
    experts = lax.axis_size("expert")
    tensor_size = lax.axis_size("tensor")
    e = lax.axis_index("expert")
    t = lax.axis_index("tensor")
    p = lax.axis_index("dp")
    tok_count, width = tokens.shape
    capacity = 2 * tok_count // experts
    share = width // tensor_size
    half = width // 2
    where = jnp.stack([t ^ (2 * p), e * capacity, p * half]).astype(I32)

    def swap(x):
        return lax.ppermute(x, "dp", [(0, 1), (1, 0)])

    def across(x, j):
        return lax.ppermute(x, "tensor", [(i, i ^ j) for i in range(tensor_size)])

    def shift(x, k):
        return lax.ppermute(x, "expert", [(i, (i + k) % experts) for i in range(experts)])

    def after(x, *others):
        return lax.optimization_barrier((x,) + others)[0]

    def spread(rows, *before):
        x, y = across(rows, 1), across(rows, 2)
        if before:
            x, y = after(x, *before), after(y, *before)
        return [rows, x, y, across(y[:, :share], 1), across(x[:, share:], 2)]

    def collect(blocks):
        got = [across(blocks[j], j) for j in (1, 2, 3)]

        def total(lo, hi):
            terms = [b[lo:hi].astype(F32) for b in [blocks[0]] + got]
            return (terms[0] + terms[1] + (terms[2] + terms[3])).astype(BF16)

        return total, got

    position = (expert_index * capacity + slot_index).reshape(1, tok_count)
    gate = gate_prob.reshape(1, tok_count)
    up_own, down_own = up_weight[0], down_weight[0]

    weights = [up_own, swap(up_own), down_own, swap(down_own)]

    if experts == 4:
        shifts = (1, 3, 2)
        firsts = [((e + k) % experts) * capacity for k in shifts]
        sends = place([capacity] * 3, firsts, t, position, gate, tokens, grad_output, share)
        one, three = shift(sends[0], 1), shift(sends[1], 3)
        own = [capacity, position, gate, tokens, grad_output]
        kept, blocks = expert_rows(where, own, [], weights, 4 * capacity, 0, capacity, 0, None, None)
        two = shift(after(sends[2], blocks[0]), 2)
        backs = [collect(blocks)[0](0, capacity)]
        near = spread(jnp.concatenate([after(one, blocks[0]), three], 0), backs[0])
        far = spread(two)
        kept, blocks = expert_rows(
            where, None, [near], weights, 4 * capacity, capacity, 2 * capacity, 0, kept, None
        )
        total, got = collect(blocks)
        backs += [shift(total(i * capacity, (i + 1) * capacity), -k) for i, k in ((0, 1), (1, 3))]
        kept, blocks = expert_rows(where, None, [far], weights, 4 * capacity, 3 * capacity, capacity, 0, kept, None)
        last, got_last = collect(blocks)
        got += got_last
        backs.append(shift(last(0, capacity), -2))
        places = [e * capacity] + firsts
    else:
        rows = experts * capacity

        def exchange(x):
            moved = lax.all_to_all(
                x.reshape(experts, capacity, x.shape[1]), "expert", split_axis=0, concat_axis=0, tiled=True
            )
            return moved.reshape(rows, x.shape[1])

        (send,) = place([rows], [jnp.int32(0)], t, position, gate, tokens, grad_output, share)
        kept, blocks = expert_rows(where, None, [spread(exchange(send))], weights, rows, 0, rows, 0, None, None)
        total, got = collect(blocks)
        backs = [exchange(total(0, rows))]
        places = [jnp.int32(0)]

    grad_tokens = unplace(places, position, backs)
    tok_rows, grad_rows, hidden, slope = kept

    hidden, slope = after(hidden, *got), after(slope, *got)
    got_up = swap(outer(tok_rows, slope, 1, None))
    got_down = swap(outer(grad_rows, hidden, 1, None))
    return grad_tokens, outer(tok_rows, slope, 0, got_up)[None], outer(grad_rows, hidden, 0, got_down)[None]


def solution(mesh):
    placed = (
        P(("expert", "dp"), None),
        P(("expert", "dp"), None),
        P(("expert", "dp")),
        P(("expert", "dp"), None),
        P(("expert", "dp"), None),
        P("expert", "dp", "tensor"),
        P("expert", "dp", "tensor"),
    )
    return jax.shard_map(
        local,
        mesh=mesh,
        in_specs=placed,
        out_specs=(
            P(("expert", "dp"), "tensor"),
            P("expert", "dp", "tensor"),
            P("expert", "dp", "tensor"),
        ),
        check_vma=False,
    )
```

```python
import functools

import jax
import jax.numpy as jnp
from jax import lax
from jax.experimental import pallas as pl
from jax.experimental.pallas import tpu as pltpu
from jax.sharding import PartitionSpec as P

F32 = jnp.float32
BF16 = jnp.bfloat16
I32 = jnp.int32
ANY = pl.BlockSpec(memory_space=pl.ANY)
VMEM = pl.BlockSpec(memory_space=pltpu.VMEM)
SMEM = pl.BlockSpec(memory_space=pltpu.SMEM)
HBM = pl.BlockSpec(memory_space=pltpu.HBM)
LIMIT = 22 * 2**20


def dot(lhs, rhs, left=1, right=0):
    return lax.dot_general(lhs, rhs, (((left,), (right,)), ((), ())), preferred_element_type=F32)


def hits(position, first, rows):
    ids = lax.broadcasted_iota(I32, (rows, position.shape[1]), 0) + first
    return ids == position


def places(index, slot, capacity):
    return index[...] * capacity + slot[...]


def expert_first(k, capacity):
    experts = lax.axis_size("expert")
    return 0 if k is None else lax.rem(lax.axis_index("expert") + k, experts) * capacity


def gate_of(hit, gate):
    return jnp.sum(jnp.where(hit, gate, 0.0), axis=1, keepdims=True)


def place_kernel(spans, shifts, capacity, index, slot, gate, tokens, grad_output, *refs):
    outs, (tok, grad, sem) = refs[: len(spans)], refs[len(spans) :]
    share = tok.shape[1]
    columns = pl.ds(pl.multiple_of(lax.axis_index("tensor") * share, share), share)
    first = pltpu.make_async_copy(tokens.at[:, columns], tok, sem.at[0])
    second = pltpu.make_async_copy(grad_output.at[:, columns], grad, sem.at[1])
    first.start()
    second.start()
    position = places(index, slot, capacity)
    found = [hits(position, expert_first(k, capacity), rows) for k, rows in zip(shifts, spans)]
    first.wait()
    second.wait()
    for hit, out in zip(found, outs):
        hot = hit.astype(BF16)
        out[:, :share] = dot(hot, tok[...]).astype(BF16)
        out[:, share:] = (dot(hot, grad[...]) * gate_of(hit, gate[...])).astype(BF16)


def place(spans, shifts, capacity, index, slot, gate, tokens, grad_output, share):
    count = tokens.shape[0]
    return pl.pallas_call(
        functools.partial(place_kernel, spans, shifts, capacity),
        out_shape=[jax.ShapeDtypeStruct((rows, 2 * share), BF16) for rows in spans],
        in_specs=[VMEM, VMEM, VMEM, HBM, HBM],
        out_specs=[VMEM] * len(spans),
        scratch_shapes=[
            pltpu.VMEM((count, share), BF16), pltpu.VMEM((count, share), BF16), pltpu.SemaphoreType.DMA((2,))
        ],
        compiler_params=pltpu.CompilerParams(vmem_limit_bytes=LIMIT),
        cost_estimate=pl.CostEstimate(
            flops=4 * sum(spans) * count * share, bytes_accessed=4 * (count + sum(spans)) * share, transcendentals=0
        ),
        name="place_rows",
    )(index, slot, gate, tokens, grad_output)


def gelu_parts(pre):
    c = 0.7978845608028654
    square = pre * pre
    th = jnp.tanh(c * (pre + 0.044715 * (pre * square)))
    half = 0.5 * (1.0 + th)
    return pre * half, half + 0.5 * pre * (1.0 - th * th) * (c + (3 * 0.044715 * c) * square)


def expert_kernel(own_rows, chunk_rows, base, block_base, aliased, *refs):
    refs = list(refs)
    take = lambda n: [refs.pop(0) for _ in range(n)]
    if own_rows:
        index, slot, gate, tokens, grad_output = take(5)
    chunks = [take(5) for _ in chunk_rows]
    up_halves, down_halves = take(2), take(2)
    take(aliased)
    tok_out, grad_out, hidden_out, slope_out = take(4)
    blocks = take(4)
    tok, grad, up, down, hidden, slope, back = take(7)
    if own_rows:
        tokens_in, grad_in = take(2)
    (sem,) = take(1)
    rows, width = tok.shape
    half, share = width // 2, width // 4
    mine = lax.axis_index("dp")
    order = lax.axis_index("tensor") ^ (2 * mine)
    count = [0]

    def copy(src, dst):
        c = pltpu.make_async_copy(src, dst, sem.at[count[0]])
        count[0] += 1
        c.start()
        return c

    waits = []
    if own_rows:
        for src, dst in ((tokens, tokens_in), (grad_output, grad_in)):
            for start, place_at in ((mine * half, 0), ((1 - mine) * half, half)):
                start = pl.multiple_of(start, half)
                waits.append(copy(src.at[:, pl.ds(start, half)], dst.at[:, pl.ds(place_at, half)]))
    at = own_rows
    for (z, x, y, tok_d, grad_d), n in zip(chunks, chunk_rows):
        tok_slots = [r.at[:, pl.ds(0, share)] for r in (z, x, y)] + [tok_d]
        grad_slots = [r.at[:, pl.ds(share, share)] for r in (z, x, y)] + [grad_d]
        for j in range(4):
            columns = pl.ds(pl.multiple_of((order ^ j) * share, share), share)
            waits.append(copy(tok_slots[j], tok.at[pl.ds(at, n), columns]))
            waits.append(copy(grad_slots[j], grad.at[pl.ds(at, n), columns]))
        at += n
    hid = hidden.shape[1]
    step = 256
    tiles = []
    for n in range(0, hid, step):
        cols = pl.ds(n, step)
        tiles.append([])
        for halves, dst in ((up_halves, up), (down_halves, down)):
            for i in range(2):
                tiles[-1].append(copy(halves[i].at[:, cols], dst.at[pl.ds(i * half, half), cols]))
    if own_rows:
        hit = hits(places(index, slot, own_rows), expert_first(0, own_rows), own_rows)
        hot = hit.astype(BF16)
        scale = gate_of(hit, gate[...])
    for w in waits:
        w.wait()
    if own_rows:
        tok[:own_rows, :] = dot(hot, tokens_in[...]).astype(BF16)
        grad[:own_rows, :] = (dot(hot, grad_in[...]) * scale).astype(BF16)
    outs = [copy(tok, tok_out.at[pl.ds(base, rows), :]), copy(grad, grad_out.at[pl.ds(base, rows), :])]
    for n, arrived in zip(range(0, hid, step), tiles):
        cols = slice(n, n + step)
        for w in arrived:
            w.wait()
        pre = dot(tok[...], up[:, cols])
        hidden_grad = dot(grad[...], down[:, cols])
        act, deriv = gelu_parts(pre)
        hidden[:, cols] = act.astype(BF16)
        slope[:, cols] = (hidden_grad * deriv).astype(BF16)
    outs.append(copy(hidden, hidden_out.at[pl.ds(base, rows), :]))
    outs.append(copy(slope, slope_out.at[pl.ds(base, rows), :]))
    for j in range(4):
        quarter = pl.ds(pl.multiple_of((order ^ j) * share, share), share)
        back[j] = dot(slope[...], up[quarter, :], 1, 1).astype(BF16)
        outs.append(copy(back.at[j], blocks[j].at[pl.ds(block_base, rows), :]))
    for w in outs:
        w.wait()


def expert_rows(own, chunks, weights, total_rows, base, block_rows, block_base, kept, blocks):
    own_rows = own[0] if own else 0
    chunk_rows = [c[0].shape[0] for c in chunks]
    rows = own_rows + sum(chunk_rows)
    half, hid = weights[0].shape
    width, share = 2 * half, half // 2
    operands = []
    specs = []
    if own:
        operands += own[1:]
        specs += [VMEM, VMEM, VMEM, HBM, HBM]
    for c in chunks:
        operands += c
        specs += [ANY] * 5
    operands += weights
    specs += [HBM] * 4
    aliases = {}
    for first, previous in ((0, kept), (4, blocks)):
        if previous:
            aliases.update({len(operands) + i: first + i for i in range(4)})
            operands += previous
            specs += [ANY] * 4
    shape = lambda *s: jax.ShapeDtypeStruct(s, BF16)
    buf = lambda *s: pltpu.VMEM(s, BF16)
    scratch = [
        buf(rows, width), buf(rows, width), buf(width, hid), buf(width, hid),
        buf(rows, hid), buf(rows, hid), buf(4, rows, share),
    ]
    copies = 8 + 8 * len(chunks) + 4 * (hid // 256)
    if own:
        count = own[4].shape[0]
        scratch += [buf(count, width), buf(count, width)]
        copies += 4
    scratch.append(pltpu.SemaphoreType.DMA((copies,)))
    out = pl.pallas_call(
        functools.partial(expert_kernel, own_rows, chunk_rows, base, block_base, len(aliases)),
        out_shape=[shape(total_rows, width)] * 2 + [shape(total_rows, hid)] * 2 + [shape(block_rows, share)] * 4,
        in_specs=specs,
        out_specs=[ANY] * 8,
        scratch_shapes=scratch,
        input_output_aliases=aliases,
        compiler_params=pltpu.CompilerParams(vmem_limit_bytes=LIMIT + rows * 2**15),
        cost_estimate=pl.CostEstimate(
            flops=6 * rows * width * hid, bytes_accessed=4 * width * hid + 8 * rows * width, transcendentals=rows * hid
        ),
        name="expert_rows",
    )(*operands)
    return list(out[:4]), list(out[4:])


def unplace_kernel(spans, shifts, capacity, index, slot, *refs):
    out = refs[-1]
    position = places(index, slot, capacity)
    total = None
    for k, rows, back in zip(shifts, spans, refs[:-1]):
        hot = hits(position, expert_first(k, capacity), rows).astype(BF16)
        part = dot(hot, back[...], 0, 0)
        total = part if total is None else total + part
    out[...] = total.astype(BF16)


def unplace(shifts, capacity, index, slot, backs):
    spans = [b.shape[0] for b in backs]
    count, share = index.shape[1], backs[0].shape[1]
    return pl.pallas_call(
        functools.partial(unplace_kernel, spans, shifts, capacity),
        out_shape=jax.ShapeDtypeStruct((count, share), BF16),
        in_specs=[VMEM] * (2 + len(backs)),
        out_specs=VMEM,
        compiler_params=pltpu.CompilerParams(vmem_limit_bytes=LIMIT),
        cost_estimate=pl.CostEstimate(
            flops=2 * sum(spans) * count * share, bytes_accessed=2 * (count + sum(spans)) * share, transcendentals=0
        ),
        name="unplace_rows",
    )(index, slot, *backs)


def outer_kernel(rows, out, *refs):
    total = dot(rows[...], out[...], 0, 0).astype(BF16)
    if len(refs) > 1:
        total = (total.astype(F32) + refs[0][...].astype(F32)).astype(BF16)
    refs[-1][...] = total


def outer(rows, out, which, got):
    count, width = rows.shape
    hid = out.shape[1]
    half, block = width // 2, width // 8
    steps = half // block
    tile = pl.BlockSpec((block, hid), lambda i: (i, 0))
    operands = [rows, out] + ([] if got is None else [got])
    return pl.pallas_call(
        outer_kernel,
        out_shape=jax.ShapeDtypeStruct((half, hid), BF16),
        grid=(steps,),
        in_specs=[
            pl.BlockSpec((count, block), lambda i: (0, which * steps + i)),
            pl.BlockSpec((count, hid), lambda i: (0, 0)),
        ]
        + [tile] * (len(operands) - 2),
        out_specs=tile,
        compiler_params=pltpu.CompilerParams(vmem_limit_bytes=LIMIT),
        cost_estimate=pl.CostEstimate(
            flops=2 * count * half * hid, bytes_accessed=2 * (count * (half + hid) + half * hid), transcendentals=0
        ),
        name="weight_grad",
    )(*operands)


def local(tokens, grad_output, gate_prob, expert_index, slot_index, up_weight, down_weight):
    experts = lax.axis_size("expert")
    tensor_size = lax.axis_size("tensor")
    tok_count, width = tokens.shape
    capacity = 2 * tok_count // experts
    share = width // tensor_size

    def swap(x):
        return lax.ppermute(x, "dp", [(0, 1), (1, 0)])

    def across(x, j):
        return lax.ppermute(x, "tensor", [(i, i ^ j) for i in range(tensor_size)])

    def shift(x, k):
        return lax.ppermute(x, "expert", [(i, (i + k) % experts) for i in range(experts)])

    def after(x, *others):
        return lax.optimization_barrier((x,) + others)[0]

    def spread(rows, *before):
        x, y = across(rows, 1), across(rows, 2)
        half_y, half_x = y[:, :share], x[:, share:]
        if before:
            half_y, half_x = after(half_y, *before), after(half_x, *before)
        return [rows, x, y, across(half_y, 1), across(half_x, 2)]

    def collect(blocks):
        got = [across(blocks[j], j) for j in (1, 2, 3)]

        def total(lo, hi):
            terms = [b[lo:hi].astype(F32) for b in [blocks[0]] + got]
            return (terms[0] + terms[1] + (terms[2] + terms[3])).astype(BF16)

        return total, got

    index, slot = expert_index.reshape(1, tok_count), slot_index.reshape(1, tok_count)
    gate = gate_prob.reshape(1, tok_count)
    up_own, down_own = up_weight[0], down_weight[0]
    weights = [up_own, swap(up_own), down_own, swap(down_own)]

    if experts == 4:
        shifts = [1, 3, 2]
        sends = place([capacity] * 3, shifts, capacity, index, slot, gate, tokens, grad_output, share)
        one, three = shift(sends[0], 1), shift(sends[1], 3)
        own = [capacity, index, slot, gate, tokens, grad_output]
        most = 3 * capacity
        kept, blocks = expert_rows(own, [], weights, 4 * capacity, 0, most, 0, None, None)
        two = shift(after(sends[2], blocks[0]), 2)
        near = spread(jnp.concatenate([after(one, blocks[0]), three], 0))
        kept, blocks = expert_rows(None, [near], weights, 4 * capacity, capacity, most, capacity, kept, blocks)
        far = spread(after(two, *near[3:]), blocks[0])
        total, got = collect(blocks)
        sums = [total(i * capacity, (i + 1) * capacity) for i in range(3)]
        kept, blocks = expert_rows(None, [far], weights, 4 * capacity, most, capacity, 0, kept, None)
        total, _ = collect([blocks[0]] + [after(b, got[0]) for b in blocks[1:]])
        sums.append(total(0, capacity))
        backs = sums[:1] + [shift(x, -k) for x, k in zip(sums[1:], shifts)]
        shifts = [0] + shifts
    else:
        rows = experts * capacity
        shifts = [None]

        def exchange(x):
            moved = lax.all_to_all(
                x.reshape(experts, capacity, x.shape[1]), "expert", split_axis=0, concat_axis=0, tiled=True
            )
            return moved.reshape(rows, x.shape[1])

        (send,) = place([rows], shifts, capacity, index, slot, gate, tokens, grad_output, share)
        kept, blocks = expert_rows(None, [spread(exchange(send))], weights, rows, 0, rows, 0, None, None)
        total, _ = collect(blocks)
        sums = [total(0, rows)]
        backs = [exchange(sums[0])]

    tok_rows, grad_rows, hidden, slope = kept
    hidden, slope = after(hidden, *sums), after(slope, *sums)
    got_up = swap(outer(tok_rows, slope, 1, None))
    got_down = swap(outer(grad_rows, hidden, 1, None))
    grad_up, grad_down = outer(tok_rows, slope, 0, got_up), outer(grad_rows, hidden, 0, got_down)
    backs[-1] = after(backs[-1], grad_up, grad_down)
    return unplace(shifts, capacity, index, slot, backs), grad_up[None], grad_down[None]


def solution(mesh):
    placed = (
        P(("expert", "dp"), None),
        P(("expert", "dp"), None),
        P(("expert", "dp")),
        P(("expert", "dp"), None),
        P(("expert", "dp"), None),
        P("expert", "dp", "tensor"),
        P("expert", "dp", "tensor"),
    )
    return jax.shard_map(
        local,
        mesh=mesh,
        in_specs=placed,
        out_specs=(
            P(("expert", "dp"), "tensor"),
            P("expert", "dp", "tensor"),
            P("expert", "dp", "tensor"),
        ),
        check_vma=False,
    )
```

```python
import functools

import jax
import jax.numpy as jnp
from jax import lax
from jax.experimental import pallas as pl
from jax.experimental.pallas import tpu as pltpu
from jax.sharding import PartitionSpec as P

F32 = jnp.float32
BF16 = jnp.bfloat16
I32 = jnp.int32
ANY = pl.BlockSpec(memory_space=pl.ANY)
VMEM = pl.BlockSpec(memory_space=pltpu.VMEM)
SMEM = pl.BlockSpec(memory_space=pltpu.SMEM)
HBM = pl.BlockSpec(memory_space=pltpu.HBM)
LIMIT = 22 * 2**20
SMALL = pl.CostEstimate(flops=1000, bytes_accessed=1000, transcendentals=0)


def dot(lhs, rhs, left=1, right=0):
    return lax.dot_general(lhs, rhs, (((left,), (right,)), ((), ())), preferred_element_type=F32)


def hits(position, first, rows):
    ids = lax.broadcasted_iota(I32, (rows, position.shape[1]), 0) + first
    return ids == position


def places(index, slot, capacity):
    return index[...] * capacity + slot[...]


def expert_first(k, capacity):
    experts = lax.axis_size("expert")
    return 0 if k is None else lax.rem(lax.axis_index("expert") + k, experts) * capacity


def gate_of(hit, gate):
    return jnp.sum(jnp.where(hit, gate, 0.0), axis=1, keepdims=True)


def place_kernel(spans, shifts, capacity, index, slot, gate, tokens, grad_output, *refs):
    outs, (tok, grad, sem) = refs[: len(spans)], refs[len(spans) :]
    share = tok.shape[1]
    columns = pl.ds(pl.multiple_of(lax.axis_index("tensor") * share, share), share)
    first = pltpu.make_async_copy(tokens.at[:, columns], tok, sem.at[0])
    second = pltpu.make_async_copy(grad_output.at[:, columns], grad, sem.at[1])
    first.start()
    second.start()
    position = places(index, slot, capacity)
    found = [hits(position, expert_first(k, capacity), rows) for k, rows in zip(shifts, spans)]
    first.wait()
    second.wait()
    for hit, out in zip(found, outs):
        hot = hit.astype(BF16)
        out[:, :share] = dot(hot, tok[...]).astype(BF16)
        out[:, share:] = (dot(hot, grad[...]) * gate_of(hit, gate[...])).astype(BF16)


def place(spans, shifts, capacity, index, slot, gate, tokens, grad_output, share):
    count = tokens.shape[0]
    return pl.pallas_call(
        functools.partial(place_kernel, spans, shifts, capacity),
        out_shape=[jax.ShapeDtypeStruct((rows, 2 * share), BF16) for rows in spans],
        in_specs=[VMEM, VMEM, VMEM, HBM, HBM],
        out_specs=[VMEM] * len(spans),
        scratch_shapes=[
            pltpu.VMEM((count, share), BF16), pltpu.VMEM((count, share), BF16), pltpu.SemaphoreType.DMA((2,))
        ],
        compiler_params=pltpu.CompilerParams(vmem_limit_bytes=54 * 2**20),
        cost_estimate=SMALL,
        name="place_rows",
    )(index, slot, gate, tokens, grad_output)


def gelu_parts(pre):
    c = 0.7978845608028654
    square = pre * pre
    th = jnp.tanh(c * (pre + 0.044715 * (pre * square)))
    half = 0.5 * (1.0 + th)
    return pre * half, half + 0.5 * pre * (1.0 - th * th) * (c + (3 * 0.044715 * c) * square)


def expert_kernel(own_rows, chunk_rows, base, block_base, aliased, *refs):
    refs = list(refs)
    take = lambda n: [refs.pop(0) for _ in range(n)]
    if own_rows:
        index, slot, gate, tokens, grad_output = take(5)
    chunks = [take(5) for _ in chunk_rows]
    up_halves, down_halves = take(2), take(2)
    take(aliased)
    tok_out, grad_out, hidden_out, slope_out = take(4)
    blocks = take(4)
    tok, grad, up, down, hidden, slope, back = take(7)
    if own_rows:
        tokens_in, grad_in = take(2)
    (sem,) = take(1)
    rows, width = tok.shape
    half, share = width // 2, width // 4
    mine = lax.axis_index("dp")
    order = lax.axis_index("tensor") ^ (2 * mine)
    count = [0]

    def copy(src, dst):
        c = pltpu.make_async_copy(src, dst, sem.at[count[0]])
        count[0] += 1
        c.start()
        return c

    waits = []
    if own_rows:
        for src, dst in ((tokens, tokens_in), (grad_output, grad_in)):
            for start, place_at in ((mine * half, 0), ((1 - mine) * half, half)):
                start = pl.multiple_of(start, half)
                waits.append(copy(src.at[:, pl.ds(start, half)], dst.at[:, pl.ds(place_at, half)]))
    at = own_rows
    for (z, x, y, tok_d, grad_d), n in zip(chunks, chunk_rows):
        tok_slots = [r.at[:, pl.ds(0, share)] for r in (z, x, y)] + [tok_d]
        grad_slots = [r.at[:, pl.ds(share, share)] for r in (z, x, y)] + [grad_d]
        for j in range(4):
            columns = pl.ds(pl.multiple_of((order ^ j) * share, share), share)
            waits.append(copy(tok_slots[j], tok.at[pl.ds(at, n), columns]))
            waits.append(copy(grad_slots[j], grad.at[pl.ds(at, n), columns]))
        at += n
    hid = hidden.shape[1]
    step = 256
    tiles = []
    for n in range(0, hid, step):
        cols = pl.ds(n, step)
        tiles.append([])
        for halves, dst in ((up_halves, up), (down_halves, down)):
            for i in range(2):
                tiles[-1].append(copy(halves[i].at[:, cols], dst.at[pl.ds(i * half, half), cols]))
    if own_rows:
        hit = hits(places(index, slot, own_rows), expert_first(0, own_rows), own_rows)
        hot = hit.astype(BF16)
        scale = gate_of(hit, gate[...])
    for w in waits:
        w.wait()
    if own_rows:
        tok[:own_rows, :] = dot(hot, tokens_in[...]).astype(BF16)
        grad[:own_rows, :] = (dot(hot, grad_in[...]) * scale).astype(BF16)
    outs = [copy(tok, tok_out.at[pl.ds(base, rows), :]), copy(grad, grad_out.at[pl.ds(base, rows), :])]
    for n, arrived in zip(range(0, hid, step), tiles):
        cols = slice(n, n + step)
        for w in arrived:
            w.wait()
        pre = dot(tok[...], up[:, cols])
        hidden_grad = dot(grad[...], down[:, cols])
        act, deriv = gelu_parts(pre)
        hidden[:, cols] = act.astype(BF16)
        slope[:, cols] = (hidden_grad * deriv).astype(BF16)
    outs.append(copy(hidden, hidden_out.at[pl.ds(base, rows), :]))
    outs.append(copy(slope, slope_out.at[pl.ds(base, rows), :]))
    for j in range(4):
        quarter = pl.ds(pl.multiple_of((order ^ j) * share, share), share)
        back[j] = dot(slope[...], up[quarter, :], 1, 1).astype(BF16)
        outs.append(copy(back.at[j], blocks[j].at[pl.ds(block_base, rows), :]))
    for w in outs:
        w.wait()


def expert_rows(own, chunks, weights, total_rows, base, block_rows, block_base, kept, blocks):
    own_rows = own[0] if own else 0
    chunk_rows = [c[0].shape[0] for c in chunks]
    rows = own_rows + sum(chunk_rows)
    half, hid = weights[0].shape
    width, share = 2 * half, half // 2
    operands = []
    specs = []
    if own:
        operands += own[1:]
        specs += [VMEM, VMEM, VMEM, HBM, HBM]
    for c in chunks:
        operands += c
        specs += [ANY] * 5
    operands += weights
    specs += [ANY] * 4
    aliases = {}
    for first, previous in ((0, kept), (4, blocks)):
        if previous:
            aliases.update({len(operands) + i: first + i for i in range(4)})
            operands += previous
            specs += [ANY] * 4
    shape = lambda *s: jax.ShapeDtypeStruct(s, BF16)
    buf = lambda *s: pltpu.VMEM(s, BF16)
    scratch = [
        buf(rows, width), buf(rows, width), buf(width, hid), buf(width, hid),
        buf(rows, hid), buf(rows, hid), buf(4, rows, share),
    ]
    copies = 8 + 8 * len(chunks) + 4 * (hid // 256)
    if own:
        count = own[4].shape[0]
        scratch += [buf(count, width), buf(count, width)]
        copies += 4
    scratch.append(pltpu.SemaphoreType.DMA((copies,)))
    out = pl.pallas_call(
        functools.partial(expert_kernel, own_rows, chunk_rows, base, block_base, len(aliases)),
        out_shape=[shape(total_rows, width)] * 2 + [shape(total_rows, hid)] * 2 + [shape(block_rows, share)] * 4,
        in_specs=specs,
        out_specs=[ANY] * 8,
        scratch_shapes=scratch,
        input_output_aliases=aliases,
        compiler_params=pltpu.CompilerParams(vmem_limit_bytes=LIMIT + rows * 2**15),
        cost_estimate=pl.CostEstimate(
            flops=6 * rows * width * hid, bytes_accessed=4 * width * hid + 8 * rows * width, transcendentals=rows * hid
        ),
        name="expert_rows",
    )(*operands)
    return list(out[:4]), list(out[4:])


def unplace_kernel(spans, shifts, capacity, index, slot, *refs):
    out = refs[-1]
    position = places(index, slot, capacity)
    total = None
    for k, rows, back in zip(shifts, spans, refs[:-1]):
        hot = hits(position, expert_first(k, capacity), rows).astype(BF16)
        part = dot(hot, back[...], 0, 0)
        total = part if total is None else total + part
    out[...] = total.astype(BF16)


def unplace(shifts, capacity, index, slot, backs):
    spans = [b.shape[0] for b in backs]
    count, share = index.shape[1], backs[0].shape[1]
    return pl.pallas_call(
        functools.partial(unplace_kernel, spans, shifts, capacity),
        out_shape=jax.ShapeDtypeStruct((count, share), BF16),
        in_specs=[VMEM] * (2 + len(backs)),
        out_specs=VMEM,
        compiler_params=pltpu.CompilerParams(vmem_limit_bytes=LIMIT),
        cost_estimate=SMALL,
        name="unplace_rows",
    )(index, slot, *backs)


def outer_kernel(rows, out, *refs):
    total = dot(rows[...], out[...], 0, 0).astype(BF16)
    if len(refs) > 1:
        total = (total.astype(F32) + refs[0][...].astype(F32)).astype(BF16)
    refs[-1][...] = total


def outer(rows, out, which, got):
    count, width = rows.shape
    hid = out.shape[1]
    half, block = width // 2, width // 8
    steps = half // block
    tile = pl.BlockSpec((block, hid), lambda i: (i, 0))
    operands = [rows, out] + ([] if got is None else [got])
    return pl.pallas_call(
        outer_kernel,
        out_shape=jax.ShapeDtypeStruct((half, hid), BF16),
        grid=(steps,),
        in_specs=[
            pl.BlockSpec((count, block), lambda i: (0, which * steps + i)),
            pl.BlockSpec((count, hid), lambda i: (0, 0)),
        ]
        + [tile] * (len(operands) - 2),
        out_specs=tile,
        compiler_params=pltpu.CompilerParams(vmem_limit_bytes=LIMIT),
        cost_estimate=SMALL,
        name="weight_grad",
    )(*operands)


def local(tokens, grad_output, gate_prob, expert_index, slot_index, up_weight, down_weight):
    experts = lax.axis_size("expert")
    tensor_size = lax.axis_size("tensor")
    tok_count, width = tokens.shape
    capacity = 2 * tok_count // experts
    share = width // tensor_size

    def swap(x):
        return lax.ppermute(x, "dp", [(0, 1), (1, 0)])

    def across(x, j):
        return lax.ppermute(x, "tensor", [(i, i ^ j) for i in range(tensor_size)])

    def shift(x, k):
        return lax.ppermute(x, "expert", [(i, (i + k) % experts) for i in range(experts)])

    def after(x, *others):
        return lax.optimization_barrier((x,) + others)[0]

    def spread(rows, *before):
        x, y = across(rows, 1), across(rows, 2)
        half_y, half_x = y[:, :share], x[:, share:]
        if before:
            half_y, half_x = after(half_y, *before), after(half_x, *before)
        return [rows, x, y, across(half_y, 1), across(half_x, 2)]

    def collect(blocks):
        got = [across(blocks[j], j) for j in (1, 2, 3)]

        def total(lo, hi):
            terms = [b[lo:hi].astype(F32) for b in [blocks[0]] + got]
            return (terms[0] + terms[1] + (terms[2] + terms[3])).astype(BF16)

        return total, got

    def other_halves(kept):
        tok_rows, grad_rows, hidden, slope = kept
        pairs = ((tok_rows, slope), (grad_rows, hidden))
        return [dot(rows[:, width // 2 :], out, 0, 0).astype(BF16) for rows, out in pairs]

    index, slot = expert_index.reshape(1, tok_count), slot_index.reshape(1, tok_count)
    gate = gate_prob.reshape(1, tok_count)
    up_own, down_own = up_weight[0], down_weight[0]
    weights = [up_own, swap(up_own), down_own, swap(down_own)]

    if experts == 4:
        shifts = [1, 3, 2]
        sends = place([capacity] * 3, shifts, capacity, index, slot, gate, tokens, grad_output, share)
        one, three = shift(sends[0], 1), shift(sends[1], 3)
        own = [capacity, index, slot, gate, tokens, grad_output]
        most = 3 * capacity
        kept, blocks = expert_rows(own, [], weights, 4 * capacity, 0, most, 0, None, None)
        two = shift(after(sends[2], blocks[0]), 2)
        near = spread(jnp.concatenate([after(one, blocks[0]), three], 0))
        far = spread(after(two, *near[1:3]))
        near[0] = after(near[0], *far[3:])
        kept, blocks = expert_rows(None, [near], weights, 4 * capacity, capacity, most, capacity, kept, blocks)
        total, got = collect(blocks)
        backs = [total(0, capacity)]
        backs += [shift(total(i * capacity, (i + 1) * capacity), -k) for i, k in ((1, 1), (2, 3))]
        kept, blocks = expert_rows(None, [far], weights, 4 * capacity, most, capacity, 0, kept, None)
        others = other_halves(kept)
        total, _ = collect([blocks[0]] + [after(b, *got, *others) for b in blocks[1:]])
        backs.append(shift(after(total(0, capacity), *backs[1:]), -2))
        shifts = [0] + shifts
    else:
        rows = experts * capacity
        shifts = [None]

        def exchange(x):
            moved = lax.all_to_all(
                x.reshape(experts, capacity, x.shape[1]), "expert", split_axis=0, concat_axis=0, tiled=True
            )
            return moved.reshape(rows, x.shape[1])

        (send,) = place([rows], shifts, capacity, index, slot, gate, tokens, grad_output, share)
        kept, blocks = expert_rows(None, [spread(exchange(send))], weights, rows, 0, rows, 0, None, None)
        others = other_halves(kept)
        total, got = collect(blocks)
        backs = [exchange(total(0, rows))]

    tok_rows, grad_rows, hidden, slope = kept
    got_up, got_down = [swap(after(x, *got)) for x in others]
    grad_up, grad_down = outer(tok_rows, slope, 0, got_up), outer(grad_rows, hidden, 0, got_down)
    backs[-1] = after(backs[-1], grad_up, grad_down)
    return unplace(shifts, capacity, index, slot, backs), grad_up[None], grad_down[None]


def solution(mesh):
    placed = (
        P(("expert", "dp"), None),
        P(("expert", "dp"), None),
        P(("expert", "dp")),
        P(("expert", "dp"), None),
        P(("expert", "dp"), None),
        P("expert", "dp", "tensor"),
        P("expert", "dp", "tensor"),
    )
    return jax.shard_map(
        local,
        mesh=mesh,
        in_specs=placed,
        out_specs=(
            P(("expert", "dp"), "tensor"),
            P("expert", "dp", "tensor"),
            P("expert", "dp", "tensor"),
        ),
        check_vma=False,
    )
```

```python
import functools

import jax
import jax.numpy as jnp
from jax import lax
from jax.experimental import pallas as pl
from jax.experimental.pallas import tpu as pltpu
from jax.sharding import PartitionSpec as P

F32 = jnp.float32
BF16 = jnp.bfloat16
I32 = jnp.int32
ANY = pl.BlockSpec(memory_space=pl.ANY)
VMEM = pl.BlockSpec(memory_space=pltpu.VMEM)
SMEM = pl.BlockSpec(memory_space=pltpu.SMEM)
HBM = pl.BlockSpec(memory_space=pltpu.HBM)
LIMIT = 22 * 2**20
SMALL = pl.CostEstimate(flops=1000, bytes_accessed=1000, transcendentals=0)


def dot(lhs, rhs, left=1, right=0):
    return lax.dot_general(lhs, rhs, (((left,), (right,)), ((), ())), preferred_element_type=F32)


def hits(position, first, rows):
    ids = lax.broadcasted_iota(I32, (rows, position.shape[1]), 0) + first
    return ids == position


def places(index, slot, capacity):
    return index[...] * capacity + slot[...]


def expert_first(k, capacity):
    experts = lax.axis_size("expert")
    return 0 if k is None else lax.rem(lax.axis_index("expert") + k, experts) * capacity


def gate_of(hit, gate):
    return jnp.sum(jnp.where(hit, gate, 0.0), axis=1, keepdims=True)


def place_kernel(spans, shifts, capacity, index, slot, gate, tokens, grad_output, *refs):
    outs, (tok, grad, sem) = refs[: len(spans)], refs[len(spans) :]
    share = tok.shape[1]
    columns = pl.ds(pl.multiple_of(lax.axis_index("tensor") * share, share), share)
    first = pltpu.make_async_copy(tokens.at[:, columns], tok, sem.at[0])
    second = pltpu.make_async_copy(grad_output.at[:, columns], grad, sem.at[1])
    first.start()
    second.start()
    position = places(index, slot, capacity)
    found = [hits(position, expert_first(k, capacity), rows) for k, rows in zip(shifts, spans)]
    first.wait()
    second.wait()
    for hit, out in zip(found, outs):
        hot = hit.astype(BF16)
        out[:, :share] = dot(hot, tok[...]).astype(BF16)
        out[:, share:] = (dot(hot, grad[...]) * gate_of(hit, gate[...])).astype(BF16)


def place(spans, shifts, capacity, index, slot, gate, tokens, grad_output, share):
    count = tokens.shape[0]
    return pl.pallas_call(
        functools.partial(place_kernel, spans, shifts, capacity),
        out_shape=[jax.ShapeDtypeStruct((rows, 2 * share), BF16) for rows in spans],
        in_specs=[VMEM, VMEM, VMEM, HBM, HBM],
        out_specs=[VMEM] * len(spans),
        scratch_shapes=[
            pltpu.VMEM((count, share), BF16), pltpu.VMEM((count, share), BF16), pltpu.SemaphoreType.DMA((2,))
        ],
        compiler_params=pltpu.CompilerParams(vmem_limit_bytes=54 * 2**20),
        cost_estimate=SMALL,
        name="place_rows",
    )(index, slot, gate, tokens, grad_output)


def place_own_kernel(capacity, index, slot, gate, tokens, grad_output, tok, grad, tok_in, grad_in, sem):
    half = tok.shape[1] // 2
    mine = lax.axis_index("dp")
    waits = []
    for k, (src, dst) in enumerate(((tokens, tok_in), (grad_output, grad_in))):
        for i, start in enumerate((mine * half, (1 - mine) * half)):
            source = src.at[:, pl.ds(pl.multiple_of(start, half), half)]
            waits.append(pltpu.make_async_copy(source, dst.at[:, pl.ds(i * half, half)], sem.at[2 * k + i]))
            waits[-1].start()
    hit = hits(places(index, slot, capacity), expert_first(0, capacity), capacity)
    hot = hit.astype(BF16)
    scale = gate_of(hit, gate[...])
    for w in waits:
        w.wait()
    tok[...] = dot(hot, tok_in[...]).astype(BF16)
    grad[...] = (dot(hot, grad_in[...]) * scale).astype(BF16)


def place_own(capacity, index, slot, gate, tokens, grad_output):
    count, width = tokens.shape
    return pl.pallas_call(
        functools.partial(place_own_kernel, capacity),
        out_shape=[jax.ShapeDtypeStruct((capacity, width), BF16)] * 2,
        in_specs=[VMEM, VMEM, VMEM, HBM, HBM],
        out_specs=[VMEM] * 2,
        scratch_shapes=[
            pltpu.VMEM((count, width), BF16), pltpu.VMEM((count, width), BF16), pltpu.SemaphoreType.DMA((4,))
        ],
        compiler_params=pltpu.CompilerParams(vmem_limit_bytes=54 * 2**20),
        cost_estimate=SMALL,
        name="place_own_rows",
    )(index, slot, gate, tokens, grad_output)


def gelu_parts(pre):
    c = 0.7978845608028654
    square = pre * pre
    th = jnp.tanh(c * (pre + 0.044715 * (pre * square)))
    half = 0.5 * (1.0 + th)
    return pre * half, half + 0.5 * pre * (1.0 - th * th) * (c + (3 * 0.044715 * c) * square)


def expert_kernel(own_rows, chunk_rows, base, block_base, aliased, *refs):
    refs = list(refs)
    take = lambda n: [refs.pop(0) for _ in range(n)]
    if own_rows:
        tok_own, grad_own = take(2)
    chunks = [take(5) for _ in chunk_rows]
    up_halves, down_halves = take(2), take(2)
    take(aliased)
    tok_out, grad_out, hidden_out, slope_out = take(4)
    blocks = take(4)
    tok, grad, up, down, hidden, slope, back = take(7)
    (sem,) = take(1)
    rows, width = tok.shape
    half, share = width // 2, width // 4
    mine = lax.axis_index("dp")
    order = lax.axis_index("tensor") ^ (2 * mine)
    count = [0]

    def copy(src, dst):
        c = pltpu.make_async_copy(src, dst, sem.at[count[0]])
        count[0] += 1
        c.start()
        return c

    waits = []
    if own_rows:
        waits.append(copy(tok_own, tok.at[pl.ds(0, own_rows), :]))
        waits.append(copy(grad_own, grad.at[pl.ds(0, own_rows), :]))
    at = own_rows
    for (z, x, y, tok_d, grad_d), n in zip(chunks, chunk_rows):
        tok_slots = [r.at[:, pl.ds(0, share)] for r in (z, x, y)] + [tok_d]
        grad_slots = [r.at[:, pl.ds(share, share)] for r in (z, x, y)] + [grad_d]
        for j in range(4):
            columns = pl.ds(pl.multiple_of((order ^ j) * share, share), share)
            waits.append(copy(tok_slots[j], tok.at[pl.ds(at, n), columns]))
            waits.append(copy(grad_slots[j], grad.at[pl.ds(at, n), columns]))
        at += n
    hid = hidden.shape[1]
    step = 256
    tiles = []
    for n in range(0, hid, step):
        cols = pl.ds(n, step)
        tiles.append([])
        for halves, dst in ((up_halves, up), (down_halves, down)):
            for i in range(2):
                tiles[-1].append(copy(halves[i].at[:, cols], dst.at[pl.ds(i * half, half), cols]))
    for w in waits:
        w.wait()
    outs = [copy(tok, tok_out.at[pl.ds(base, rows), :]), copy(grad, grad_out.at[pl.ds(base, rows), :])]
    for n, arrived in zip(range(0, hid, step), tiles):
        cols = slice(n, n + step)
        for w in arrived:
            w.wait()
        pre = dot(tok[...], up[:, cols])
        hidden_grad = dot(grad[...], down[:, cols])
        act, deriv = gelu_parts(pre)
        hidden[:, cols] = act.astype(BF16)
        slope[:, cols] = (hidden_grad * deriv).astype(BF16)
    outs.append(copy(hidden, hidden_out.at[pl.ds(base, rows), :]))
    outs.append(copy(slope, slope_out.at[pl.ds(base, rows), :]))
    for j in range(4):
        quarter = pl.ds(pl.multiple_of((order ^ j) * share, share), share)
        back[j] = dot(slope[...], up[quarter, :], 1, 1).astype(BF16)
        outs.append(copy(back.at[j], blocks[j].at[pl.ds(block_base, rows), :]))
    for w in outs:
        w.wait()


def expert_rows(own, chunks, weights, total_rows, base, block_rows, block_base, kept, blocks):
    own_rows = own[0].shape[0] if own else 0
    chunk_rows = [c[0].shape[0] for c in chunks]
    rows = own_rows + sum(chunk_rows)
    half, hid = weights[0].shape
    width, share = 2 * half, half // 2
    operands = []
    specs = []
    if own:
        operands += own
        specs += [ANY] * 2
    for c in chunks:
        operands += c
        specs += [ANY] * 5
    operands += weights
    specs += [ANY] * 4
    aliases = {}
    for first, previous in ((0, kept), (4, blocks)):
        if previous:
            aliases.update({len(operands) + i: first + i for i in range(4)})
            operands += previous
            specs += [ANY] * 4
    shape = lambda *s: jax.ShapeDtypeStruct(s, BF16)
    buf = lambda *s: pltpu.VMEM(s, BF16)
    scratch = [
        buf(rows, width), buf(rows, width), buf(width, hid), buf(width, hid),
        buf(rows, hid), buf(rows, hid), buf(4, rows, share),
    ]
    copies = 8 + 8 * len(chunks) + 4 * (hid // 256)
    if own:
        copies += 2
    scratch.append(pltpu.SemaphoreType.DMA((copies,)))
    out = pl.pallas_call(
        functools.partial(expert_kernel, own_rows, chunk_rows, base, block_base, len(aliases)),
        out_shape=[shape(total_rows, width)] * 2 + [shape(total_rows, hid)] * 2 + [shape(block_rows, share)] * 4,
        in_specs=specs,
        out_specs=[ANY] * 8,
        scratch_shapes=scratch,
        input_output_aliases=aliases,
        compiler_params=pltpu.CompilerParams(vmem_limit_bytes=LIMIT + rows * 2**15),
        cost_estimate=pl.CostEstimate(
            flops=6 * rows * width * hid, bytes_accessed=4 * width * hid + 8 * rows * width, transcendentals=rows * hid
        ),
        name="expert_rows",
    )(*operands)
    return list(out[:4]), list(out[4:])


def unplace_kernel(spans, shifts, capacity, index, slot, *refs):
    out = refs[-1]
    position = places(index, slot, capacity)
    total = None
    for k, rows, back in zip(shifts, spans, refs[:-1]):
        hot = hits(position, expert_first(k, capacity), rows).astype(BF16)
        part = dot(hot, back[...], 0, 0)
        total = part if total is None else total + part
    out[...] = total.astype(BF16)


def unplace(shifts, capacity, index, slot, backs):
    spans = [b.shape[0] for b in backs]
    count, share = index.shape[1], backs[0].shape[1]
    return pl.pallas_call(
        functools.partial(unplace_kernel, spans, shifts, capacity),
        out_shape=jax.ShapeDtypeStruct((count, share), BF16),
        in_specs=[VMEM] * (2 + len(backs)),
        out_specs=VMEM,
        compiler_params=pltpu.CompilerParams(vmem_limit_bytes=LIMIT),
        cost_estimate=SMALL,
        name="unplace_rows",
    )(index, slot, *backs)


def outer_kernel(rows, out, *refs):
    total = dot(rows[...], out[...], 0, 0).astype(BF16)
    if len(refs) > 1:
        total = (total.astype(F32) + refs[0][...].astype(F32)).astype(BF16)
    refs[-1][...] = total


def outer(rows, out, which, got):
    count, width = rows.shape
    hid = out.shape[1]
    half, block = width // 2, width // 8
    steps = half // block
    tile = pl.BlockSpec((block, hid), lambda i: (i, 0))
    operands = [rows, out] + ([] if got is None else [got])
    return pl.pallas_call(
        outer_kernel,
        out_shape=jax.ShapeDtypeStruct((half, hid), BF16),
        grid=(steps,),
        in_specs=[
            pl.BlockSpec((count, block), lambda i: (0, which * steps + i)),
            pl.BlockSpec((count, hid), lambda i: (0, 0)),
        ]
        + [tile] * (len(operands) - 2),
        out_specs=tile,
        compiler_params=pltpu.CompilerParams(vmem_limit_bytes=LIMIT),
        cost_estimate=SMALL,
        name="weight_grad",
    )(*operands)


def local(tokens, grad_output, gate_prob, expert_index, slot_index, up_weight, down_weight):
    experts = lax.axis_size("expert")
    tensor_size = lax.axis_size("tensor")
    tok_count, width = tokens.shape
    capacity = 2 * tok_count // experts
    share = width // tensor_size

    def swap(x):
        return lax.ppermute(x, "dp", [(0, 1), (1, 0)])

    def across(x, j):
        return lax.ppermute(x, "tensor", [(i, i ^ j) for i in range(tensor_size)])

    def shift(x, k):
        return lax.ppermute(x, "expert", [(i, (i + k) % experts) for i in range(experts)])

    def after(x, *others):
        return lax.optimization_barrier((x,) + others)[0]

    def spread(rows, *before):
        x, y = across(rows, 1), across(rows, 2)
        half_y, half_x = y[:, :share], x[:, share:]
        if before:
            half_y, half_x = after(half_y, *before), after(half_x, *before)
        return [rows, x, y, across(half_y, 1), across(half_x, 2)]

    def collect(blocks):
        got = [across(blocks[j], j) for j in (1, 2, 3)]

        def total(lo, hi):
            terms = [b[lo:hi].astype(F32) for b in [blocks[0]] + got]
            return (terms[0] + terms[1] + (terms[2] + terms[3])).astype(BF16)

        return total, got

    def other_halves(kept):
        tok_rows, grad_rows, hidden, slope = kept
        pairs = ((tok_rows, slope), (grad_rows, hidden))
        return [dot(rows[:, width // 2 :], out, 0, 0).astype(BF16) for rows, out in pairs]

    index, slot = expert_index.reshape(1, tok_count), slot_index.reshape(1, tok_count)
    gate = gate_prob.reshape(1, tok_count)
    up_own, down_own = up_weight[0], down_weight[0]
    weights = [up_own, swap(up_own), down_own, swap(down_own)]

    if experts == 4:
        shifts = [1, 3, 2]
        sends = place([capacity] * 3, shifts, capacity, index, slot, gate, tokens, grad_output, share)
        one, three = shift(sends[0], 1), shift(sends[1], 3)
        own = place_own(capacity, index, slot, gate, after(tokens, sends[0]), grad_output)
        kept, blocks = expert_rows(own, [], weights, 4 * capacity, 0, capacity, 0, None, None)
        total, got = collect(blocks)
        backs = [total(0, capacity)]
        two = shift(after(sends[2], blocks[0]), 2)
        near = spread(jnp.concatenate([after(one, *got), three], 0))
        far = spread(after(two, *near[1:3]))
        near[0] = after(near[0], *far[1:3])
        kept, blocks = expert_rows(None, [near], weights, 4 * capacity, capacity, 2 * capacity, 0, kept, None)
        total, got = collect(blocks)
        backs += [shift(total(i * capacity, (i + 1) * capacity), -k) for i, k in ((0, 1), (1, 3))]
        kept, blocks = expert_rows(None, [far], weights, 4 * capacity, 3 * capacity, capacity, 0, kept, None)
        others = other_halves(kept)
        total, _ = collect([blocks[0]] + [after(b, *got, *others) for b in blocks[1:]])
        backs.append(shift(total(0, capacity), -2))
        shifts = [0] + shifts
    else:
        rows = experts * capacity
        shifts = [None]

        def exchange(x):
            moved = lax.all_to_all(
                x.reshape(experts, capacity, x.shape[1]), "expert", split_axis=0, concat_axis=0, tiled=True
            )
            return moved.reshape(rows, x.shape[1])

        (send,) = place([rows], shifts, capacity, index, slot, gate, tokens, grad_output, share)
        kept, blocks = expert_rows(None, [spread(exchange(send))], weights, rows, 0, rows, 0, None, None)
        others = other_halves(kept)
        total, got = collect(blocks)
        backs = [exchange(total(0, rows))]

    tok_rows, grad_rows, hidden, slope = kept
    got_up, got_down = [swap(after(x, *got)) for x in others]
    grad_up, grad_down = outer(tok_rows, slope, 0, got_up), outer(grad_rows, hidden, 0, got_down)
    backs[-1] = after(backs[-1], grad_up, grad_down)
    return unplace(shifts, capacity, index, slot, backs), grad_up[None], grad_down[None]


def solution(mesh):
    placed = (
        P(("expert", "dp"), None),
        P(("expert", "dp"), None),
        P(("expert", "dp")),
        P(("expert", "dp"), None),
        P(("expert", "dp"), None),
        P("expert", "dp", "tensor"),
        P("expert", "dp", "tensor"),
    )
    return jax.shard_map(
        local,
        mesh=mesh,
        in_specs=placed,
        out_specs=(
            P(("expert", "dp"), "tensor"),
            P("expert", "dp", "tensor"),
            P("expert", "dp", "tensor"),
        ),
        check_vma=False,
    )
```

```python
import functools

import jax
import jax.numpy as jnp
from jax import lax
from jax.experimental import pallas as pl
from jax.experimental.pallas import tpu as pltpu
from jax.sharding import PartitionSpec as P

F32 = jnp.float32
BF16 = jnp.bfloat16
I32 = jnp.int32
ANY = pl.BlockSpec(memory_space=pl.ANY)
VMEM = pl.BlockSpec(memory_space=pltpu.VMEM)
SMEM = pl.BlockSpec(memory_space=pltpu.SMEM)
HBM = pl.BlockSpec(memory_space=pltpu.HBM)
LIMIT = 22 * 2**20
SMALL = pl.CostEstimate(flops=1000, bytes_accessed=1000, transcendentals=0)


def dot(lhs, rhs, left=1, right=0):
    return lax.dot_general(lhs, rhs, (((left,), (right,)), ((), ())), preferred_element_type=F32)


def hits(position, first, rows):
    ids = lax.broadcasted_iota(I32, (rows, position.shape[1]), 0) + first
    return ids == position


def places(index, slot, capacity):
    return index[...] * capacity + slot[...]


def expert_first(k, capacity):
    experts = lax.axis_size("expert")
    return 0 if k is None else lax.rem(lax.axis_index("expert") + k, experts) * capacity


def gate_of(hit, gate):
    return jnp.sum(jnp.where(hit, gate, 0.0), axis=1, keepdims=True)


class Copies:
    def __init__(self, sem):
        self.sem, self.count = sem, 0

    def start(self, src, dst):
        copy = pltpu.make_async_copy(src, dst, self.sem.at[self.count])
        self.count += 1
        copy.start()
        return copy

    def rows(self, src, dst, count, pieces):
        step = count // pieces
        return [self.start(src.at[pl.ds(i * step, step), :], dst.at[pl.ds(i * step, step), :]) for i in range(pieces)]


def wait(copies):
    for copy in copies:
        copy.wait()


def place_kernel(spans, shifts, capacity, own, index, slot, gate, tokens, grad_output, *refs):
    sends, refs = refs[: len(spans)], refs[len(spans) :]
    if own:
        owns, refs = refs[:2], refs[2:]
    tok, grad, packed = refs[:3]
    copies = Copies(refs[-1])
    count, width = tok.shape
    half, share = width // 2, width // 4
    arrive = copies.rows(tokens, tok, count, 8) + copies.rows(grad_output, grad, count, 8)
    position = places(index, slot, capacity)
    found = [hits(position, expert_first(k, capacity), rows) for k, rows in zip(shifts, spans)]
    scales = [gate_of(hit, gate[...]) for hit in found]
    hots = [hit.astype(BF16) for hit in found]
    columns = pl.ds(pl.multiple_of(lax.axis_index("tensor") * share, share), share)
    wait(arrive)
    leave = []
    at = 0
    for hot, scale, rows, out in zip(hots, scales, spans, sends):
        packed[at : at + rows, :share] = dot(hot, tok[:, columns]).astype(BF16)
        packed[at : at + rows, share:] = (dot(hot, grad[:, columns]) * scale).astype(BF16)
        leave += copies.rows(packed.at[pl.ds(at, rows), :], out, rows, 2)
        at += rows
    if own:
        mine = lax.axis_index("dp")
        hit = hits(position, expert_first(0, capacity), capacity)
        hot, scale = hit.astype(BF16), gate_of(hit, gate[...])
        placed = refs[3:5]
        for i, start in enumerate((mine * half, (1 - mine) * half)):
            source = pl.ds(pl.multiple_of(start, half), half)
            target = slice(i * half, (i + 1) * half)
            placed[0][:, target] = dot(hot, tok[:, source]).astype(BF16)
            placed[1][:, target] = (dot(hot, grad[:, source]) * scale).astype(BF16)
        for src, dst in zip(placed, owns):
            leave += copies.rows(src, dst, capacity, 2)
    wait(leave)


def place(spans, shifts, capacity, own, index, slot, gate, tokens, grad_output):
    count, width = tokens.shape
    shapes = [(rows, width // 2) for rows in spans] + [(capacity, width)] * (2 if own else 0)
    buf = lambda *shape: pltpu.VMEM(shape, BF16)
    scratch = [buf(count, width), buf(count, width), buf(sum(spans), width // 2)]
    scratch += [buf(capacity, width)] * (2 if own else 0)
    return pl.pallas_call(
        functools.partial(place_kernel, spans, shifts, capacity, own),
        out_shape=[jax.ShapeDtypeStruct(shape, BF16) for shape in shapes],
        in_specs=[VMEM, VMEM, VMEM, HBM, HBM],
        out_specs=[ANY] * len(shapes),
        scratch_shapes=scratch + [pltpu.SemaphoreType.DMA((16 + 2 * len(shapes),))],
        compiler_params=pltpu.CompilerParams(vmem_limit_bytes=54 * 2**20),
        cost_estimate=SMALL,
        name="place_rows",
    )(index, slot, gate, tokens, grad_output)


def gelu_parts(pre):
    c = 0.7978845608028654
    square = pre * pre
    th = jnp.tanh(c * (pre + 0.044715 * (pre * square)))
    half = 0.5 * (1.0 + th)
    return pre * half, half + 0.5 * pre * (1.0 - th * th) * (c + (3 * 0.044715 * c) * square)


def expert_kernel(first, base, groups, aliased, *refs):
    refs = list(refs)
    take = lambda n: [refs.pop(0) for _ in range(n)]
    slots = take(2 if first is None else 5)
    up_halves, down_halves = take(2), take(2)
    take(aliased)
    kept_rows, kept_acts = take(2)
    targets = [take(4 if step is None else 2) for _, step in groups]
    tok, grad, up, down, hidden, slope, back = take(7)
    copies = Copies(take(1)[0])
    rows, width = tok.shape
    half, share = width // 2, width // 4
    order = lax.axis_index("tensor") ^ (2 * lax.axis_index("dp"))
    arrive = []
    if first is None:
        arrive += copies.rows(slots[0], tok, rows, 2) + copies.rows(slots[1], grad, rows, 2)
    else:
        span = pl.ds(first, rows)
        for j in range(4):
            columns = pl.ds(pl.multiple_of((order ^ j) * share, share), share)
            if j < 3:
                sources = [slots[j].at[span, pl.ds(0, share)], slots[j].at[span, pl.ds(share, share)]]
            else:
                sources = [slots[3].at[span, :], slots[4].at[span, :]]
            arrive += [copies.start(src, dst.at[:, columns]) for src, dst in zip(sources, (tok, grad))]
    hid = hidden.shape[1]
    step = 256
    tiles = []
    for n in range(0, hid, step):
        cols = pl.ds(n, step)
        tiles.append([])
        for halves, dst in ((up_halves, up), (down_halves, down)):
            for i in range(2):
                tiles[-1].append(copies.start(halves[i].at[:, cols], dst.at[pl.ds(i * half, half), cols]))
    wait(arrive)
    mine = pl.ds(base, rows)
    leave = [copies.start(src, kept_rows.at[i, mine, :]) for i, src in enumerate((tok, grad))]
    for n, arrived in zip(range(0, hid, step), tiles):
        cols = slice(n, n + step)
        wait(arrived)
        pre = dot(tok[...], up[:, cols])
        hidden_grad = dot(grad[...], down[:, cols])
        act, deriv = gelu_parts(pre)
        hidden[:, cols] = act.astype(BF16)
        slope[:, cols] = (hidden_grad * deriv).astype(BF16)
    leave += [copies.start(src, kept_acts.at[i, mine, :]) for i, src in enumerate((slope, hidden))]
    for j in range(4):
        quarter = pl.ds(pl.multiple_of((order ^ j) * share, share), share)
        back[j] = dot(slope[...], up[quarter, :], 1, 1).astype(BF16)
        at = 0
        for (n, step), outs in zip(groups, targets):
            out = outs[j] if step is None else outs[(j & step) // step].at[(j & (3 - step)) // (3 - step)]
            leave.append(copies.start(back.at[j, pl.ds(at, n), :], out))
            at += n
    wait(leave)


def expert_rows(slots, first, groups, weights, total_rows, base, kept):
    rows = sum(n for n, _ in groups)
    half, hid = weights[0].shape
    width, share = 2 * half, half // 2
    operands = list(slots) + list(weights) + list(kept or [])
    aliases = {len(slots) + 4 + i: i for i in range(2)} if kept else {}
    shape = lambda *s: jax.ShapeDtypeStruct(s, BF16)
    buf = lambda *s: pltpu.VMEM(s, BF16)
    quarters = [[shape(n, share)] * 4 if step is None else [shape(2, n, share)] * 2 for n, step in groups]
    counts = [len(q) for q in quarters]
    out = pl.pallas_call(
        functools.partial(expert_kernel, first, base, groups, len(aliases)),
        out_shape=[shape(2, total_rows, width), shape(2, total_rows, hid)] + sum(quarters, []),
        in_specs=[ANY] * len(operands),
        out_specs=[ANY] * (2 + sum(counts)),
        scratch_shapes=[
            buf(rows, width), buf(rows, width), buf(width, hid), buf(width, hid),
            buf(rows, hid), buf(rows, hid), buf(4, rows, share),
            pltpu.SemaphoreType.DMA((12 + 4 * (hid // 256) + 4 * len(groups),)),
        ],
        input_output_aliases=aliases,
        compiler_params=pltpu.CompilerParams(vmem_limit_bytes=LIMIT + rows * 2**15),
        cost_estimate=pl.CostEstimate(
            flops=6 * rows * width * hid, bytes_accessed=4 * width * hid + 8 * rows * width, transcendentals=rows * hid
        ),
        name="expert_rows",
    )(*operands)
    starts = [2 + sum(counts[:i]) for i in range(len(counts))]
    return list(out[:2]), [list(out[i : i + n]) for i, n in zip(starts, counts)]


def unplace_kernel(spans, shifts, capacity, index, slot, *refs):
    out = refs[-1]
    position = places(index, slot, capacity)
    total = None
    for k, rows, back in zip(shifts, spans, refs[:-1]):
        hot = hits(position, expert_first(k, capacity), rows).astype(BF16)
        part = dot(hot, back[...], 0, 0)
        total = part if total is None else total + part
    out[...] = total.astype(BF16)


def unplace(shifts, capacity, index, slot, backs):
    spans = [b.shape[0] for b in backs]
    count, share = index.shape[1], backs[0].shape[1]
    return pl.pallas_call(
        functools.partial(unplace_kernel, spans, shifts, capacity),
        out_shape=jax.ShapeDtypeStruct((count, share), BF16),
        in_specs=[VMEM] * (2 + len(backs)),
        out_specs=VMEM,
        compiler_params=pltpu.CompilerParams(vmem_limit_bytes=LIMIT),
        cost_estimate=SMALL,
        name="unplace_rows",
    )(index, slot, *backs)


def weight_grad_kernel(rows, acts, got, up_out, down_out, total, sem):
    copies = Copies(sem)
    half = total.shape[1]
    step = 128
    leave = []
    for i, out in enumerate((up_out, down_out)):
        for n in range(0, half, step):
            mine = dot(rows[i, :, n : n + step], acts[i], 0, 0).astype(BF16).astype(F32)
            total[i, n : n + step, :] = (mine + got[i, n : n + step, :].astype(F32)).astype(BF16)
            leave.append(copies.start(total.at[i, pl.ds(n, step), :], out.at[pl.ds(n, step), :]))
    wait(leave)


def weight_grads(kept_rows, kept_acts, got):
    _, count, width = kept_rows.shape
    hid = kept_acts.shape[2]
    half = width // 2
    return pl.pallas_call(
        weight_grad_kernel,
        out_shape=[jax.ShapeDtypeStruct((half, hid), BF16)] * 2,
        grid=(1,),
        in_specs=[
            pl.BlockSpec((2, count, half), lambda i: (0, 0, 0)),
            pl.BlockSpec((2, count, hid), lambda i: (0, 0, 0)),
            pl.BlockSpec((2, half, hid), lambda i: (0, 0, 0)),
        ],
        out_specs=[ANY] * 2,
        scratch_shapes=[pltpu.VMEM((2, half, hid), BF16), pltpu.SemaphoreType.DMA((2 * (half // 128),))],
        compiler_params=pltpu.CompilerParams(vmem_limit_bytes=40 * 2**20),
        cost_estimate=SMALL,
        name="weight_grads",
    )(kept_rows, kept_acts, got)


def local(tokens, grad_output, gate_prob, expert_index, slot_index, up_weight, down_weight):
    experts = lax.axis_size("expert")
    tensor_size = lax.axis_size("tensor")
    tok_count, width = tokens.shape
    capacity = 2 * tok_count // experts
    share = width // tensor_size

    def swap(x):
        return lax.ppermute(x, "dp", [(0, 1), (1, 0)])

    def across(x, j):
        return lax.ppermute(x, "tensor", [(i, i ^ j) for i in range(tensor_size)])

    def shift(x, k):
        return lax.ppermute(x, "expert", [(i, (i + k) % experts) for i in range(experts)])

    def after(x, *others):
        return lax.optimization_barrier((x,) + others)[0]

    def spread(rows, *before):
        x, y = across(rows, 1), across(rows, 2)
        half_y, half_x = y[:, :share], x[:, share:]
        if before:
            half_y, half_x = after(half_y, *before), after(half_x, *before)
        return [rows, x, y, across(half_y, 1), across(half_x, 2)]

    def collect(blocks):
        got = [across(blocks[j], j) for j in (1, 2, 3)]
        terms = [b.astype(F32) for b in [blocks[0]] + got]
        return (terms[0] + terms[1] + (terms[2] + terms[3])).astype(BF16), got

    def collect_pair(pair, step):
        keep, send = pair
        got = across(send, step)
        last = across((keep[1].astype(F32) + got[1].astype(F32)).astype(BF16), 3 - step)
        return (keep[0].astype(F32) + got[0].astype(F32) + last.astype(F32)).astype(BF16), got

    def other_halves(kept):
        rows, acts = kept
        dims = (((1,), (1,)), ((0,), (0,)))
        return lax.dot_general(rows[:, :, width // 2 :], acts, dims, preferred_element_type=F32).astype(BF16)

    index, slot = expert_index.reshape(1, tok_count), slot_index.reshape(1, tok_count)
    gate = gate_prob.reshape(1, tok_count)
    up_own, down_own = up_weight[0], down_weight[0]
    weights = [up_own, swap(up_own), down_own, swap(down_own)]

    if experts == 4:
        shifts = [1, 3, 2]
        placed = place([capacity] * 3, shifts, capacity, True, index, slot, gate, tokens, grad_output)
        moved = [shift(rows, k) for rows, k in zip(placed, shifts)]
        everything = 4 * capacity
        slots = spread(jnp.concatenate(moved, 0))
        own = [after(placed[3], *moved), placed[4]]
        kept, (pair,) = expert_rows(own, None, [(capacity, 1)], weights, everything, 0, None)
        back, got_own = collect_pair([pair[0], after(pair[1], *slots[3:])], 1)
        backs = [back]
        kept, pairs = expert_rows(slots, 0, [(capacity, 1), (capacity, 2)], weights, everything, capacity, kept)
        (one, got_one), (three, got_three) = collect_pair(pairs[0], 1), collect_pair(pairs[1], 2)
        backs += [shift(one, -1), shift(three, -3)]
        kept, (blocks,) = expert_rows(
            [after(slots[0], got_own)] + slots[1:], 2 * capacity, [(capacity, None)], weights, everything, 3 * capacity, kept
        )
        others = other_halves([kept[0], after(kept[1], got_one, got_three)])
        grads = weight_grads(*kept, swap(others))
        two, _ = collect([blocks[0]] + [after(b, got_one, got_three) for b in blocks[1:]])
        backs.append(after(shift(two, -2), *grads))
        shifts = [0] + shifts
    else:
        rows = experts * capacity
        shifts = [None]

        def exchange(x):
            moved = lax.all_to_all(
                x.reshape(experts, capacity, x.shape[1]), "expert", split_axis=0, concat_axis=0, tiled=True
            )
            return moved.reshape(rows, x.shape[1])

        (send,) = place([rows], shifts, capacity, False, index, slot, gate, tokens, grad_output)
        kept, (blocks,) = expert_rows(spread(exchange(send)), 0, [(rows, None)], weights, rows, 0, None)
        others = other_halves(kept)
        grads = weight_grads(*kept, swap(others))
        total, _ = collect(blocks)
        backs = [exchange(total)]

    return unplace(shifts, capacity, index, slot, backs), grads[0][None], grads[1][None]


def solution(mesh):
    placed = (
        P(("expert", "dp"), None),
        P(("expert", "dp"), None),
        P(("expert", "dp")),
        P(("expert", "dp"), None),
        P(("expert", "dp"), None),
        P("expert", "dp", "tensor"),
        P("expert", "dp", "tensor"),
    )
    return jax.shard_map(
        local,
        mesh=mesh,
        in_specs=placed,
        out_specs=(
            P(("expert", "dp"), "tensor"),
            P("expert", "dp", "tensor"),
            P("expert", "dp", "tensor"),
        ),
        check_vma=False,
    )
```

```python
import functools

import jax
import jax.numpy as jnp
from jax import lax
from jax.experimental import pallas as pl
from jax.experimental.pallas import tpu as pltpu
from jax.sharding import PartitionSpec as P

F32 = jnp.float32
BF16 = jnp.bfloat16
I32 = jnp.int32
ANY = pl.BlockSpec(memory_space=pl.ANY)
VMEM = pl.BlockSpec(memory_space=pltpu.VMEM)
SMEM = pl.BlockSpec(memory_space=pltpu.SMEM)
HBM = pl.BlockSpec(memory_space=pltpu.HBM)
LIMIT = 22 * 2**20
SMALL = pl.CostEstimate(flops=1000, bytes_accessed=1000, transcendentals=0)


def dot(lhs, rhs, left=1, right=0):
    return lax.dot_general(lhs, rhs, (((left,), (right,)), ((), ())), preferred_element_type=F32)


def hits(position, first, rows):
    ids = lax.broadcasted_iota(I32, (rows, position.shape[1]), 0) + first
    return ids == position


def places(index, slot, capacity):
    return index[...] * capacity + slot[...]


def expert_first(k, capacity):
    experts = lax.axis_size("expert")
    return 0 if k is None else lax.rem(lax.axis_index("expert") + k, experts) * capacity


def gate_of(hit, gate):
    return jnp.sum(jnp.where(hit, gate, 0.0), axis=1, keepdims=True)


class Copies:
    def __init__(self, sem):
        self.sem, self.count = sem, 0

    def start(self, src, dst):
        copy = pltpu.make_async_copy(src, dst, self.sem.at[self.count])
        self.count += 1
        copy.start()
        return copy

    def rows(self, src, dst, count, pieces):
        step = count // pieces
        return [self.start(src.at[pl.ds(i * step, step), :], dst.at[pl.ds(i * step, step), :]) for i in range(pieces)]


def wait(copies):
    for copy in copies:
        copy.wait()


def place_kernel(spans, shifts, capacity, own, index, slot, gate, tokens, grad_output, *refs):
    sends, refs = refs[: len(spans)], refs[len(spans) :]
    if own:
        owns, refs = refs[:2], refs[2:]
    tok, grad, packed = refs[:3]
    copies = Copies(refs[-1])
    count, width = tok.shape
    half, share = width // 2, width // 4
    arrive = copies.rows(tokens, tok, count, 8) + copies.rows(grad_output, grad, count, 8)
    position = places(index, slot, capacity)
    found = [hits(position, expert_first(k, capacity), rows) for k, rows in zip(shifts, spans)]
    scales = [gate_of(hit, gate[...]) for hit in found]
    hots = [hit.astype(BF16) for hit in found]
    columns = pl.ds(pl.multiple_of(lax.axis_index("tensor") * share, share), share)
    wait(arrive)
    leave = []
    at = 0
    for hot, scale, rows, out in zip(hots, scales, spans, sends):
        packed[at : at + rows, :share] = dot(hot, tok[:, columns]).astype(BF16)
        packed[at : at + rows, share:] = (dot(hot, grad[:, columns]) * scale).astype(BF16)
        leave += copies.rows(packed.at[pl.ds(at, rows), :], out, rows, 2)
        at += rows
    if own:
        mine = lax.axis_index("dp")
        hit = hits(position, expert_first(0, capacity), capacity)
        hot, scale = hit.astype(BF16), gate_of(hit, gate[...])
        placed = refs[3:5]
        for i, start in enumerate((mine * half, (1 - mine) * half)):
            source = pl.ds(pl.multiple_of(start, half), half)
            target = slice(i * half, (i + 1) * half)
            placed[0][:, target] = dot(hot, tok[:, source]).astype(BF16)
            placed[1][:, target] = (dot(hot, grad[:, source]) * scale).astype(BF16)
        for src, dst in zip(placed, owns):
            leave += copies.rows(src, dst, capacity, 2)
    wait(leave)


def place(spans, shifts, capacity, own, index, slot, gate, tokens, grad_output):
    count, width = tokens.shape
    shapes = [(rows, width // 2) for rows in spans] + [(capacity, width)] * (2 if own else 0)
    buf = lambda *shape: pltpu.VMEM(shape, BF16)
    scratch = [buf(count, width), buf(count, width), buf(sum(spans), width // 2)]
    scratch += [buf(capacity, width)] * (2 if own else 0)
    return pl.pallas_call(
        functools.partial(place_kernel, spans, shifts, capacity, own),
        out_shape=[jax.ShapeDtypeStruct(shape, BF16) for shape in shapes],
        in_specs=[VMEM, VMEM, VMEM, HBM, HBM],
        out_specs=[ANY] * len(shapes),
        scratch_shapes=scratch + [pltpu.SemaphoreType.DMA((16 + 2 * len(shapes),))],
        compiler_params=pltpu.CompilerParams(vmem_limit_bytes=54 * 2**20),
        cost_estimate=SMALL,
        name="place_rows",
    )(index, slot, gate, tokens, grad_output)


def gelu_parts(pre):
    c = 0.7978845608028654
    square = pre * pre
    th = jnp.tanh(c * (pre + 0.044715 * (pre * square)))
    half = 0.5 * (1.0 + th)
    return pre * half, half + 0.5 * pre * (1.0 - th * th) * (c + (3 * 0.044715 * c) * square)


def expert_kernel(first, base, groups, aliased, *refs):
    refs = list(refs)
    take = lambda n: [refs.pop(0) for _ in range(n)]
    slots = take(2 if first is None else 5)
    up_halves, down_halves = take(2), take(2)
    take(aliased)
    kept_rows, kept_acts = take(2)
    targets = [take(4 if step is None else 2) for _, step in groups]
    tok, grad, up, down, hidden, slope, back = take(7)
    copies = Copies(take(1)[0])
    rows, width = tok.shape
    half, share = width // 2, width // 4
    order = lax.axis_index("tensor") ^ (2 * lax.axis_index("dp"))
    arrive = []
    if first is None:
        arrive += copies.rows(slots[0], tok, rows, 2) + copies.rows(slots[1], grad, rows, 2)
    else:
        span = pl.ds(first, rows)
        for j in range(4):
            columns = pl.ds(pl.multiple_of((order ^ j) * share, share), share)
            if j < 3:
                sources = [slots[j].at[span, pl.ds(0, share)], slots[j].at[span, pl.ds(share, share)]]
            else:
                sources = [slots[3].at[span, :], slots[4].at[span, :]]
            arrive += [copies.start(src, dst.at[:, columns]) for src, dst in zip(sources, (tok, grad))]
    hid = hidden.shape[1]
    step = 256
    tiles = []
    for n in range(0, hid, step):
        cols = pl.ds(n, step)
        tiles.append([])
        for halves, dst in ((up_halves, up), (down_halves, down)):
            for i in range(2):
                tiles[-1].append(copies.start(halves[i].at[:, cols], dst.at[pl.ds(i * half, half), cols]))
    wait(arrive)
    mine = pl.ds(base, rows)
    leave = [copies.start(src, kept_rows.at[i, mine, :]) for i, src in enumerate((tok, grad))]
    for n, arrived in zip(range(0, hid, step), tiles):
        cols = slice(n, n + step)
        wait(arrived)
        pre = dot(tok[...], up[:, cols])
        hidden_grad = dot(grad[...], down[:, cols])
        act, deriv = gelu_parts(pre)
        hidden[:, cols] = act.astype(BF16)
        slope[:, cols] = (hidden_grad * deriv).astype(BF16)
    leave += [copies.start(src, kept_acts.at[i, mine, :]) for i, src in enumerate((slope, hidden))]
    for j in range(4):
        quarter = pl.ds(pl.multiple_of((order ^ j) * share, share), share)
        back[j] = dot(slope[...], up[quarter, :], 1, 1).astype(BF16)
        at = 0
        for (n, step), outs in zip(groups, targets):
            out = outs[j] if step is None else outs[(j & step) // step].at[(j & (3 - step)) // (3 - step)]
            leave.append(copies.start(back.at[j, pl.ds(at, n), :], out))
            at += n
    wait(leave)


def expert_rows(slots, first, groups, weights, total_rows, base, kept):
    rows = sum(n for n, _ in groups)
    half, hid = weights[0].shape
    width, share = 2 * half, half // 2
    operands = list(slots) + list(weights) + list(kept or [])
    aliases = {len(slots) + 4 + i: i for i in range(2)} if kept else {}
    shape = lambda *s: jax.ShapeDtypeStruct(s, BF16)
    buf = lambda *s: pltpu.VMEM(s, BF16)
    quarters = [[shape(n, share)] * 4 if step is None else [shape(2, n, share)] * 2 for n, step in groups]
    counts = [len(q) for q in quarters]
    out = pl.pallas_call(
        functools.partial(expert_kernel, first, base, groups, len(aliases)),
        out_shape=[shape(2, total_rows, width), shape(2, total_rows, hid)] + sum(quarters, []),
        in_specs=[ANY] * len(operands),
        out_specs=[ANY] * (2 + sum(counts)),
        scratch_shapes=[
            buf(rows, width), buf(rows, width), buf(width, hid), buf(width, hid),
            buf(rows, hid), buf(rows, hid), buf(4, rows, share),
            pltpu.SemaphoreType.DMA((12 + 4 * (hid // 256) + 4 * len(groups),)),
        ],
        input_output_aliases=aliases,
        compiler_params=pltpu.CompilerParams(vmem_limit_bytes=LIMIT + rows * 2**15),
        cost_estimate=pl.CostEstimate(
            flops=6 * rows * width * hid, bytes_accessed=4 * width * hid + 8 * rows * width, transcendentals=rows * hid
        ),
        name="expert_rows",
    )(*operands)
    starts = [2 + sum(counts[:i]) for i in range(len(counts))]
    return list(out[:2]), [list(out[i : i + n]) for i, n in zip(starts, counts)]


def unplace_kernel(spans, shifts, capacity, index, slot, *refs):
    out = refs[-1]
    position = places(index, slot, capacity)
    total = None
    for k, rows, back in zip(shifts, spans, refs[:-1]):
        hot = hits(position, expert_first(k, capacity), rows).astype(BF16)
        part = dot(hot, back[...], 0, 0)
        total = part if total is None else total + part
    out[...] = total.astype(BF16)


def unplace(shifts, capacity, index, slot, backs):
    spans = [b.shape[0] for b in backs]
    count, share = index.shape[1], backs[0].shape[1]
    return pl.pallas_call(
        functools.partial(unplace_kernel, spans, shifts, capacity),
        out_shape=jax.ShapeDtypeStruct((count, share), BF16),
        in_specs=[VMEM] * (2 + len(backs)),
        out_specs=VMEM,
        compiler_params=pltpu.CompilerParams(vmem_limit_bytes=LIMIT),
        cost_estimate=SMALL,
        name="unplace_rows",
    )(index, slot, *backs)


def weight_grad_kernel(rows, acts, got, up_out, down_out, total, sem):
    copies = Copies(sem)
    half = total.shape[1]
    step = 128
    leave = []
    for i, out in enumerate((up_out, down_out)):
        for n in range(0, half, step):
            mine = dot(rows[i, :, n : n + step], acts[i], 0, 0).astype(BF16).astype(F32)
            total[i, n : n + step, :] = (mine + got[i, n : n + step, :].astype(F32)).astype(BF16)
            leave.append(copies.start(total.at[i, pl.ds(n, step), :], out.at[pl.ds(n, step), :]))
    wait(leave)


def weight_grads(kept_rows, kept_acts, got):
    _, count, width = kept_rows.shape
    hid = kept_acts.shape[2]
    half = width // 2
    return pl.pallas_call(
        weight_grad_kernel,
        out_shape=[jax.ShapeDtypeStruct((half, hid), BF16)] * 2,
        grid=(1,),
        in_specs=[
            pl.BlockSpec((2, count, half), lambda i: (0, 0, 0)),
            pl.BlockSpec((2, count, hid), lambda i: (0, 0, 0)),
            pl.BlockSpec((2, half, hid), lambda i: (0, 0, 0)),
        ],
        out_specs=[ANY] * 2,
        scratch_shapes=[pltpu.VMEM((2, half, hid), BF16), pltpu.SemaphoreType.DMA((2 * (half // 128),))],
        compiler_params=pltpu.CompilerParams(vmem_limit_bytes=40 * 2**20),
        cost_estimate=SMALL,
        name="weight_grads",
    )(kept_rows, kept_acts, got)


def local(tokens, grad_output, gate_prob, expert_index, slot_index, up_weight, down_weight):
    experts = lax.axis_size("expert")
    tensor_size = lax.axis_size("tensor")
    tok_count, width = tokens.shape
    capacity = 2 * tok_count // experts
    share = width // tensor_size

    def swap(x):
        return lax.ppermute(x, "dp", [(0, 1), (1, 0)])

    def across(x, j):
        return lax.ppermute(x, "tensor", [(i, i ^ j) for i in range(tensor_size)])

    def shift(x, k):
        return lax.ppermute(x, "expert", [(i, (i + k) % experts) for i in range(experts)])

    def after(x, *others):
        return lax.optimization_barrier((x,) + others)[0]

    def spread(rows, *before):
        x, y = across(rows, 1), across(rows, 2)
        half_y, half_x = y[:, :share], x[:, share:]
        if before:
            half_y, half_x = after(half_y, *before), after(half_x, *before)
        return [rows, x, y, across(half_y, 1), across(half_x, 2)]

    def collect(blocks):
        got = [across(blocks[j], j) for j in (1, 2, 3)]
        terms = [b.astype(F32) for b in [blocks[0]] + got]
        return (terms[0] + terms[1] + (terms[2] + terms[3])).astype(BF16), got

    def collect_pair(pair, step):
        keep, send = pair
        got = across(send, step)
        last = across((keep[1].astype(F32) + got[1].astype(F32)).astype(BF16), 3 - step)
        return (keep[0].astype(F32) + got[0].astype(F32) + last.astype(F32)).astype(BF16), got

    def other_halves(kept):
        rows, acts = kept
        dims = (((1,), (1,)), ((0,), (0,)))
        return lax.dot_general(rows[:, :, width // 2 :], acts, dims, preferred_element_type=F32).astype(BF16)

    index, slot = expert_index.reshape(1, tok_count), slot_index.reshape(1, tok_count)
    gate = gate_prob.reshape(1, tok_count)
    up_own, down_own = up_weight[0], down_weight[0]
    weights = [up_own, swap(up_own), down_own, swap(down_own)]

    if experts == 4:
        shifts = [1, 3, 2]
        placed = place([capacity] * 3, shifts, capacity, True, index, slot, gate, tokens, grad_output)
        moved = [shift(rows, k) for rows, k in zip(placed, shifts)]
        everything = 4 * capacity
        kept, (pair,) = expert_rows(placed[3:], None, [(capacity, 1)], weights, everything, 0, None)
        near = spread(jnp.concatenate([after(moved[0], pair[0]), moved[1]], 0))
        far = spread(after(moved[2], *near[1:3]))
        near[0] = after(near[0], *far[1:3])
        back, got_own = collect_pair([pair[0], after(pair[1], *near[3:])], 1)
        backs = [back]
        kept, pairs = expert_rows(near, 0, [(capacity, 1), (capacity, 2)], weights, everything, capacity, kept)
        (one, got_one), (three, got_three) = collect_pair(pairs[0], 1), collect_pair(pairs[1], 2)
        backs += [shift(one, -1), shift(three, -3)]
        kept, (blocks,) = expert_rows(
            [after(far[0], got_own)] + far[1:], 0, [(capacity, None)], weights, everything, 3 * capacity, kept
        )
        others = other_halves([kept[0], after(kept[1], got_one, got_three)])
        grads = weight_grads(*kept, swap(others))
        two, _ = collect([blocks[0]] + [after(b, got_one, got_three) for b in blocks[1:]])
        backs.append(after(shift(two, -2), *grads))
        shifts = [0] + shifts
    else:
        rows = experts * capacity
        shifts = [None]

        def exchange(x):
            moved = lax.all_to_all(
                x.reshape(experts, capacity, x.shape[1]), "expert", split_axis=0, concat_axis=0, tiled=True
            )
            return moved.reshape(rows, x.shape[1])

        (send,) = place([rows], shifts, capacity, False, index, slot, gate, tokens, grad_output)
        kept, (blocks,) = expert_rows(spread(exchange(send)), 0, [(rows, None)], weights, rows, 0, None)
        others = other_halves(kept)
        grads = weight_grads(*kept, swap(others))
        total, _ = collect(blocks)
        backs = [exchange(total)]

    return unplace(shifts, capacity, index, slot, backs), grads[0][None], grads[1][None]


def solution(mesh):
    placed = (
        P(("expert", "dp"), None),
        P(("expert", "dp"), None),
        P(("expert", "dp")),
        P(("expert", "dp"), None),
        P(("expert", "dp"), None),
        P("expert", "dp", "tensor"),
        P("expert", "dp", "tensor"),
    )
    return jax.shard_map(
        local,
        mesh=mesh,
        in_specs=placed,
        out_specs=(
            P(("expert", "dp"), "tensor"),
            P("expert", "dp", "tensor"),
            P("expert", "dp", "tensor"),
        ),
        check_vma=False,
    )
```

```python
import functools

import jax
import jax.numpy as jnp
from jax import lax
from jax.experimental import pallas as pl
from jax.experimental.pallas import tpu as pltpu
from jax.sharding import PartitionSpec as P

F32 = jnp.float32
BF16 = jnp.bfloat16
I32 = jnp.int32
ANY = pl.BlockSpec(memory_space=pl.ANY)
VMEM = pl.BlockSpec(memory_space=pltpu.VMEM)
SMEM = pl.BlockSpec(memory_space=pltpu.SMEM)
HBM = pl.BlockSpec(memory_space=pltpu.HBM)
LIMIT = 22 * 2**20
SMALL = pl.CostEstimate(flops=1000, bytes_accessed=1000, transcendentals=0)


def dot(lhs, rhs, left=1, right=0):
    return lax.dot_general(lhs, rhs, (((left,), (right,)), ((), ())), preferred_element_type=F32)


def hits(position, first, rows):
    ids = lax.broadcasted_iota(I32, (rows, position.shape[1]), 0) + first
    return ids == position


def places(index, slot, capacity):
    return index[...] * capacity + slot[...]


def expert_first(k, capacity):
    experts = lax.axis_size("expert")
    return 0 if k is None else lax.rem(lax.axis_index("expert") + k, experts) * capacity


def gate_of(hit, gate):
    return jnp.sum(jnp.where(hit, gate, 0.0), axis=1, keepdims=True)


class Copies:
    def __init__(self, sem):
        self.sem, self.count = sem, 0

    def start(self, src, dst):
        copy = pltpu.make_async_copy(src, dst, self.sem.at[self.count])
        self.count += 1
        copy.start()
        return copy

    def rows(self, src, dst, count, pieces):
        step = count // pieces
        return [self.start(src.at[pl.ds(i * step, step), :], dst.at[pl.ds(i * step, step), :]) for i in range(pieces)]


def wait(copies):
    for copy in copies:
        copy.wait()


def place_kernel(spans, shifts, capacity, index, slot, gate, tokens, grad_output, *refs):
    sends, (index_in, slot_in, gate_in, tok, grad, packed, sem) = refs[: len(spans)], refs[len(spans) :]
    copies = Copies(sem)
    count, share = tok.shape
    columns = pl.ds(pl.multiple_of(lax.axis_index("tensor") * share, share), share)
    small = [copies.start(src, dst) for src, dst in ((index, index_in), (slot, slot_in), (gate, gate_in))]
    arrive = copies.rows(tokens.at[:, columns], tok, count, 4) + copies.rows(grad_output.at[:, columns], grad, count, 4)
    wait(small)
    position = places(index_in, slot_in, capacity)
    found = [hits(position, expert_first(k, capacity), rows) for k, rows in zip(shifts, spans)]
    scales = [gate_of(hit, gate_in[...]) for hit in found]
    hots = [hit.astype(BF16) for hit in found]
    wait(arrive)
    leave = []
    at = 0
    for hot, scale, rows, out in zip(hots, scales, spans, sends):
        packed[at : at + rows, :share] = dot(hot, tok[...]).astype(BF16)
        packed[at : at + rows, share:] = (dot(hot, grad[...]) * scale).astype(BF16)
        leave += copies.rows(packed.at[pl.ds(at, rows), :], out, rows, 2)
        at += rows
    wait(leave)


def place(spans, shifts, capacity, index, slot, gate, tokens, grad_output):
    count, width = tokens.shape
    share = width // 4
    buf = lambda *shape: pltpu.VMEM(shape, BF16)
    return pl.pallas_call(
        functools.partial(place_kernel, spans, shifts, capacity),
        out_shape=[jax.ShapeDtypeStruct((rows, 2 * share), BF16) for rows in spans],
        in_specs=[ANY] * 5,
        out_specs=[ANY] * len(spans),
        scratch_shapes=[
            pltpu.VMEM((1, count), I32), pltpu.VMEM((1, count), I32), pltpu.VMEM((1, count), F32),
            buf(count, share), buf(count, share), buf(sum(spans), 2 * share),
            pltpu.SemaphoreType.DMA((11 + 2 * len(spans),)),
        ],
        compiler_params=pltpu.CompilerParams(vmem_limit_bytes=54 * 2**20),
        cost_estimate=SMALL,
        name="place_rows",
    )(index, slot, gate, tokens, grad_output)


def gelu_parts(pre):
    c = 0.7978845608028654
    square = pre * pre
    th = jnp.tanh(c * (pre + 0.044715 * (pre * square)))
    half = 0.5 * (1.0 + th)
    return pre * half, half + 0.5 * pre * (1.0 - th * th) * (c + (3 * 0.044715 * c) * square)


def expert_kernel(first, base, groups, aliased, *refs):
    refs = list(refs)
    take = lambda n: [refs.pop(0) for _ in range(n)]
    slots = take(5)
    up_halves, down_halves = take(2), take(2)
    take(aliased)
    kept_rows, kept_acts = take(2)
    targets = [take(4 if step is None else 2) for _, step in groups]
    tok, grad, up, down, hidden, slope, back = take(7)
    if first is None:
        tok_in, grad_in = take(2)
    copies = Copies(take(1)[0])
    rows, width = tok.shape
    half, share = width // 2, width // 4
    order = lax.axis_index("tensor") ^ (2 * lax.axis_index("dp"))
    arrive = []
    if first is None:
        mine = lax.axis_index("dp")
        count = tok_in.shape[0]
        for src, dst in zip(slots[3:], (tok_in, grad_in)):
            for i, start in enumerate((mine * half, (1 - mine) * half)):
                source = src.at[:, pl.ds(pl.multiple_of(start, half), half)]
                arrive += copies.rows(source, dst.at[:, pl.ds(i * half, half)], count, 2)
    else:
        span = pl.ds(first, rows)
        for j in range(4):
            columns = pl.ds(pl.multiple_of((order ^ j) * share, share), share)
            if j < 3:
                sources = [slots[j].at[span, pl.ds(0, share)], slots[j].at[span, pl.ds(share, share)]]
            else:
                sources = [slots[3].at[span, :], slots[4].at[span, :]]
            arrive += [copies.start(src, dst.at[:, columns]) for src, dst in zip(sources, (tok, grad))]
    hid = hidden.shape[1]
    step = 256
    tiles = []
    for n in range(0, hid, step):
        cols = pl.ds(n, step)
        tiles.append([])
        for halves, dst in ((up_halves, up), (down_halves, down)):
            for i in range(2):
                tiles[-1].append(copies.start(halves[i].at[:, cols], dst.at[pl.ds(i * half, half), cols]))
    if first is None:
        hit = hits(places(slots[0], slots[1], rows), expert_first(0, rows), rows)
        hot, scale = hit.astype(BF16), gate_of(hit, slots[2][...])
    wait(arrive)
    if first is None:
        tok[...] = dot(hot, tok_in[...]).astype(BF16)
        grad[...] = (dot(hot, grad_in[...]) * scale).astype(BF16)
    mine = pl.ds(base, rows)
    leave = [copies.start(src, kept_rows.at[i, mine, :]) for i, src in enumerate((tok, grad))]
    for n, arrived in zip(range(0, hid, step), tiles):
        cols = slice(n, n + step)
        wait(arrived)
        pre = dot(tok[...], up[:, cols])
        hidden_grad = dot(grad[...], down[:, cols])
        act, deriv = gelu_parts(pre)
        hidden[:, cols] = act.astype(BF16)
        slope[:, cols] = (hidden_grad * deriv).astype(BF16)
    leave += [copies.start(src, kept_acts.at[i, mine, :]) for i, src in enumerate((slope, hidden))]
    for j in range(4):
        quarter = pl.ds(pl.multiple_of((order ^ j) * share, share), share)
        back[j] = dot(slope[...], up[quarter, :], 1, 1).astype(BF16)
        at = 0
        for (n, step), outs in zip(groups, targets):
            out = outs[j] if step is None else outs[(j & step) // step].at[(j & (3 - step)) // (3 - step)]
            leave.append(copies.start(back.at[j, pl.ds(at, n), :], out))
            at += n
    wait(leave)


def expert_rows(slots, first, groups, weights, total_rows, base, kept):
    rows = sum(n for n, _ in groups)
    half, hid = weights[0].shape
    width, share = 2 * half, half // 2
    operands = list(slots) + list(weights) + list(kept or [])
    aliases = {len(slots) + 4 + i: i for i in range(2)} if kept else {}
    shape = lambda *s: jax.ShapeDtypeStruct(s, BF16)
    buf = lambda *s: pltpu.VMEM(s, BF16)
    quarters = [[shape(n, share)] * 4 if step is None else [shape(2, n, share)] * 2 for n, step in groups]
    counts = [len(q) for q in quarters]
    out = pl.pallas_call(
        functools.partial(expert_kernel, first, base, groups, len(aliases)),
        out_shape=[shape(2, total_rows, width), shape(2, total_rows, hid)] + sum(quarters, []),
        in_specs=([VMEM] * 3 if first is None else [ANY] * 3) + [ANY] * (len(operands) - 3),
        out_specs=[ANY] * (2 + sum(counts)),
        scratch_shapes=[
            buf(rows, width), buf(rows, width), buf(width, hid), buf(width, hid),
            buf(rows, hid), buf(rows, hid), buf(4, rows, share),
        ]
        + ([buf(*slots[3].shape)] * 2 if first is None else [])
        + [pltpu.SemaphoreType.DMA((12 + 4 * (hid // 256) + 4 * len(groups),))],
        input_output_aliases=aliases,
        compiler_params=pltpu.CompilerParams(vmem_limit_bytes=LIMIT + rows * 2**15),
        cost_estimate=pl.CostEstimate(
            flops=6 * rows * width * hid, bytes_accessed=4 * width * hid + 8 * rows * width, transcendentals=rows * hid
        ),
        name="expert_rows",
    )(*operands)
    starts = [2 + sum(counts[:i]) for i in range(len(counts))]
    return list(out[:2]), [list(out[i : i + n]) for i, n in zip(starts, counts)]


def unplace_kernel(spans, shifts, capacity, index, slot, *refs):
    out = refs[-1]
    position = places(index, slot, capacity)
    total = None
    for k, rows, back in zip(shifts, spans, refs[:-1]):
        hot = hits(position, expert_first(k, capacity), rows).astype(BF16)
        part = dot(hot, back[...], 0, 0)
        total = part if total is None else total + part
    out[...] = total.astype(BF16)


def unplace(shifts, capacity, index, slot, backs):
    spans = [b.shape[0] for b in backs]
    count, share = index.shape[1], backs[0].shape[1]
    return pl.pallas_call(
        functools.partial(unplace_kernel, spans, shifts, capacity),
        out_shape=jax.ShapeDtypeStruct((count, share), BF16),
        in_specs=[VMEM] * (2 + len(backs)),
        out_specs=VMEM,
        compiler_params=pltpu.CompilerParams(vmem_limit_bytes=LIMIT),
        cost_estimate=SMALL,
        name="unplace_rows",
    )(index, slot, *backs)


def weight_grad_kernel(rows, acts, got, up_out, down_out, total, sem):
    copies = Copies(sem)
    half = total.shape[1]
    step = 128
    leave = []
    for i, out in enumerate((up_out, down_out)):
        for n in range(0, half, step):
            mine = dot(rows[i, :, n : n + step], acts[i], 0, 0).astype(BF16).astype(F32)
            total[i, n : n + step, :] = (mine + got[i, n : n + step, :].astype(F32)).astype(BF16)
            leave.append(copies.start(total.at[i, pl.ds(n, step), :], out.at[pl.ds(n, step), :]))
    wait(leave)


def weight_grads(kept_rows, kept_acts, got):
    _, count, width = kept_rows.shape
    hid = kept_acts.shape[2]
    half = width // 2
    return pl.pallas_call(
        weight_grad_kernel,
        out_shape=[jax.ShapeDtypeStruct((half, hid), BF16)] * 2,
        grid=(1,),
        in_specs=[
            pl.BlockSpec((2, count, half), lambda i: (0, 0, 0)),
            pl.BlockSpec((2, count, hid), lambda i: (0, 0, 0)),
            pl.BlockSpec((2, half, hid), lambda i: (0, 0, 0)),
        ],
        out_specs=[ANY] * 2,
        scratch_shapes=[pltpu.VMEM((2, half, hid), BF16), pltpu.SemaphoreType.DMA((2 * (half // 128),))],
        compiler_params=pltpu.CompilerParams(vmem_limit_bytes=40 * 2**20),
        cost_estimate=SMALL,
        name="weight_grads",
    )(kept_rows, kept_acts, got)


def local(tokens, grad_output, gate_prob, expert_index, slot_index, up_weight, down_weight):
    experts = lax.axis_size("expert")
    tensor_size = lax.axis_size("tensor")
    tok_count, width = tokens.shape
    capacity = 2 * tok_count // experts
    share = width // tensor_size

    def swap(x):
        return lax.ppermute(x, "dp", [(0, 1), (1, 0)])

    def across(x, j):
        return lax.ppermute(x, "tensor", [(i, i ^ j) for i in range(tensor_size)])

    def shift(x, k):
        return lax.ppermute(x, "expert", [(i, (i + k) % experts) for i in range(experts)])

    def after(x, *others):
        return lax.optimization_barrier((x,) + others)[0]

    def spread(rows, *before):
        x, y = across(rows, 1), across(rows, 2)
        half_y, half_x = y[:, :share], x[:, share:]
        if before:
            half_y, half_x = after(half_y, *before), after(half_x, *before)
        return [rows, x, y, across(half_y, 1), across(half_x, 2)]

    def collect(blocks):
        got = [across(blocks[j], j) for j in (1, 2, 3)]
        terms = [b.astype(F32) for b in [blocks[0]] + got]
        return (terms[0] + terms[1] + (terms[2] + terms[3])).astype(BF16), got

    def collect_pair(pair, step):
        keep, send = pair
        got = across(send, step)
        last = across((keep[1].astype(F32) + got[1].astype(F32)).astype(BF16), 3 - step)
        return (keep[0].astype(F32) + got[0].astype(F32) + last.astype(F32)).astype(BF16), got

    def other_halves(kept):
        rows, acts = kept
        dims = (((1,), (1,)), ((0,), (0,)))
        return lax.dot_general(rows[:, :, width // 2 :], acts, dims, preferred_element_type=F32).astype(BF16)

    index, slot = expert_index.reshape(1, tok_count), slot_index.reshape(1, tok_count)
    gate = gate_prob.reshape(1, tok_count)
    up_own, down_own = up_weight[0], down_weight[0]
    weights = [up_own, swap(up_own), down_own, swap(down_own)]

    if experts == 4:
        shifts = [1, 3, 2]
        sends = place([capacity] * 3, shifts, capacity, index, slot, gate, tokens, grad_output)
        moved = [shift(rows, k) for rows, k in zip(sends, shifts)]
        everything = 4 * capacity
        own = [index, slot, gate, tokens, grad_output]
        kept, (pair,) = expert_rows(own, None, [(capacity, 1)], weights, everything, 0, None)
        near = spread(jnp.concatenate([after(moved[0], pair[0]), moved[1]], 0))
        far = spread(after(moved[2], *near[1:3]))
        near[0] = after(near[0], *far[1:3])
        back, got_own = collect_pair([pair[0], after(pair[1], *near[3:])], 1)
        kept, (blocks,) = expert_rows(near, 0, [(2 * capacity, None)], weights, everything, capacity, kept)
        total, got = collect(blocks)
        backs = [back, shift(total[:capacity], -1), shift(total[capacity:], -3)]
        slots = [after(far[0], got_own)] + far[1:]
        kept, (blocks,) = expert_rows(slots, 0, [(capacity, None)], weights, everything, 3 * capacity, kept)
        others = other_halves(kept)
        grads = weight_grads(*kept, swap(after(others, *got)))
        total, _ = collect([blocks[0]] + [after(b, got[0], others) for b in blocks[1:]])
        backs.append(after(shift(total, -2), *grads))
        shifts = [0] + shifts
    else:
        rows = experts * capacity
        shifts = [None]

        def exchange(x):
            moved = lax.all_to_all(
                x.reshape(experts, capacity, x.shape[1]), "expert", split_axis=0, concat_axis=0, tiled=True
            )
            return moved.reshape(rows, x.shape[1])

        (send,) = place([rows], shifts, capacity, index, slot, gate, tokens, grad_output)
        kept, (blocks,) = expert_rows(spread(exchange(send)), 0, [(rows, None)], weights, rows, 0, None)
        others = other_halves(kept)
        grads = weight_grads(*kept, swap(others))
        total, _ = collect(blocks)
        backs = [exchange(total)]

    return unplace(shifts, capacity, index, slot, backs), grads[0][None], grads[1][None]


def solution(mesh):
    placed = (
        P(("expert", "dp"), None),
        P(("expert", "dp"), None),
        P(("expert", "dp")),
        P(("expert", "dp"), None),
        P(("expert", "dp"), None),
        P("expert", "dp", "tensor"),
        P("expert", "dp", "tensor"),
    )
    return jax.shard_map(
        local,
        mesh=mesh,
        in_specs=placed,
        out_specs=(
            P(("expert", "dp"), "tensor"),
            P("expert", "dp", "tensor"),
            P("expert", "dp", "tensor"),
        ),
        check_vma=False,
    )
```

```python
import functools

import jax
import jax.numpy as jnp
from jax import lax
from jax.experimental import pallas as pl
from jax.experimental.pallas import tpu as pltpu
from jax.sharding import PartitionSpec as P

F32 = jnp.float32
BF16 = jnp.bfloat16
I32 = jnp.int32
ANY = pl.BlockSpec(memory_space=pl.ANY)
VMEM = pl.BlockSpec(memory_space=pltpu.VMEM)
SMEM = pl.BlockSpec(memory_space=pltpu.SMEM)
HBM = pl.BlockSpec(memory_space=pltpu.HBM)
LIMIT = 22 * 2**20
SMALL = pl.CostEstimate(flops=1000, bytes_accessed=1000, transcendentals=0)


def dot(lhs, rhs, left=1, right=0):
    return lax.dot_general(lhs, rhs, (((left,), (right,)), ((), ())), preferred_element_type=F32)


def hits(position, first, rows):
    ids = lax.broadcasted_iota(I32, (rows, position.shape[1]), 0) + first
    return ids == position


def places(index, slot, capacity):
    return index[...] * capacity + slot[...]


def expert_first(k, capacity):
    experts = lax.axis_size("expert")
    return 0 if k is None else lax.rem(lax.axis_index("expert") + k, experts) * capacity


def gate_of(hit, gate):
    return jnp.sum(jnp.where(hit, gate, 0.0), axis=1, keepdims=True)


class Copies:
    def __init__(self, sem):
        self.sem, self.count = sem, 0

    def start(self, src, dst):
        copy = pltpu.make_async_copy(src, dst, self.sem.at[self.count])
        self.count += 1
        copy.start()
        return copy

    def rows(self, src, dst, count, pieces):
        step = count // pieces
        return [self.start(src.at[pl.ds(i * step, step), :], dst.at[pl.ds(i * step, step), :]) for i in range(pieces)]


def wait(copies):
    for copy in copies:
        copy.wait()


def place_kernel(spans, shifts, capacity, index, slot, gate, tokens, grad_output, *refs):
    sends, (index_in, slot_in, gate_in, tok, grad, packed, sem) = refs[: len(spans)], refs[len(spans) :]
    copies = Copies(sem)
    count, share = tok.shape
    columns = pl.ds(pl.multiple_of(lax.axis_index("tensor") * share, share), share)
    small = [copies.start(src, dst) for src, dst in ((index, index_in), (slot, slot_in), (gate, gate_in))]
    arrive = copies.rows(tokens.at[:, columns], tok, count, 4) + copies.rows(grad_output.at[:, columns], grad, count, 4)
    wait(small)
    position = places(index_in, slot_in, capacity)
    found = [hits(position, expert_first(k, capacity), rows) for k, rows in zip(shifts, spans)]
    scales = [gate_of(hit, gate_in[...]) for hit in found]
    hots = [hit.astype(BF16) for hit in found]
    wait(arrive)
    leave = []
    at = 0
    for hot, scale, rows, out in zip(hots, scales, spans, sends):
        packed[at : at + rows, :share] = dot(hot, tok[...]).astype(BF16)
        packed[at : at + rows, share:] = (dot(hot, grad[...]) * scale).astype(BF16)
        leave += copies.rows(packed.at[pl.ds(at, rows), :], out, rows, 2)
        at += rows
    wait(leave)


def place(spans, shifts, capacity, index, slot, gate, tokens, grad_output):
    count, width = tokens.shape
    share = width // 4
    buf = lambda *shape: pltpu.VMEM(shape, BF16)
    return pl.pallas_call(
        functools.partial(place_kernel, spans, shifts, capacity),
        out_shape=[jax.ShapeDtypeStruct((rows, 2 * share), BF16) for rows in spans],
        in_specs=[ANY] * 5,
        out_specs=[ANY] * len(spans),
        scratch_shapes=[
            pltpu.VMEM((1, count), I32), pltpu.VMEM((1, count), I32), pltpu.VMEM((1, count), F32),
            buf(count, share), buf(count, share), buf(sum(spans), 2 * share),
            pltpu.SemaphoreType.DMA((11 + 2 * len(spans),)),
        ],
        compiler_params=pltpu.CompilerParams(vmem_limit_bytes=54 * 2**20),
        cost_estimate=SMALL,
        name="place_rows",
    )(index, slot, gate, tokens, grad_output)


def gelu_parts(pre):
    c = 0.7978845608028654
    square = pre * pre
    th = jnp.tanh(c * (pre + 0.044715 * (pre * square)))
    half = 0.5 * (1.0 + th)
    return pre * half, half + 0.5 * pre * (1.0 - th * th) * (c + (3 * 0.044715 * c) * square)


def expert_kernel(chunks, base, groups, aliased, *refs):
    refs = list(refs)
    take = lambda n: [refs.pop(0) for _ in range(n)]
    slots = take(5) if chunks is None else [take(n) for n in chunks]
    up_halves, down_halves = take(2), take(2)
    take(aliased)
    kept_rows, kept_acts = take(2)
    targets = [take(4 if step is None else 2) for _, step in groups]
    tok, grad, up, down, hidden, slope, back = take(7)
    if chunks is None:
        tok_in, grad_in = take(2)
    copies = Copies(take(1)[0])
    rows, width = tok.shape
    half, share = width // 2, width // 4
    order = lax.axis_index("tensor") ^ (2 * lax.axis_index("dp"))
    arrive = []
    if chunks is None:
        mine = lax.axis_index("dp")
        count = tok_in.shape[0]
        for src, dst in zip(slots[3:], (tok_in, grad_in)):
            for i, start in enumerate((mine * half, (1 - mine) * half)):
                source = src.at[:, pl.ds(pl.multiple_of(start, half), half)]
                arrive += copies.rows(source, dst.at[:, pl.ds(i * half, half)], count, 2)
    else:
        at = 0
        for chunk in slots:
            n = chunk[0].shape[0]
            for j in range(4):
                columns = pl.ds(pl.multiple_of((order ^ j) * share, share), share)
                if j == 3 and len(chunk) == 5:
                    sources = chunk[3:]
                else:
                    sources = [chunk[j].at[:, pl.ds(i * share, share)] for i in range(2)]
                arrive += [copies.start(src, dst.at[pl.ds(at, n), columns]) for src, dst in zip(sources, (tok, grad))]
            at += n
    hid = hidden.shape[1]
    step = 256
    tiles = []
    for n in range(0, hid, step):
        cols = pl.ds(n, step)
        tiles.append([])
        for halves, dst in ((up_halves, up), (down_halves, down)):
            for i in range(2):
                tiles[-1].append(copies.start(halves[i].at[:, cols], dst.at[pl.ds(i * half, half), cols]))
    if chunks is None:
        hit = hits(places(slots[0], slots[1], rows), expert_first(0, rows), rows)
        hot, scale = hit.astype(BF16), gate_of(hit, slots[2][...])
    wait(arrive)
    if chunks is None:
        tok[...] = dot(hot, tok_in[...]).astype(BF16)
        grad[...] = (dot(hot, grad_in[...]) * scale).astype(BF16)
    mine = pl.ds(base, rows)
    leave = [copies.start(src, kept_rows.at[i, mine, :]) for i, src in enumerate((tok, grad))]
    for n, arrived in zip(range(0, hid, step), tiles):
        cols = slice(n, n + step)
        wait(arrived)
        pre = dot(tok[...], up[:, cols])
        hidden_grad = dot(grad[...], down[:, cols])
        act, deriv = gelu_parts(pre)
        hidden[:, cols] = act.astype(BF16)
        slope[:, cols] = (hidden_grad * deriv).astype(BF16)
    leave += [copies.start(src, kept_acts.at[i, mine, :]) for i, src in enumerate((slope, hidden))]
    for j in range(4):
        quarter = pl.ds(pl.multiple_of((order ^ j) * share, share), share)
        back[j] = dot(slope[...], up[quarter, :], 1, 1).astype(BF16)
        at = 0
        for (n, step), outs in zip(groups, targets):
            out = outs[j] if step is None else outs[(j & step) // step].at[(j & (3 - step)) // (3 - step)]
            leave.append(copies.start(back.at[j, pl.ds(at, n), :], out))
            at += n
    wait(leave)


def expert_rows(own, chunks, groups, weights, total_rows, base, kept):
    slots = own or sum(chunks, [])
    counts_in = None if own else [len(c) for c in chunks]
    rows = sum(n for n, _ in groups)
    half, hid = weights[0].shape
    width, share = 2 * half, half // 2
    operands = list(slots) + list(weights) + list(kept or [])
    aliases = {len(slots) + 4 + i: i for i in range(2)} if kept else {}
    shape = lambda *s: jax.ShapeDtypeStruct(s, BF16)
    buf = lambda *s: pltpu.VMEM(s, BF16)
    quarters = [[shape(n, share)] * 4 if step is None else [shape(2, n, share)] * 2 for n, step in groups]
    counts = [len(q) for q in quarters]
    out = pl.pallas_call(
        functools.partial(expert_kernel, counts_in, base, groups, len(aliases)),
        out_shape=[shape(2, total_rows, width), shape(2, total_rows, hid)] + sum(quarters, []),
        in_specs=([VMEM] * 3 if own else [ANY] * 3) + [ANY] * (len(operands) - 3),
        out_specs=[ANY] * (2 + sum(counts)),
        scratch_shapes=[
            buf(rows, width), buf(rows, width), buf(width, hid), buf(width, hid),
            buf(rows, hid), buf(rows, hid), buf(4, rows, share),
        ]
        + ([buf(*own[3].shape)] * 2 if own else [])
        + [pltpu.SemaphoreType.DMA((16 + 4 * (hid // 256) + 4 * len(groups) + 4,))],
        input_output_aliases=aliases,
        compiler_params=pltpu.CompilerParams(vmem_limit_bytes=LIMIT + rows * 2**15),
        cost_estimate=pl.CostEstimate(
            flops=6 * rows * width * hid, bytes_accessed=4 * width * hid + 8 * rows * width, transcendentals=rows * hid
        ),
        name="expert_rows",
    )(*operands)
    starts = [2 + sum(counts[:i]) for i in range(len(counts))]
    return list(out[:2]), [list(out[i : i + n]) for i, n in zip(starts, counts)]


def unplace_kernel(spans, shifts, capacity, index, slot, *refs):
    out = refs[-1]
    position = places(index, slot, capacity)
    total = None
    for k, rows, back in zip(shifts, spans, refs[:-1]):
        hot = hits(position, expert_first(k, capacity), rows).astype(BF16)
        part = dot(hot, back[...], 0, 0)
        total = part if total is None else total + part
    out[...] = total.astype(BF16)


def unplace(shifts, capacity, index, slot, backs):
    spans = [b.shape[0] for b in backs]
    count, share = index.shape[1], backs[0].shape[1]
    return pl.pallas_call(
        functools.partial(unplace_kernel, spans, shifts, capacity),
        out_shape=jax.ShapeDtypeStruct((count, share), BF16),
        in_specs=[VMEM] * (2 + len(backs)),
        out_specs=VMEM,
        compiler_params=pltpu.CompilerParams(vmem_limit_bytes=LIMIT),
        cost_estimate=SMALL,
        name="unplace_rows",
    )(index, slot, *backs)


def weight_grad_kernel(rows, acts, got, up_out, down_out, total, sem):
    copies = Copies(sem)
    half = total.shape[1]
    step = 128
    leave = []
    for i, out in enumerate((up_out, down_out)):
        for n in range(0, half, step):
            mine = dot(rows[i, :, n : n + step], acts[i], 0, 0).astype(BF16).astype(F32)
            total[i, n : n + step, :] = (mine + got[i, n : n + step, :].astype(F32)).astype(BF16)
            leave.append(copies.start(total.at[i, pl.ds(n, step), :], out.at[pl.ds(n, step), :]))
    wait(leave)


def weight_grads(kept_rows, kept_acts, got):
    _, count, width = kept_rows.shape
    hid = kept_acts.shape[2]
    half = width // 2
    return pl.pallas_call(
        weight_grad_kernel,
        out_shape=[jax.ShapeDtypeStruct((half, hid), BF16)] * 2,
        grid=(1,),
        in_specs=[
            pl.BlockSpec((2, count, half), lambda i: (0, 0, 0)),
            pl.BlockSpec((2, count, hid), lambda i: (0, 0, 0)),
            pl.BlockSpec((2, half, hid), lambda i: (0, 0, 0)),
        ],
        out_specs=[ANY] * 2,
        scratch_shapes=[pltpu.VMEM((2, half, hid), BF16), pltpu.SemaphoreType.DMA((2 * (half // 128),))],
        compiler_params=pltpu.CompilerParams(vmem_limit_bytes=40 * 2**20),
        cost_estimate=SMALL,
        name="weight_grads",
    )(kept_rows, kept_acts, got)


def local(tokens, grad_output, gate_prob, expert_index, slot_index, up_weight, down_weight):
    experts = lax.axis_size("expert")
    tensor_size = lax.axis_size("tensor")
    tok_count, width = tokens.shape
    capacity = 2 * tok_count // experts
    share = width // tensor_size

    def swap(x):
        return lax.ppermute(x, "dp", [(0, 1), (1, 0)])

    def across(x, j):
        return lax.ppermute(x, "tensor", [(i, i ^ j) for i in range(tensor_size)])

    def shift(x, k):
        return lax.ppermute(x, "expert", [(i, (i + k) % experts) for i in range(experts)])

    def after(x, *others):
        return lax.optimization_barrier((x,) + others)[0]

    def spread(rows, *before):
        x, y = across(rows, 1), across(rows, 2)
        half_y, half_x = y[:, :share], x[:, share:]
        if before:
            half_y, half_x = after(half_y, *before), after(half_x, *before)
        return [rows, x, y, across(half_y, 1), across(half_x, 2)]

    def collect(blocks):
        got = [across(blocks[j], j) for j in (1, 2, 3)]
        terms = [b.astype(F32) for b in [blocks[0]] + got]
        return (terms[0] + terms[1] + (terms[2] + terms[3])).astype(BF16), got

    def collect_pair(pair, step):
        keep, send = pair
        got = across(send, step)
        last = across((keep[1].astype(F32) + got[1].astype(F32)).astype(BF16), 3 - step)
        return (keep[0].astype(F32) + got[0].astype(F32) + last.astype(F32)).astype(BF16), got

    def other_halves(kept):
        rows, acts = kept
        dims = (((1,), (1,)), ((0,), (0,)))
        return lax.dot_general(rows[:, :, width // 2 :], acts, dims, preferred_element_type=F32).astype(BF16)

    index, slot = expert_index.reshape(1, tok_count), slot_index.reshape(1, tok_count)
    gate = gate_prob.reshape(1, tok_count)
    up_own, down_own = up_weight[0], down_weight[0]
    weights = [up_own, swap(up_own), down_own, swap(down_own)]

    if experts == 4:
        shifts = [1, 2, 3]
        sends = place([capacity] * 3, shifts, capacity, index, slot, gate, tokens, grad_output)
        everything = 4 * capacity
        one = shift(sends[0], 1)
        two = shift(after(sends[1], one, weights[1], weights[3]), 2)
        own = [after(index, one), slot, gate, tokens, grad_output]
        kept, (pair,) = expert_rows(own, None, [(capacity, 1)], weights, everything, 0, None)
        first = spread(one)
        three = shift(after(sends[2], two, *first[1:3]), 3)
        second = spread(after(two, pair[0]))
        third = after(three, *second[1:3])
        third = [third] + [across(third, j) for j in (1, 2, 3)]
        back, got_own = collect_pair([pair[0], after(pair[1], *first[3:])], 1)
        kept, (blocks,) = expert_rows(
            None, [first, second], [(2 * capacity, None)], weights, everything, capacity, kept
        )
        total, got = collect(blocks)
        backs = [back, shift(total[:capacity], -1), shift(total[capacity:], -2)]
        third[0] = after(third[0], got_own)
        kept, (blocks,) = expert_rows(None, [third], [(capacity, None)], weights, everything, 3 * capacity, kept)
        others = other_halves(kept)
        grads = weight_grads(*kept, swap(after(others, *got)))
        total, _ = collect([blocks[0]] + [after(b, got[0], others) for b in blocks[1:]])
        backs.append(after(shift(total, -3), *grads))
        shifts = [0] + shifts
    else:
        rows = experts * capacity
        shifts = [None]

        def exchange(x):
            moved = lax.all_to_all(
                x.reshape(experts, capacity, x.shape[1]), "expert", split_axis=0, concat_axis=0, tiled=True
            )
            return moved.reshape(rows, x.shape[1])

        (send,) = place([rows], shifts, capacity, index, slot, gate, tokens, grad_output)
        kept, (blocks,) = expert_rows(None, [spread(exchange(send))], [(rows, None)], weights, rows, 0, None)
        others = other_halves(kept)
        grads = weight_grads(*kept, swap(others))
        total, _ = collect(blocks)
        backs = [exchange(total)]

    return unplace(shifts, capacity, index, slot, backs), grads[0][None], grads[1][None]


def solution(mesh):
    placed = (
        P(("expert", "dp"), None),
        P(("expert", "dp"), None),
        P(("expert", "dp")),
        P(("expert", "dp"), None),
        P(("expert", "dp"), None),
        P("expert", "dp", "tensor"),
        P("expert", "dp", "tensor"),
    )
    return jax.shard_map(
        local,
        mesh=mesh,
        in_specs=placed,
        out_specs=(
            P(("expert", "dp"), "tensor"),
            P("expert", "dp", "tensor"),
            P("expert", "dp", "tensor"),
        ),
        check_vma=False,
    )
```

```python
import functools

import jax
import jax.numpy as jnp
from jax import lax
from jax.experimental import pallas as pl
from jax.experimental.pallas import tpu as pltpu
from jax.sharding import PartitionSpec as P

F32 = jnp.float32
BF16 = jnp.bfloat16
I32 = jnp.int32
ANY = pl.BlockSpec(memory_space=pl.ANY)
VMEM = pl.BlockSpec(memory_space=pltpu.VMEM)
SMEM = pl.BlockSpec(memory_space=pltpu.SMEM)
HBM = pl.BlockSpec(memory_space=pltpu.HBM)
LIMIT = 22 * 2**20
SMALL = pl.CostEstimate(flops=1000, bytes_accessed=1000, transcendentals=0)


def dot(lhs, rhs, left=1, right=0):
    return lax.dot_general(lhs, rhs, (((left,), (right,)), ((), ())), preferred_element_type=F32)


def hits(position, first, rows):
    ids = lax.broadcasted_iota(I32, (rows, position.shape[1]), 0) + first
    return ids == position


def places(index, slot, capacity):
    return index[...] * capacity + slot[...]


def expert_first(k, capacity):
    experts = lax.axis_size("expert")
    return 0 if k is None else lax.rem(lax.axis_index("expert") + k, experts) * capacity


def gate_of(hit, gate):
    return jnp.sum(jnp.where(hit, gate, 0.0), axis=1, keepdims=True)


class Copies:
    def __init__(self, sem):
        self.sem, self.count = sem, 0

    def start(self, src, dst):
        copy = pltpu.make_async_copy(src, dst, self.sem.at[self.count])
        self.count += 1
        copy.start()
        return copy

    def rows(self, src, dst, count, pieces):
        step = count // pieces
        return [self.start(src.at[pl.ds(i * step, step), :], dst.at[pl.ds(i * step, step), :]) for i in range(pieces)]


def wait(copies):
    for copy in copies:
        copy.wait()


def place_kernel(spans, shifts, capacity, index, slot, gate, tokens, grad_output, *refs):
    sends, (index_in, slot_in, gate_in, tok, grad, packed, sem) = refs[: len(spans)], refs[len(spans) :]
    copies = Copies(sem)
    count, share = tok.shape
    columns = pl.ds(pl.multiple_of(lax.axis_index("tensor") * share, share), share)
    small = [copies.start(src, dst) for src, dst in ((index, index_in), (slot, slot_in), (gate, gate_in))]
    arrive = copies.rows(tokens.at[:, columns], tok, count, 4) + copies.rows(grad_output.at[:, columns], grad, count, 4)
    wait(small)
    position = places(index_in, slot_in, capacity)
    found = [hits(position, expert_first(k, capacity), rows) for k, rows in zip(shifts, spans)]
    scales = [gate_of(hit, gate_in[...]) for hit in found]
    hots = [hit.astype(BF16) for hit in found]
    wait(arrive)
    leave = []
    at = 0
    for hot, scale, rows, out in zip(hots, scales, spans, sends):
        packed[at : at + rows, :share] = dot(hot, tok[...]).astype(BF16)
        packed[at : at + rows, share:] = (dot(hot, grad[...]) * scale).astype(BF16)
        leave += copies.rows(packed.at[pl.ds(at, rows), :], out, rows, 2)
        at += rows
    wait(leave)


def place(spans, shifts, capacity, index, slot, gate, tokens, grad_output):
    count, width = tokens.shape
    share = width // 4
    buf = lambda *shape: pltpu.VMEM(shape, BF16)
    return pl.pallas_call(
        functools.partial(place_kernel, spans, shifts, capacity),
        out_shape=[jax.ShapeDtypeStruct((rows, 2 * share), BF16) for rows in spans],
        in_specs=[ANY] * 5,
        out_specs=[ANY] * len(spans),
        scratch_shapes=[
            pltpu.VMEM((1, count), I32), pltpu.VMEM((1, count), I32), pltpu.VMEM((1, count), F32),
            buf(count, share), buf(count, share), buf(sum(spans), 2 * share),
            pltpu.SemaphoreType.DMA((11 + 2 * len(spans),)),
        ],
        compiler_params=pltpu.CompilerParams(vmem_limit_bytes=54 * 2**20),
        cost_estimate=SMALL,
        name="place_rows",
    )(index, slot, gate, tokens, grad_output)


def gelu_parts(pre):
    c = 0.7978845608028654
    square = pre * pre
    th = jnp.tanh(c * (pre + 0.044715 * (pre * square)))
    half = 0.5 * (1.0 + th)
    return pre * half, half + 0.5 * pre * (1.0 - th * th) * (c + (3 * 0.044715 * c) * square)


def expert_kernel(chunks, base, groups, aliased, *refs):
    refs = list(refs)
    take = lambda n: [refs.pop(0) for _ in range(n)]
    slots = take(5) if chunks is None else [take(n) for n in chunks]
    up_halves, down_halves = take(2), take(2)
    take(aliased)
    kept_rows, kept_acts = take(2)
    targets = [take(4 if step is None else 2) for _, step in groups]
    tok, grad, up, down, hidden, slope, back = take(7)
    if chunks is None:
        tok_in, grad_in = take(2)
    copies = Copies(take(1)[0])
    rows, width = tok.shape
    half, share = width // 2, width // 4
    order = lax.axis_index("tensor") ^ (2 * lax.axis_index("dp"))
    arrive = []
    if chunks is None:
        mine = lax.axis_index("dp")
        count = tok_in.shape[0]
        for src, dst in zip(slots[3:], (tok_in, grad_in)):
            for i, start in enumerate((mine * half, (1 - mine) * half)):
                source = src.at[:, pl.ds(pl.multiple_of(start, half), half)]
                arrive += copies.rows(source, dst.at[:, pl.ds(i * half, half)], count, 2)
    else:
        at = 0
        for chunk in slots:
            n = chunk[0].shape[0]
            for j in range(4):
                columns = pl.ds(pl.multiple_of((order ^ j) * share, share), share)
                if j == 3 and len(chunk) == 5:
                    sources = chunk[3:]
                else:
                    sources = [chunk[j].at[:, pl.ds(i * share, share)] for i in range(2)]
                arrive += [copies.start(src, dst.at[pl.ds(at, n), columns]) for src, dst in zip(sources, (tok, grad))]
            at += n
    hid = hidden.shape[1]
    step = 256
    tiles = []
    for n in range(0, hid, step):
        cols = pl.ds(n, step)
        tiles.append([])
        for halves, dst in ((up_halves, up), (down_halves, down)):
            for i in range(2):
                tiles[-1].append(copies.start(halves[i].at[:, cols], dst.at[pl.ds(i * half, half), cols]))
    if chunks is None:
        hit = hits(places(slots[0], slots[1], rows), expert_first(0, rows), rows)
        hot, scale = hit.astype(BF16), gate_of(hit, slots[2][...])
    wait(arrive)
    if chunks is None:
        tok[...] = dot(hot, tok_in[...]).astype(BF16)
        grad[...] = (dot(hot, grad_in[...]) * scale).astype(BF16)
    mine = pl.ds(base, rows)
    leave = [copies.start(src, kept_rows.at[i, mine, :]) for i, src in enumerate((tok, grad))]
    for n, arrived in zip(range(0, hid, step), tiles):
        cols = slice(n, n + step)
        wait(arrived)
        pre = dot(tok[...], up[:, cols])
        hidden_grad = dot(grad[...], down[:, cols])
        act, deriv = gelu_parts(pre)
        hidden[:, cols] = act.astype(BF16)
        slope[:, cols] = (hidden_grad * deriv).astype(BF16)
    leave += [copies.start(src, kept_acts.at[i, mine, :]) for i, src in enumerate((slope, hidden))]
    for j in range(4):
        quarter = pl.ds(pl.multiple_of((order ^ j) * share, share), share)
        back[j] = dot(slope[...], up[quarter, :], 1, 1).astype(BF16)
        at = 0
        for (n, step), outs in zip(groups, targets):
            out = outs[j] if step is None else outs[(j & step) // step].at[(j & (3 - step)) // (3 - step)]
            leave.append(copies.start(back.at[j, pl.ds(at, n), :], out))
            at += n
    wait(leave)


def expert_rows(own, chunks, groups, weights, total_rows, base, kept):
    slots = own or sum(chunks, [])
    counts_in = None if own else [len(c) for c in chunks]
    rows = sum(n for n, _ in groups)
    half, hid = weights[0].shape
    width, share = 2 * half, half // 2
    operands = list(slots) + list(weights) + list(kept or [])
    aliases = {len(slots) + 4 + i: i for i in range(2)} if kept else {}
    shape = lambda *s: jax.ShapeDtypeStruct(s, BF16)
    buf = lambda *s: pltpu.VMEM(s, BF16)
    quarters = [[shape(n, share)] * 4 if step is None else [shape(2, n, share)] * 2 for n, step in groups]
    counts = [len(q) for q in quarters]
    out = pl.pallas_call(
        functools.partial(expert_kernel, counts_in, base, groups, len(aliases)),
        out_shape=[shape(2, total_rows, width), shape(2, total_rows, hid)] + sum(quarters, []),
        in_specs=([VMEM] * 3 if own else [ANY] * 3) + [ANY] * (len(operands) - 3),
        out_specs=[ANY] * (2 + sum(counts)),
        scratch_shapes=[
            buf(rows, width), buf(rows, width), buf(width, hid), buf(width, hid),
            buf(rows, hid), buf(rows, hid), buf(4, rows, share),
        ]
        + ([buf(*own[3].shape)] * 2 if own else [])
        + [pltpu.SemaphoreType.DMA((16 + 4 * (hid // 256) + 4 * len(groups) + 4,))],
        input_output_aliases=aliases,
        compiler_params=pltpu.CompilerParams(vmem_limit_bytes=LIMIT + rows * 2**15),
        cost_estimate=pl.CostEstimate(
            flops=6 * rows * width * hid, bytes_accessed=4 * width * hid + 8 * rows * width, transcendentals=rows * hid
        ),
        name="expert_rows",
    )(*operands)
    starts = [2 + sum(counts[:i]) for i in range(len(counts))]
    return list(out[:2]), [list(out[i : i + n]) for i, n in zip(starts, counts)]


def unplace_kernel(spans, shifts, capacity, index, slot, *refs):
    out = refs[-1]
    position = places(index, slot, capacity)
    total = None
    for k, rows, back in zip(shifts, spans, refs[:-1]):
        hot = hits(position, expert_first(k, capacity), rows).astype(BF16)
        part = dot(hot, back[...], 0, 0)
        total = part if total is None else total + part
    out[...] = total.astype(BF16)


def unplace(shifts, capacity, index, slot, backs):
    spans = [b.shape[0] for b in backs]
    count, share = index.shape[1], backs[0].shape[1]
    return pl.pallas_call(
        functools.partial(unplace_kernel, spans, shifts, capacity),
        out_shape=jax.ShapeDtypeStruct((count, share), BF16),
        in_specs=[VMEM] * (2 + len(backs)),
        out_specs=VMEM,
        compiler_params=pltpu.CompilerParams(vmem_limit_bytes=LIMIT),
        cost_estimate=SMALL,
        name="unplace_rows",
    )(index, slot, *backs)


def weight_grad_kernel(rows, acts, got, up_out, down_out, total, sem):
    copies = Copies(sem)
    half = total.shape[1]
    step = 128
    leave = []
    for i, out in enumerate((up_out, down_out)):
        for n in range(0, half, step):
            mine = dot(rows[i, :, n : n + step], acts[i], 0, 0).astype(BF16).astype(F32)
            total[i, n : n + step, :] = (mine + got[i, n : n + step, :].astype(F32)).astype(BF16)
            leave.append(copies.start(total.at[i, pl.ds(n, step), :], out.at[pl.ds(n, step), :]))
    wait(leave)


def weight_grads(kept_rows, kept_acts, got):
    _, count, width = kept_rows.shape
    hid = kept_acts.shape[2]
    half = width // 2
    return pl.pallas_call(
        weight_grad_kernel,
        out_shape=[jax.ShapeDtypeStruct((half, hid), BF16)] * 2,
        grid=(1,),
        in_specs=[
            pl.BlockSpec((2, count, half), lambda i: (0, 0, 0)),
            pl.BlockSpec((2, count, hid), lambda i: (0, 0, 0)),
            pl.BlockSpec((2, half, hid), lambda i: (0, 0, 0)),
        ],
        out_specs=[ANY] * 2,
        scratch_shapes=[pltpu.VMEM((2, half, hid), BF16), pltpu.SemaphoreType.DMA((2 * (half // 128),))],
        compiler_params=pltpu.CompilerParams(vmem_limit_bytes=40 * 2**20),
        cost_estimate=SMALL,
        name="weight_grads",
    )(kept_rows, kept_acts, got)


def local(tokens, grad_output, gate_prob, expert_index, slot_index, up_weight, down_weight):
    experts = lax.axis_size("expert")
    tensor_size = lax.axis_size("tensor")
    tok_count, width = tokens.shape
    capacity = 2 * tok_count // experts
    share = width // tensor_size

    def swap(x):
        return lax.ppermute(x, "dp", [(0, 1), (1, 0)])

    def across(x, j):
        return lax.ppermute(x, "tensor", [(i, i ^ j) for i in range(tensor_size)])

    def shift(x, k):
        return lax.ppermute(x, "expert", [(i, (i + k) % experts) for i in range(experts)])

    def after(x, *others):
        return lax.optimization_barrier((x,) + others)[0]

    def spread(rows, *before):
        x, y = across(rows, 1), across(rows, 2)
        half_y, half_x = y[:, :share], x[:, share:]
        if before:
            half_y, half_x = after(half_y, *before), after(half_x, *before)
        return [rows, x, y, across(half_y, 1), across(half_x, 2)]

    def collect(blocks):
        got = [across(blocks[j], j) for j in (1, 2, 3)]
        terms = [b.astype(F32) for b in [blocks[0]] + got]
        return (terms[0] + terms[1] + (terms[2] + terms[3])).astype(BF16), got

    def collect_pair(pair, step):
        keep, send = pair
        got = across(send, step)
        last = across((keep[1].astype(F32) + got[1].astype(F32)).astype(BF16), 3 - step)
        return (keep[0].astype(F32) + got[0].astype(F32) + last.astype(F32)).astype(BF16), got

    def other_halves(kept):
        rows, acts = kept
        dims = (((1,), (1,)), ((0,), (0,)))
        return lax.dot_general(rows[:, :, width // 2 :], acts, dims, preferred_element_type=F32).astype(BF16)

    index, slot = expert_index.reshape(1, tok_count), slot_index.reshape(1, tok_count)
    gate = gate_prob.reshape(1, tok_count)
    up_own, down_own = up_weight[0], down_weight[0]
    weights = [up_own, swap(up_own), down_own, swap(down_own)]

    if experts == 4:
        shifts = [1, 3, 2]
        sends = place([capacity] * 3, shifts, capacity, index, slot, gate, tokens, grad_output)
        everything = 4 * capacity
        moved = [shift(rows, k) for rows, k in zip(sends, shifts)]
        own = [index, slot, gate, tokens, grad_output]
        kept, (pair,) = expert_rows(own, None, [(capacity, 1)], weights, everything, 0, None)
        near = spread(jnp.concatenate([after(moved[0], pair[0]), moved[1]], 0))
        far = after(moved[2], *near[1:3])
        far = [far] + [across(far, j) for j in (1, 2, 3)]
        near[0] = after(near[0], far[1])
        back, got_own = collect_pair([pair[0], after(pair[1], *near[3:])], 1)
        kept, (blocks,) = expert_rows(None, [near], [(2 * capacity, None)], weights, everything, capacity, kept)
        total, got = collect(blocks)
        backs = [back, shift(total[:capacity], -1), shift(total[capacity:], -3)]
        far[0] = after(far[0], got_own)
        kept, (blocks,) = expert_rows(None, [far], [(capacity, None)], weights, everything, 3 * capacity, kept)
        others = other_halves(kept)
        grads = weight_grads(*kept, swap(after(others, *got)))
        total, _ = collect([blocks[0]] + [after(b, got[0], others) for b in blocks[1:]])
        backs.append(after(shift(total, -2), *grads))
        shifts = [0] + shifts
    else:
        rows = experts * capacity
        shifts = [None]

        def exchange(x):
            moved = lax.all_to_all(
                x.reshape(experts, capacity, x.shape[1]), "expert", split_axis=0, concat_axis=0, tiled=True
            )
            return moved.reshape(rows, x.shape[1])

        (send,) = place([rows], shifts, capacity, index, slot, gate, tokens, grad_output)
        kept, (blocks,) = expert_rows(None, [spread(exchange(send))], [(rows, None)], weights, rows, 0, None)
        others = other_halves(kept)
        grads = weight_grads(*kept, swap(others))
        total, _ = collect(blocks)
        backs = [exchange(total)]

    return unplace(shifts, capacity, index, slot, backs), grads[0][None], grads[1][None]


def solution(mesh):
    placed = (
        P(("expert", "dp"), None),
        P(("expert", "dp"), None),
        P(("expert", "dp")),
        P(("expert", "dp"), None),
        P(("expert", "dp"), None),
        P("expert", "dp", "tensor"),
        P("expert", "dp", "tensor"),
    )
    return jax.shard_map(
        local,
        mesh=mesh,
        in_specs=placed,
        out_specs=(
            P(("expert", "dp"), "tensor"),
            P("expert", "dp", "tensor"),
            P("expert", "dp", "tensor"),
        ),
        check_vma=False,
    )
```

```python
import functools

import jax
import jax.numpy as jnp
from jax import lax
from jax.experimental import pallas as pl
from jax.experimental.pallas import tpu as pltpu
from jax.sharding import PartitionSpec as P

F32 = jnp.float32
BF16 = jnp.bfloat16
I32 = jnp.int32
ANY = pl.BlockSpec(memory_space=pl.ANY)
VMEM = pl.BlockSpec(memory_space=pltpu.VMEM)
SMEM = pl.BlockSpec(memory_space=pltpu.SMEM)
HBM = pl.BlockSpec(memory_space=pltpu.HBM)
LIMIT = 22 * 2**20
SMALL = pl.CostEstimate(flops=1000, bytes_accessed=1000, transcendentals=0)


def dot(lhs, rhs, left=1, right=0):
    return lax.dot_general(lhs, rhs, (((left,), (right,)), ((), ())), preferred_element_type=F32)


def hits(position, first, rows):
    ids = lax.broadcasted_iota(I32, (rows, position.shape[1]), 0) + first
    return ids == position


def places(index, slot, capacity):
    return index[...] * capacity + slot[...]


def expert_first(k, capacity):
    experts = lax.axis_size("expert")
    return 0 if k is None else lax.rem(lax.axis_index("expert") + k, experts) * capacity


def gate_of(hit, gate):
    return jnp.sum(jnp.where(hit, gate, 0.0), axis=1, keepdims=True)


class Copies:
    def __init__(self, sem):
        self.sem, self.count = sem, 0

    def start(self, src, dst):
        copy = pltpu.make_async_copy(src, dst, self.sem.at[self.count])
        self.count += 1
        copy.start()
        return copy

    def rows(self, src, dst, count, pieces):
        step = count // pieces
        return [self.start(src.at[pl.ds(i * step, step), :], dst.at[pl.ds(i * step, step), :]) for i in range(pieces)]


def wait(copies):
    for copy in copies:
        copy.wait()


def place_kernel(spans, shifts, capacity, index, slot, gate, tokens, grad_output, *refs):
    sends, (index_in, slot_in, gate_in, tok, grad, packed, sem) = refs[: len(spans)], refs[len(spans) :]
    copies = Copies(sem)
    count, share = tok.shape
    columns = pl.ds(pl.multiple_of(lax.axis_index("tensor") * share, share), share)
    small = [copies.start(src, dst) for src, dst in ((index, index_in), (slot, slot_in), (gate, gate_in))]
    arrive = copies.rows(tokens.at[:, columns], tok, count, 4) + copies.rows(grad_output.at[:, columns], grad, count, 4)
    wait(small)
    position = places(index_in, slot_in, capacity)
    found = [hits(position, expert_first(k, capacity), rows) for k, rows in zip(shifts, spans)]
    scales = [gate_of(hit, gate_in[...]) for hit in found]
    hots = [hit.astype(BF16) for hit in found]
    wait(arrive)
    leave = []
    at = 0
    for hot, scale, rows, out in zip(hots, scales, spans, sends):
        packed[at : at + rows, :share] = dot(hot, tok[...]).astype(BF16)
        packed[at : at + rows, share:] = (dot(hot, grad[...]) * scale).astype(BF16)
        leave += copies.rows(packed.at[pl.ds(at, rows), :], out, rows, 2)
        at += rows
    wait(leave)


def place(spans, shifts, capacity, index, slot, gate, tokens, grad_output):
    count, width = tokens.shape
    share = width // 4
    buf = lambda *shape: pltpu.VMEM(shape, BF16)
    return pl.pallas_call(
        functools.partial(place_kernel, spans, shifts, capacity),
        out_shape=[jax.ShapeDtypeStruct((rows, 2 * share), BF16) for rows in spans],
        in_specs=[ANY] * 5,
        out_specs=[ANY] * len(spans),
        scratch_shapes=[
            pltpu.VMEM((1, count), I32), pltpu.VMEM((1, count), I32), pltpu.VMEM((1, count), F32),
            buf(count, share), buf(count, share), buf(sum(spans), 2 * share),
            pltpu.SemaphoreType.DMA((11 + 2 * len(spans),)),
        ],
        compiler_params=pltpu.CompilerParams(vmem_limit_bytes=54 * 2**20),
        cost_estimate=SMALL,
        name="place_rows",
    )(index, slot, gate, tokens, grad_output)


def gelu_parts(pre):
    c = 0.7978845608028654
    square = pre * pre
    th = jnp.tanh(c * (pre + 0.044715 * (pre * square)))
    half = 0.5 * (1.0 + th)
    return pre * half, half + 0.5 * pre * (1.0 - th * th) * (c + (3 * 0.044715 * c) * square)


def expert_kernel(chunks, base, block_base, aliased, *refs):
    refs = list(refs)
    take = lambda n: [refs.pop(0) for _ in range(n)]
    slots = take(5) if chunks is None else [take(n) for n in chunks]
    up_halves, down_halves = take(2), take(2)
    take(aliased)
    kept, mate = take(2)
    blocks = take(4)
    tok, grad, up, down, hidden, slope, back = take(7)
    if chunks is None:
        tok_in, grad_in = take(2)
    copies = Copies(take(1)[0])
    rows, width = tok.shape
    half, share = width // 2, width // 4
    order = lax.axis_index("tensor") ^ (2 * lax.axis_index("dp"))
    arrive = []
    if chunks is None:
        mine = lax.axis_index("dp")
        count = tok_in.shape[0]
        for src, dst in zip(slots[3:], (tok_in, grad_in)):
            for i, start in enumerate((mine * half, (1 - mine) * half)):
                source = src.at[:, pl.ds(pl.multiple_of(start, half), half)]
                arrive += copies.rows(source, dst.at[:, pl.ds(i * half, half)], count, 2)
    else:
        at = 0
        for chunk in slots:
            n = chunk[0].shape[0]
            for j in range(4):
                columns = pl.ds(pl.multiple_of((order ^ j) * share, share), share)
                if j == 3 and len(chunk) == 5:
                    sources = chunk[3:]
                else:
                    sources = [chunk[j].at[:, pl.ds(i * share, share)] for i in range(2)]
                arrive += [copies.start(src, dst.at[pl.ds(at, n), columns]) for src, dst in zip(sources, (tok, grad))]
            at += n
    hid = hidden.shape[1]
    step = 256
    tiles = []
    for n in range(0, hid, step):
        cols = pl.ds(n, step)
        tiles.append([])
        for halves, dst in ((up_halves, up), (down_halves, down)):
            for i in range(2):
                tiles[-1].append(copies.start(halves[i].at[:, cols], dst.at[pl.ds(i * half, half), cols]))
    if chunks is None:
        hit = hits(places(slots[0], slots[1], rows), expert_first(0, rows), rows)
        hot, scale = hit.astype(BF16), gate_of(hit, slots[2][...])
    wait(arrive)
    if chunks is None:
        tok[...] = dot(hot, tok_in[...]).astype(BF16)
        grad[...] = (dot(hot, grad_in[...]) * scale).astype(BF16)
    mine, theirs = pl.ds(base, rows), pl.ds(block_base, rows)
    leave = []
    for i, src in enumerate((tok, grad)):
        leave.append(copies.start(src.at[:, pl.ds(0, half)], kept.at[i, mine, :]))
        leave.append(copies.start(src.at[:, pl.ds(half, half)], mate.at[i, theirs, :]))
    for n, arrived in zip(range(0, hid, step), tiles):
        cols = slice(n, n + step)
        wait(arrived)
        pre = dot(tok[...], up[:, cols])
        hidden_grad = dot(grad[...], down[:, cols])
        act, deriv = gelu_parts(pre)
        hidden[:, cols] = act.astype(BF16)
        slope[:, cols] = (hidden_grad * deriv).astype(BF16)
    for i, src in enumerate((slope, hidden)):
        leave += [copies.start(src, kept.at[2 + i, mine, :]), copies.start(src, mate.at[2 + i, theirs, :])]
    for j in range(4):
        quarter = pl.ds(pl.multiple_of((order ^ j) * share, share), share)
        back[j] = dot(slope[...], up[quarter, :], 1, 1).astype(BF16)
        leave.append(copies.start(back.at[j], blocks[j].at[theirs, :]))
    wait(leave)


def expert_rows(own, chunks, rows, weights, total_rows, base, block_rows, block_base, kept, sent):
    slots = own or sum(chunks, [])
    counts_in = None if own else [len(c) for c in chunks]
    half, hid = weights[0].shape
    width, share = 2 * half, half // 2
    operands = list(slots) + list(weights)
    aliases = {}
    for at, previous in ((0, [] if kept is None else [kept]), (1, sent or [])):
        aliases.update({len(operands) + i: at + i for i in range(len(previous))})
        operands += previous
    shape = lambda *s: jax.ShapeDtypeStruct(s, BF16)
    buf = lambda *s: pltpu.VMEM(s, BF16)
    out = pl.pallas_call(
        functools.partial(expert_kernel, counts_in, base, block_base, len(aliases)),
        out_shape=[shape(4, total_rows, half), shape(4, block_rows, half)] + [shape(block_rows, share)] * 4,
        in_specs=([VMEM] * 3 if own else [ANY] * 3) + [ANY] * (len(operands) - 3),
        out_specs=[ANY] * 6,
        scratch_shapes=[
            buf(rows, width), buf(rows, width), buf(width, hid), buf(width, hid),
            buf(rows, hid), buf(rows, hid), buf(4, rows, share),
        ]
        + ([buf(*own[3].shape)] * 2 if own else [])
        + [pltpu.SemaphoreType.DMA((28 + 4 * (hid // 256),))],
        input_output_aliases=aliases,
        compiler_params=pltpu.CompilerParams(vmem_limit_bytes=LIMIT + rows * 2**15),
        cost_estimate=pl.CostEstimate(
            flops=6 * rows * width * hid, bytes_accessed=4 * width * hid + 8 * rows * width, transcendentals=rows * hid
        ),
        name="expert_rows",
    )(*operands)
    return out[0], list(out[1:])


def unplace_kernel(spans, shifts, capacity, index, slot, *refs):
    out = refs[-1]
    position = places(index, slot, capacity)
    total = None
    for k, rows, back in zip(shifts, spans, refs[:-1]):
        hot = hits(position, expert_first(k, capacity), rows).astype(BF16)
        part = dot(hot, back[...], 0, 0)
        total = part if total is None else total + part
    out[...] = total.astype(BF16)


def unplace(shifts, capacity, index, slot, backs):
    spans = [b.shape[0] for b in backs]
    count, share = index.shape[1], backs[0].shape[1]
    return pl.pallas_call(
        functools.partial(unplace_kernel, spans, shifts, capacity),
        out_shape=jax.ShapeDtypeStruct((count, share), BF16),
        in_specs=[VMEM] * (2 + len(backs)),
        out_specs=VMEM,
        compiler_params=pltpu.CompilerParams(vmem_limit_bytes=LIMIT),
        cost_estimate=SMALL,
        name="unplace_rows",
    )(index, slot, *backs)


def weight_grad_kernel(kept, *refs):
    *mates, up_out, down_out, total, sem = refs
    copies = Copies(sem)
    half = total.shape[1]
    step = 128
    leave = []
    for i, out in enumerate((up_out, down_out)):
        for n in range(0, half, step):
            mine = dot(kept[i, :, n : n + step], kept[2 + i], 0, 0)
            others = sum(dot(mate[i, :, n : n + step], mate[2 + i], 0, 0) for mate in mates)
            both = mine.astype(BF16).astype(F32) + others.astype(BF16).astype(F32)
            total[i, n : n + step, :] = both.astype(BF16)
            leave.append(copies.start(total.at[i, pl.ds(n, step), :], out.at[pl.ds(n, step), :]))
    wait(leave)


def weight_grads(kept, mates):
    _, _, half = kept.shape
    operands = [kept] + mates
    whole = lambda x: pl.BlockSpec(x.shape, lambda i: (0, 0, 0))
    return pl.pallas_call(
        weight_grad_kernel,
        out_shape=[jax.ShapeDtypeStruct((half, half), BF16)] * 2,
        grid=(1,),
        in_specs=[whole(x) for x in operands],
        out_specs=[ANY] * 2,
        scratch_shapes=[pltpu.VMEM((2, half, half), BF16), pltpu.SemaphoreType.DMA((2 * (half // 128),))],
        compiler_params=pltpu.CompilerParams(vmem_limit_bytes=40 * 2**20),
        cost_estimate=SMALL,
        name="weight_grads",
    )(*operands)


def local(tokens, grad_output, gate_prob, expert_index, slot_index, up_weight, down_weight):
    experts = lax.axis_size("expert")
    tensor_size = lax.axis_size("tensor")
    tok_count, width = tokens.shape
    capacity = 2 * tok_count // experts
    share = width // tensor_size

    def swap(x):
        return lax.ppermute(x, "dp", [(0, 1), (1, 0)])

    def across(x, j):
        return lax.ppermute(x, "tensor", [(i, i ^ j) for i in range(tensor_size)])

    def shift(x, k):
        return lax.ppermute(x, "expert", [(i, (i + k) % experts) for i in range(experts)])

    def after(x, *others):
        return lax.optimization_barrier((x,) + others)[0]

    def spread(rows, *before):
        x, y = across(rows, 1), across(rows, 2)
        half_y, half_x = y[:, :share], x[:, share:]
        if before:
            half_y, half_x = after(half_y, *before), after(half_x, *before)
        return [rows, x, y, across(half_y, 1), across(half_x, 2)]

    def collect(blocks):
        got = [across(blocks[j], j) for j in (1, 2, 3)]
        terms = [b.astype(F32) for b in [blocks[0]] + got]
        return (terms[0] + terms[1] + (terms[2] + terms[3])).astype(BF16), got

    index, slot = expert_index.reshape(1, tok_count), slot_index.reshape(1, tok_count)
    gate = gate_prob.reshape(1, tok_count)
    up_own, down_own = up_weight[0], down_weight[0]
    weights = [up_own, swap(up_own), down_own, swap(down_own)]

    if experts == 4:
        shifts = [1, 3, 2]
        sends = place([capacity] * 3, shifts, capacity, index, slot, gate, tokens, grad_output)
        everything = 4 * capacity
        moved = [shift(rows, k) for rows, k in zip(sends, shifts)]
        own = [index, slot, gate, tokens, grad_output]
        most = 3 * capacity
        kept, sent = expert_rows(own, None, capacity, weights, everything, 0, most, 0, None, None)
        near = spread(jnp.concatenate([after(moved[0], sent[1]), moved[1]], 0))
        far = after(moved[2], *near[1:3])
        far = [far] + [across(far, j) for j in (1, 2, 3)]
        near[0] = after(near[0], *far[1:])
        kept, sent = expert_rows(
            None, [near], 2 * capacity, weights, everything, capacity, most, capacity, kept, sent
        )
        total, got = collect(sent[1:])
        backs = [total[:capacity], shift(total[capacity : 2 * capacity], -1), shift(total[2 * capacity :], -3)]
        mates = [swap(sent[0])]
        kept, sent = expert_rows(None, [far], capacity, weights, everything, most, capacity, 0, kept, None)
        mates.append(swap(sent[0]))
        total, _ = collect(sent[1:2] + [after(b, got[0]) for b in sent[2:]])
        grads = weight_grads(kept, mates)
        backs.append(after(shift(total, -2), *grads))
        shifts = [0] + shifts
    else:
        rows = experts * capacity
        shifts = [None]

        def exchange(x):
            moved = lax.all_to_all(
                x.reshape(experts, capacity, x.shape[1]), "expert", split_axis=0, concat_axis=0, tiled=True
            )
            return moved.reshape(rows, x.shape[1])

        (send,) = place([rows], shifts, capacity, index, slot, gate, tokens, grad_output)
        kept, sent = expert_rows(None, [spread(exchange(send))], rows, weights, rows, 0, rows, 0, None, None)
        total, _ = collect(sent[1:])
        grads = weight_grads(kept, [swap(sent[0])])
        backs = [exchange(total)]

    return unplace(shifts, capacity, index, slot, backs), grads[0][None], grads[1][None]


def solution(mesh):
    placed = (
        P(("expert", "dp"), None),
        P(("expert", "dp"), None),
        P(("expert", "dp")),
        P(("expert", "dp"), None),
        P(("expert", "dp"), None),
        P("expert", "dp", "tensor"),
        P("expert", "dp", "tensor"),
    )
    return jax.shard_map(
        local,
        mesh=mesh,
        in_specs=placed,
        out_specs=(
            P(("expert", "dp"), "tensor"),
            P("expert", "dp", "tensor"),
            P("expert", "dp", "tensor"),
        ),
        check_vma=False,
    )
```

```python
import functools

import jax
import jax.numpy as jnp
from jax import lax
from jax.experimental import pallas as pl
from jax.experimental.pallas import tpu as pltpu
from jax.sharding import PartitionSpec as P

F32 = jnp.float32
BF16 = jnp.bfloat16
I32 = jnp.int32
ANY = pl.BlockSpec(memory_space=pl.ANY)
VMEM = pl.BlockSpec(memory_space=pltpu.VMEM)
SMEM = pl.BlockSpec(memory_space=pltpu.SMEM)
HBM = pl.BlockSpec(memory_space=pltpu.HBM)
LIMIT = 22 * 2**20
SMALL = pl.CostEstimate(flops=1000, bytes_accessed=1000, transcendentals=0)


def dot(lhs, rhs, left=1, right=0):
    return lax.dot_general(lhs, rhs, (((left,), (right,)), ((), ())), preferred_element_type=F32)


def hits(position, first, rows):
    ids = lax.broadcasted_iota(I32, (rows, position.shape[1]), 0) + first
    return ids == position


def places(index, slot, capacity):
    return index[...] * capacity + slot[...]


def expert_first(k, capacity):
    experts = lax.axis_size("expert")
    return 0 if k is None else lax.rem(lax.axis_index("expert") + k, experts) * capacity


def gate_of(hit, gate):
    return jnp.sum(jnp.where(hit, gate, 0.0), axis=1, keepdims=True)


class Copies:
    def __init__(self, sem):
        self.sem, self.count = sem, 0

    def start(self, src, dst):
        copy = pltpu.make_async_copy(src, dst, self.sem.at[self.count])
        self.count += 1
        copy.start()
        return copy

    def rows(self, src, dst, count, pieces):
        step = count // pieces
        return [self.start(src.at[pl.ds(i * step, step), :], dst.at[pl.ds(i * step, step), :]) for i in range(pieces)]


def wait(copies):
    for copy in copies:
        copy.wait()


def place_kernel(spans, shifts, capacity, index, slot, gate, tokens, grad_output, *refs):
    sends, (index_in, slot_in, gate_in, tok, grad, packed, sem) = refs[: len(spans)], refs[len(spans) :]
    copies = Copies(sem)
    count, share = tok.shape
    columns = pl.ds(pl.multiple_of(lax.axis_index("tensor") * share, share), share)
    small = [copies.start(src, dst) for src, dst in ((index, index_in), (slot, slot_in), (gate, gate_in))]
    arrive = copies.rows(tokens.at[:, columns], tok, count, 4) + copies.rows(grad_output.at[:, columns], grad, count, 4)
    wait(small)
    position = places(index_in, slot_in, capacity)
    found = [hits(position, expert_first(k, capacity), rows) for k, rows in zip(shifts, spans)]
    scales = [gate_of(hit, gate_in[...]) for hit in found]
    hots = [hit.astype(BF16) for hit in found]
    wait(arrive)
    leave = []
    at = 0
    for hot, scale, rows, out in zip(hots, scales, spans, sends):
        packed[at : at + rows, :share] = dot(hot, tok[...]).astype(BF16)
        packed[at : at + rows, share:] = (dot(hot, grad[...]) * scale).astype(BF16)
        leave += copies.rows(packed.at[pl.ds(at, rows), :], out, rows, 2)
        at += rows
    wait(leave)


def place(spans, shifts, capacity, index, slot, gate, tokens, grad_output):
    count, width = tokens.shape
    share = width // 4
    buf = lambda *shape: pltpu.VMEM(shape, BF16)
    return pl.pallas_call(
        functools.partial(place_kernel, spans, shifts, capacity),
        out_shape=[jax.ShapeDtypeStruct((rows, 2 * share), BF16) for rows in spans],
        in_specs=[ANY] * 5,
        out_specs=[ANY] * len(spans),
        scratch_shapes=[
            pltpu.VMEM((1, count), I32), pltpu.VMEM((1, count), I32), pltpu.VMEM((1, count), F32),
            buf(count, share), buf(count, share), buf(sum(spans), 2 * share),
            pltpu.SemaphoreType.DMA((11 + 2 * len(spans),)),
        ],
        compiler_params=pltpu.CompilerParams(vmem_limit_bytes=54 * 2**20),
        cost_estimate=SMALL,
        name="place_rows",
    )(index, slot, gate, tokens, grad_output)


def gelu_parts(pre):
    c = 0.7978845608028654
    square = pre * pre
    th = jnp.tanh(c * (pre + 0.044715 * (pre * square)))
    half = 0.5 * (1.0 + th)
    return pre * half, half + 0.5 * pre * (1.0 - th * th) * (c + (3 * 0.044715 * c) * square)


def expert_kernel(first, base, groups, aliased, *refs):
    refs = list(refs)
    take = lambda n: [refs.pop(0) for _ in range(n)]
    slots = take(5)
    up_halves, down_halves = take(2), take(2)
    take(aliased)
    kept_rows, kept_acts = take(2)
    targets = [take(4 if step is None else 2) for _, step in groups]
    tok, grad, up, down, hidden, slope, back = take(7)
    if first is None:
        tok_in, grad_in = take(2)
    copies = Copies(take(1)[0])
    rows, width = tok.shape
    half, share = width // 2, width // 4
    order = lax.axis_index("tensor") ^ (2 * lax.axis_index("dp"))
    arrive = []
    if first is None:
        mine = lax.axis_index("dp")
        count = tok_in.shape[0]
        for src, dst in zip(slots[3:], (tok_in, grad_in)):
            for i, start in enumerate((mine * half, (1 - mine) * half)):
                source = src.at[:, pl.ds(pl.multiple_of(start, half), half)]
                arrive += copies.rows(source, dst.at[:, pl.ds(i * half, half)], count, 2)
    else:
        span = pl.ds(first, rows)
        for j in range(4):
            columns = pl.ds(pl.multiple_of((order ^ j) * share, share), share)
            if j < 3:
                sources = [slots[j].at[span, pl.ds(0, share)], slots[j].at[span, pl.ds(share, share)]]
            else:
                sources = [slots[3].at[span, :], slots[4].at[span, :]]
            arrive += [copies.start(src, dst.at[:, columns]) for src, dst in zip(sources, (tok, grad))]
    hid = hidden.shape[1]
    step = 256
    tiles = []
    for n in range(0, hid, step):
        cols = pl.ds(n, step)
        tiles.append([])
        for halves, dst in ((up_halves, up), (down_halves, down)):
            for i in range(2):
                tiles[-1].append(copies.start(halves[i].at[:, cols], dst.at[pl.ds(i * half, half), cols]))
    if first is None:
        hit = hits(places(slots[0], slots[1], rows), expert_first(0, rows), rows)
        hot, scale = hit.astype(BF16), gate_of(hit, slots[2][...])
    wait(arrive)
    if first is None:
        tok[...] = dot(hot, tok_in[...]).astype(BF16)
        grad[...] = (dot(hot, grad_in[...]) * scale).astype(BF16)
    mine = pl.ds(base, rows)
    leave = [copies.start(src, kept_rows.at[i, mine, :]) for i, src in enumerate((tok, grad))]
    for n, arrived in zip(range(0, hid, step), tiles):
        cols = slice(n, n + step)
        wait(arrived)
        pre = dot(tok[...], up[:, cols])
        hidden_grad = dot(grad[...], down[:, cols])
        act, deriv = gelu_parts(pre)
        hidden[:, cols] = act.astype(BF16)
        slope[:, cols] = (hidden_grad * deriv).astype(BF16)
    leave += [copies.start(src, kept_acts.at[i, mine, :]) for i, src in enumerate((slope, hidden))]
    for j in range(4):
        quarter = pl.ds(pl.multiple_of((order ^ j) * share, share), share)
        back[j] = dot(slope[...], up[quarter, :], 1, 1).astype(BF16)
        at = 0
        for (n, step), outs in zip(groups, targets):
            out = outs[j] if step is None else outs[(j & step) // step].at[(j & (3 - step)) // (3 - step)]
            leave.append(copies.start(back.at[j, pl.ds(at, n), :], out))
            at += n
    wait(leave)


def expert_rows(slots, first, groups, weights, total_rows, base, kept):
    rows = sum(n for n, _ in groups)
    half, hid = weights[0].shape
    width, share = 2 * half, half // 2
    operands = list(slots) + list(weights) + list(kept or [])
    aliases = {len(slots) + 4 + i: i for i in range(2)} if kept else {}
    shape = lambda *s: jax.ShapeDtypeStruct(s, BF16)
    buf = lambda *s: pltpu.VMEM(s, BF16)
    quarters = [[shape(n, share)] * 4 if step is None else [shape(2, n, share)] * 2 for n, step in groups]
    counts = [len(q) for q in quarters]
    out = pl.pallas_call(
        functools.partial(expert_kernel, first, base, groups, len(aliases)),
        out_shape=[shape(2, total_rows, width), shape(2, total_rows, hid)] + sum(quarters, []),
        in_specs=([VMEM] * 3 if first is None else [ANY] * 3) + [ANY] * (len(operands) - 3),
        out_specs=[ANY] * (2 + sum(counts)),
        scratch_shapes=[
            buf(rows, width), buf(rows, width), buf(width, hid), buf(width, hid),
            buf(rows, hid), buf(rows, hid), buf(4, rows, share),
        ]
        + ([buf(*slots[3].shape)] * 2 if first is None else [])
        + [pltpu.SemaphoreType.DMA((12 + 4 * (hid // 256) + 4 * len(groups),))],
        input_output_aliases=aliases,
        compiler_params=pltpu.CompilerParams(vmem_limit_bytes=LIMIT + rows * 2**15),
        cost_estimate=pl.CostEstimate(
            flops=6 * rows * width * hid, bytes_accessed=4 * width * hid + 8 * rows * width, transcendentals=rows * hid
        ),
        name="expert_rows",
    )(*operands)
    starts = [2 + sum(counts[:i]) for i in range(len(counts))]
    return list(out[:2]), [list(out[i : i + n]) for i, n in zip(starts, counts)]


def unplace_kernel(spans, shifts, capacity, index, slot, *refs):
    out = refs[-1]
    position = places(index, slot, capacity)
    total = None
    for k, rows, back in zip(shifts, spans, refs[:-1]):
        hot = hits(position, expert_first(k, capacity), rows).astype(BF16)
        part = dot(hot, back[...], 0, 0)
        total = part if total is None else total + part
    out[...] = total.astype(BF16)


def unplace(shifts, capacity, index, slot, backs):
    spans = [b.shape[0] for b in backs]
    count, share = index.shape[1], backs[0].shape[1]
    return pl.pallas_call(
        functools.partial(unplace_kernel, spans, shifts, capacity),
        out_shape=jax.ShapeDtypeStruct((count, share), BF16),
        in_specs=[VMEM] * (2 + len(backs)),
        out_specs=VMEM,
        compiler_params=pltpu.CompilerParams(vmem_limit_bytes=LIMIT),
        cost_estimate=SMALL,
        name="unplace_rows",
    )(index, slot, *backs)


def weight_grad_kernel(rows, acts, got, up_out, down_out, total, sem):
    copies = Copies(sem)
    half = total.shape[1]
    step = 128
    leave = []
    for i, out in enumerate((up_out, down_out)):
        for n in range(0, half, step):
            mine = dot(rows[i, :, n : n + step], acts[i], 0, 0).astype(BF16).astype(F32)
            total[i, n : n + step, :] = (mine + got[i, n : n + step, :].astype(F32)).astype(BF16)
            leave.append(copies.start(total.at[i, pl.ds(n, step), :], out.at[pl.ds(n, step), :]))
    wait(leave)


def weight_grads(kept_rows, kept_acts, got):
    _, count, width = kept_rows.shape
    hid = kept_acts.shape[2]
    half = width // 2
    return pl.pallas_call(
        weight_grad_kernel,
        out_shape=[jax.ShapeDtypeStruct((half, hid), BF16)] * 2,
        grid=(1,),
        in_specs=[
            pl.BlockSpec((2, count, half), lambda i: (0, 0, 0)),
            pl.BlockSpec((2, count, hid), lambda i: (0, 0, 0)),
            pl.BlockSpec((2, half, hid), lambda i: (0, 0, 0)),
        ],
        out_specs=[ANY] * 2,
        scratch_shapes=[pltpu.VMEM((2, half, hid), BF16), pltpu.SemaphoreType.DMA((2 * (half // 128),))],
        compiler_params=pltpu.CompilerParams(vmem_limit_bytes=40 * 2**20),
        cost_estimate=SMALL,
        name="weight_grads",
    )(kept_rows, kept_acts, got)


def local(tokens, grad_output, gate_prob, expert_index, slot_index, up_weight, down_weight):
    experts = lax.axis_size("expert")
    tensor_size = lax.axis_size("tensor")
    tok_count, width = tokens.shape
    capacity = 2 * tok_count // experts
    share = width // tensor_size

    def swap(x):
        return lax.ppermute(x, "dp", [(0, 1), (1, 0)])

    def across(x, j):
        return lax.ppermute(x, "tensor", [(i, i ^ j) for i in range(tensor_size)])

    def shift(x, k):
        return lax.ppermute(x, "expert", [(i, (i + k) % experts) for i in range(experts)])

    def after(x, *others):
        return lax.optimization_barrier((x,) + others)[0]

    def spread(rows, *before):
        x, y = across(rows, 1), across(rows, 2)
        half_y, half_x = y[:, :share], x[:, share:]
        if before:
            half_y, half_x = after(half_y, *before), after(half_x, *before)
        return [rows, x, y, across(half_y, 1), across(half_x, 2)]

    def collect(blocks):
        got = [across(blocks[j], j) for j in (1, 2, 3)]
        terms = [b.astype(F32) for b in [blocks[0]] + got]
        return (terms[0] + terms[1] + (terms[2] + terms[3])).astype(BF16), got

    def collect_pair(pair, step):
        keep, send = pair
        got = across(send, step)
        last = across((keep[1].astype(F32) + got[1].astype(F32)).astype(BF16), 3 - step)
        return (keep[0].astype(F32) + got[0].astype(F32) + last.astype(F32)).astype(BF16), got

    def other_halves(kept):
        rows, acts = kept
        dims = (((1,), (1,)), ((0,), (0,)))
        return lax.dot_general(rows[:, :, width // 2 :], acts, dims, preferred_element_type=F32).astype(BF16)

    index, slot = expert_index.reshape(1, tok_count), slot_index.reshape(1, tok_count)
    gate = gate_prob.reshape(1, tok_count)
    up_own, down_own = up_weight[0], down_weight[0]
    weights = [up_own, swap(up_own), down_own, swap(down_own)]

    if experts == 4:
        shifts = [1, 3, 2]
        sends = place([capacity] * 3, shifts, capacity, index, slot, gate, tokens, grad_output)
        moved = [shift(rows, k) for rows, k in zip(sends, shifts)]
        everything = 4 * capacity
        own = [index, slot, gate, tokens, grad_output]
        kept, (pair,) = expert_rows(own, None, [(capacity, 1)], weights, everything, 0, None)
        near = spread(jnp.concatenate([after(moved[0], pair[0]), moved[1]], 0))
        back, got_own = collect_pair([pair[0], after(pair[1], *near[3:])], 1)
        kept, (blocks,) = expert_rows(near, 0, [(2 * capacity, None)], weights, everything, capacity, kept)
        far = spread(after(moved[2], *near[1:3]), blocks[0])
        total, got = collect(blocks)
        backs = [back, shift(total[:capacity], -1), shift(total[capacity:], -3)]
        slots = [after(far[0], got_own)] + far[1:]
        kept, (blocks,) = expert_rows(slots, 0, [(capacity, None)], weights, everything, 3 * capacity, kept)
        others = other_halves(kept)
        grads = weight_grads(*kept, swap(after(others, *got)))
        total, _ = collect([blocks[0]] + [after(b, got[0], others) for b in blocks[1:]])
        backs.append(after(shift(total, -2), *grads))
        shifts = [0] + shifts
    else:
        rows = experts * capacity
        shifts = [None]

        def exchange(x):
            moved = lax.all_to_all(
                x.reshape(experts, capacity, x.shape[1]), "expert", split_axis=0, concat_axis=0, tiled=True
            )
            return moved.reshape(rows, x.shape[1])

        (send,) = place([rows], shifts, capacity, index, slot, gate, tokens, grad_output)
        kept, (blocks,) = expert_rows(spread(exchange(send)), 0, [(rows, None)], weights, rows, 0, None)
        others = other_halves(kept)
        grads = weight_grads(*kept, swap(others))
        total, _ = collect(blocks)
        backs = [exchange(total)]

    return unplace(shifts, capacity, index, slot, backs), grads[0][None], grads[1][None]


def solution(mesh):
    placed = (
        P(("expert", "dp"), None),
        P(("expert", "dp"), None),
        P(("expert", "dp")),
        P(("expert", "dp"), None),
        P(("expert", "dp"), None),
        P("expert", "dp", "tensor"),
        P("expert", "dp", "tensor"),
    )
    return jax.shard_map(
        local,
        mesh=mesh,
        in_specs=placed,
        out_specs=(
            P(("expert", "dp"), "tensor"),
            P("expert", "dp", "tensor"),
            P("expert", "dp", "tensor"),
        ),
        check_vma=False,
    )
```

```python
import functools

import jax
import jax.numpy as jnp
from jax import lax
from jax.experimental import pallas as pl
from jax.experimental.pallas import tpu as pltpu
from jax.sharding import PartitionSpec as P

F32 = jnp.float32
BF16 = jnp.bfloat16
I32 = jnp.int32
ANY = pl.BlockSpec(memory_space=pl.ANY)
VMEM = pl.BlockSpec(memory_space=pltpu.VMEM)
SMEM = pl.BlockSpec(memory_space=pltpu.SMEM)
HBM = pl.BlockSpec(memory_space=pltpu.HBM)
LIMIT = 22 * 2**20
SMALL = pl.CostEstimate(flops=1000, bytes_accessed=1000, transcendentals=0)


def dot(lhs, rhs, left=1, right=0):
    return lax.dot_general(lhs, rhs, (((left,), (right,)), ((), ())), preferred_element_type=F32)


def hits(position, first, rows):
    ids = lax.broadcasted_iota(I32, (rows, position.shape[1]), 0) + first
    return ids == position


def places(index, slot, capacity):
    return index[...] * capacity + slot[...]


def expert_first(k, capacity):
    experts = lax.axis_size("expert")
    return 0 if k is None else lax.rem(lax.axis_index("expert") + k, experts) * capacity


def gate_of(hit, gate):
    return jnp.sum(jnp.where(hit, gate, 0.0), axis=1, keepdims=True)


class Copies:
    def __init__(self, sem):
        self.sem, self.count = sem, 0

    def start(self, src, dst):
        copy = pltpu.make_async_copy(src, dst, self.sem.at[self.count])
        self.count += 1
        copy.start()
        return copy

    def rows(self, src, dst, count, pieces):
        step = count // pieces
        return [self.start(src.at[pl.ds(i * step, step), :], dst.at[pl.ds(i * step, step), :]) for i in range(pieces)]


def wait(copies):
    for copy in copies:
        copy.wait()


def place_kernel(spans, shifts, capacity, index, slot, gate, tokens, grad_output, *refs):
    sends, (index_in, slot_in, gate_in, tok, grad, packed, sem) = refs[: len(spans)], refs[len(spans) :]
    copies = Copies(sem)
    count, share = tok.shape
    columns = pl.ds(pl.multiple_of(lax.axis_index("tensor") * share, share), share)
    small = [copies.start(src, dst) for src, dst in ((index, index_in), (slot, slot_in), (gate, gate_in))]
    arrive = copies.rows(tokens.at[:, columns], tok, count, 4) + copies.rows(grad_output.at[:, columns], grad, count, 4)
    wait(small)
    position = places(index_in, slot_in, capacity)
    found = [hits(position, expert_first(k, capacity), rows) for k, rows in zip(shifts, spans)]
    scales = [gate_of(hit, gate_in[...]) for hit in found]
    hots = [hit.astype(BF16) for hit in found]
    wait(arrive)
    leave = []
    at = 0
    for hot, scale, rows, out in zip(hots, scales, spans, sends):
        packed[at : at + rows, :share] = dot(hot, tok[...]).astype(BF16)
        packed[at : at + rows, share:] = (dot(hot, grad[...]) * scale).astype(BF16)
        leave += copies.rows(packed.at[pl.ds(at, rows), :], out, rows, 2)
        at += rows
    wait(leave)


def place(spans, shifts, capacity, index, slot, gate, tokens, grad_output):
    count, width = tokens.shape
    share = width // 4
    buf = lambda *shape: pltpu.VMEM(shape, BF16)
    return pl.pallas_call(
        functools.partial(place_kernel, spans, shifts, capacity),
        out_shape=[jax.ShapeDtypeStruct((rows, 2 * share), BF16) for rows in spans],
        in_specs=[ANY] * 5,
        out_specs=[ANY] * len(spans),
        scratch_shapes=[
            pltpu.VMEM((1, count), I32), pltpu.VMEM((1, count), I32), pltpu.VMEM((1, count), F32),
            buf(count, share), buf(count, share), buf(sum(spans), 2 * share),
            pltpu.SemaphoreType.DMA((11 + 2 * len(spans),)),
        ],
        compiler_params=pltpu.CompilerParams(vmem_limit_bytes=54 * 2**20),
        cost_estimate=SMALL,
        name="place_rows",
    )(index, slot, gate, tokens, grad_output)


def gelu_parts(pre):
    c = 0.7978845608028654
    square = pre * pre
    th = jnp.tanh(c * (pre + 0.044715 * (pre * square)))
    half = 0.5 * (1.0 + th)
    return pre * half, half + 0.5 * pre * (1.0 - th * th) * (c + (3 * 0.044715 * c) * square)


def expert_kernel(chunks, base, groups, aliased, *refs):
    refs = list(refs)
    take = lambda n: [refs.pop(0) for _ in range(n)]
    slots = take(5) if chunks is None else [take(n) for n in chunks]
    up_halves, down_halves = take(2), take(2)
    take(aliased)
    kept_rows, kept_acts = take(2)
    targets = [take(4 if step is None else 2) for _, step in groups]
    tok, grad, up, down, hidden, slope, back = take(7)
    if chunks is None:
        tok_in, grad_in = take(2)
    copies = Copies(take(1)[0])
    rows, width = tok.shape
    half, share = width // 2, width // 4
    order = lax.axis_index("tensor") ^ (2 * lax.axis_index("dp"))
    arrive = []
    if chunks is None:
        mine = lax.axis_index("dp")
        count = tok_in.shape[0]
        for src, dst in zip(slots[3:], (tok_in, grad_in)):
            for i, start in enumerate((mine * half, (1 - mine) * half)):
                source = src.at[:, pl.ds(pl.multiple_of(start, half), half)]
                arrive += copies.rows(source, dst.at[:, pl.ds(i * half, half)], count, 2)
    else:
        at = 0
        for chunk in slots:
            n = chunk[0].shape[0]
            for j in range(4):
                columns = pl.ds(pl.multiple_of((order ^ j) * share, share), share)
                if j == 3 and len(chunk) == 5:
                    sources = chunk[3:]
                else:
                    sources = [chunk[j].at[:, pl.ds(i * share, share)] for i in range(2)]
                arrive += [copies.start(src, dst.at[pl.ds(at, n), columns]) for src, dst in zip(sources, (tok, grad))]
            at += n
    hid = hidden.shape[1]
    step = 256
    tiles = []
    for n in range(0, hid, step):
        cols = pl.ds(n, step)
        tiles.append([])
        for halves, dst in ((up_halves, up), (down_halves, down)):
            for i in range(2):
                tiles[-1].append(copies.start(halves[i].at[:, cols], dst.at[pl.ds(i * half, half), cols]))
    if chunks is None:
        hit = hits(places(slots[0], slots[1], rows), expert_first(0, rows), rows)
        hot, scale = hit.astype(BF16), gate_of(hit, slots[2][...])
    wait(arrive)
    if chunks is None:
        tok[...] = dot(hot, tok_in[...]).astype(BF16)
        grad[...] = (dot(hot, grad_in[...]) * scale).astype(BF16)
    mine = pl.ds(base, rows)
    leave = [copies.start(src, kept_rows.at[i, mine, :]) for i, src in enumerate((tok, grad))]
    for n, arrived in zip(range(0, hid, step), tiles):
        cols = slice(n, n + step)
        wait(arrived)
        pre = dot(tok[...], up[:, cols])
        hidden_grad = dot(grad[...], down[:, cols])
        act, deriv = gelu_parts(pre)
        hidden[:, cols] = act.astype(BF16)
        slope[:, cols] = (hidden_grad * deriv).astype(BF16)
    leave += [copies.start(src, kept_acts.at[i, mine, :]) for i, src in enumerate((slope, hidden))]
    for j in range(4):
        quarter = pl.ds(pl.multiple_of((order ^ j) * share, share), share)
        back[j] = dot(slope[...], up[quarter, :], 1, 1).astype(BF16)
        at = 0
        for (n, step), outs in zip(groups, targets):
            out = outs[j] if step is None else outs[(j & step) // step].at[(j & (3 - step)) // (3 - step)]
            leave.append(copies.start(back.at[j, pl.ds(at, n), :], out))
            at += n
    wait(leave)


def expert_rows(own, chunks, groups, weights, total_rows, base, kept):
    slots = own or sum(chunks, [])
    counts_in = None if own else [len(c) for c in chunks]
    rows = sum(n for n, _ in groups)
    half, hid = weights[0].shape
    width, share = 2 * half, half // 2
    operands = list(slots) + list(weights) + list(kept or [])
    aliases = {len(slots) + 4 + i: i for i in range(2)} if kept else {}
    shape = lambda *s: jax.ShapeDtypeStruct(s, BF16)
    buf = lambda *s: pltpu.VMEM(s, BF16)
    quarters = [[shape(n, share)] * 4 if step is None else [shape(2, n, share)] * 2 for n, step in groups]
    counts = [len(q) for q in quarters]
    out = pl.pallas_call(
        functools.partial(expert_kernel, counts_in, base, groups, len(aliases)),
        out_shape=[shape(2, total_rows, width), shape(2, total_rows, hid)] + sum(quarters, []),
        in_specs=([VMEM] * 3 if own else [ANY] * 3) + [ANY] * (len(operands) - 3),
        out_specs=[ANY] * (2 + sum(counts)),
        scratch_shapes=[
            buf(rows, width), buf(rows, width), buf(width, hid), buf(width, hid),
            buf(rows, hid), buf(rows, hid), buf(4, rows, share),
        ]
        + ([buf(*own[3].shape)] * 2 if own else [])
        + [pltpu.SemaphoreType.DMA((16 + 4 * (hid // 256) + 4 * len(groups) + 4,))],
        input_output_aliases=aliases,
        compiler_params=pltpu.CompilerParams(vmem_limit_bytes=LIMIT + rows * 2**15),
        cost_estimate=pl.CostEstimate(
            flops=6 * rows * width * hid, bytes_accessed=4 * width * hid + 8 * rows * width, transcendentals=rows * hid
        ),
        name="expert_rows",
    )(*operands)
    starts = [2 + sum(counts[:i]) for i in range(len(counts))]
    return list(out[:2]), [list(out[i : i + n]) for i, n in zip(starts, counts)]


def unplace_kernel(spans, shifts, capacity, index, slot, *refs):
    out = refs[-1]
    position = places(index, slot, capacity)
    total = None
    for k, rows, back in zip(shifts, spans, refs[:-1]):
        hot = hits(position, expert_first(k, capacity), rows).astype(BF16)
        part = dot(hot, back[...], 0, 0)
        total = part if total is None else total + part
    out[...] = total.astype(BF16)


def unplace(shifts, capacity, index, slot, backs):
    spans = [b.shape[0] for b in backs]
    count, share = index.shape[1], backs[0].shape[1]
    return pl.pallas_call(
        functools.partial(unplace_kernel, spans, shifts, capacity),
        out_shape=jax.ShapeDtypeStruct((count, share), BF16),
        in_specs=[VMEM] * (2 + len(backs)),
        out_specs=VMEM,
        compiler_params=pltpu.CompilerParams(vmem_limit_bytes=LIMIT),
        cost_estimate=SMALL,
        name="unplace_rows",
    )(index, slot, *backs)


def weight_grad_kernel(rows, acts, got, up_out, down_out, total, sem):
    copies = Copies(sem)
    half = total.shape[1]
    step = 128
    leave = []
    for i, out in enumerate((up_out, down_out)):
        for n in range(0, half, step):
            mine = dot(rows[i, :, n : n + step], acts[i], 0, 0).astype(BF16).astype(F32)
            total[i, n : n + step, :] = (mine + got[i, n : n + step, :].astype(F32)).astype(BF16)
            leave.append(copies.start(total.at[i, pl.ds(n, step), :], out.at[pl.ds(n, step), :]))
    wait(leave)


def weight_grads(kept_rows, kept_acts, got):
    _, count, width = kept_rows.shape
    hid = kept_acts.shape[2]
    half = width // 2
    return pl.pallas_call(
        weight_grad_kernel,
        out_shape=[jax.ShapeDtypeStruct((half, hid), BF16)] * 2,
        grid=(1,),
        in_specs=[
            pl.BlockSpec((2, count, half), lambda i: (0, 0, 0)),
            pl.BlockSpec((2, count, hid), lambda i: (0, 0, 0)),
            pl.BlockSpec((2, half, hid), lambda i: (0, 0, 0)),
        ],
        out_specs=[ANY] * 2,
        scratch_shapes=[pltpu.VMEM((2, half, hid), BF16), pltpu.SemaphoreType.DMA((2 * (half // 128),))],
        compiler_params=pltpu.CompilerParams(vmem_limit_bytes=40 * 2**20),
        cost_estimate=SMALL,
        name="weight_grads",
    )(kept_rows, kept_acts, got)


def local(tokens, grad_output, gate_prob, expert_index, slot_index, up_weight, down_weight):
    experts = lax.axis_size("expert")
    tensor_size = lax.axis_size("tensor")
    tok_count, width = tokens.shape
    capacity = 2 * tok_count // experts
    share = width // tensor_size

    def swap(x):
        return lax.ppermute(x, "dp", [(0, 1), (1, 0)])

    def across(x, j):
        return lax.ppermute(x, "tensor", [(i, i ^ j) for i in range(tensor_size)])

    def shift(x, k):
        return lax.ppermute(x, "expert", [(i, (i + k) % experts) for i in range(experts)])

    def after(x, *others):
        return lax.optimization_barrier((x,) + others)[0]

    def spread(rows, *before):
        x, y = across(rows, 1), across(rows, 2)
        half_y, half_x = y[:, :share], x[:, share:]
        if before:
            half_y, half_x = after(half_y, *before), after(half_x, *before)
        return [rows, x, y, across(half_y, 1), across(half_x, 2)]

    def collect(blocks):
        got = [across(blocks[j], j) for j in (1, 2, 3)]
        terms = [b.astype(F32) for b in [blocks[0]] + got]
        return (terms[0] + terms[1] + (terms[2] + terms[3])).astype(BF16), got

    def collect_pair(pair, step):
        keep, send = pair
        got = across(send, step)
        last = across((keep[1].astype(F32) + got[1].astype(F32)).astype(BF16), 3 - step)
        return (keep[0].astype(F32) + got[0].astype(F32) + last.astype(F32)).astype(BF16), got

    def other_halves(kept):
        rows, acts = kept
        dims = (((1,), (1,)), ((0,), (0,)))
        return lax.dot_general(rows[:, :, width // 2 :], acts, dims, preferred_element_type=F32).astype(BF16)

    index, slot = expert_index.reshape(1, tok_count), slot_index.reshape(1, tok_count)
    gate = gate_prob.reshape(1, tok_count)
    up_own, down_own = up_weight[0], down_weight[0]
    weights = [up_own, swap(up_own), down_own, swap(down_own)]

    if experts == 4:
        shifts = [1, 3, 2]
        sends = place([capacity] * 3, shifts, capacity, index, slot, gate, tokens, grad_output)
        everything = 4 * capacity
        moved = [shift(rows, k) for rows, k in zip(sends, shifts)]
        own = [index, slot, gate, tokens, grad_output]
        kept, (pair,) = expert_rows(own, None, [(capacity, 1)], weights, everything, 0, None)
        near = spread(jnp.concatenate([after(moved[0], pair[0]), moved[1]], 0))
        far = after(moved[2], *near[1:3])
        far = [far] + [across(far, j) for j in (1, 2, 3)]
        back, got_own = collect_pair([pair[0], after(pair[1], *near[3:])], 1)
        kept, (blocks,) = expert_rows(None, [near], [(2 * capacity, None)], weights, everything, capacity, kept)
        total, got = collect(blocks)
        backs = [back, shift(total[:capacity], -1), shift(total[capacity:], -3)]
        far[0] = after(far[0], got_own)
        kept, (blocks,) = expert_rows(None, [far], [(capacity, None)], weights, everything, 3 * capacity, kept)
        others = other_halves(kept)
        grads = weight_grads(*kept, swap(after(others, *got)))
        total, _ = collect([blocks[0]] + [after(b, got[0], others) for b in blocks[1:]])
        backs.append(after(shift(total, -2), *grads))
        shifts = [0] + shifts
    else:
        rows = experts * capacity
        shifts = [None]

        def exchange(x):
            moved = lax.all_to_all(
                x.reshape(experts, capacity, x.shape[1]), "expert", split_axis=0, concat_axis=0, tiled=True
            )
            return moved.reshape(rows, x.shape[1])

        (send,) = place([rows], shifts, capacity, index, slot, gate, tokens, grad_output)
        kept, (blocks,) = expert_rows(None, [spread(exchange(send))], [(rows, None)], weights, rows, 0, None)
        others = other_halves(kept)
        grads = weight_grads(*kept, swap(others))
        total, _ = collect(blocks)
        backs = [exchange(total)]

    return unplace(shifts, capacity, index, slot, backs), grads[0][None], grads[1][None]


def solution(mesh):
    placed = (
        P(("expert", "dp"), None),
        P(("expert", "dp"), None),
        P(("expert", "dp")),
        P(("expert", "dp"), None),
        P(("expert", "dp"), None),
        P("expert", "dp", "tensor"),
        P("expert", "dp", "tensor"),
    )
    return jax.shard_map(
        local,
        mesh=mesh,
        in_specs=placed,
        out_specs=(
            P(("expert", "dp"), "tensor"),
            P("expert", "dp", "tensor"),
            P("expert", "dp", "tensor"),
        ),
        check_vma=False,
    )
```

```python
import functools

import jax
import jax.numpy as jnp
from jax import lax
from jax.experimental import pallas as pl
from jax.experimental.pallas import tpu as pltpu
from jax.sharding import PartitionSpec as P

F32 = jnp.float32
BF16 = jnp.bfloat16
I32 = jnp.int32
ANY = pl.BlockSpec(memory_space=pl.ANY)
VMEM = pl.BlockSpec(memory_space=pltpu.VMEM)
SMEM = pl.BlockSpec(memory_space=pltpu.SMEM)
HBM = pl.BlockSpec(memory_space=pltpu.HBM)
LIMIT = 22 * 2**20
SMALL = pl.CostEstimate(flops=1000, bytes_accessed=1000, transcendentals=0)


def dot(lhs, rhs, left=1, right=0):
    return lax.dot_general(lhs, rhs, (((left,), (right,)), ((), ())), preferred_element_type=F32)


def hits(position, first, rows):
    ids = lax.broadcasted_iota(I32, (rows, position.shape[1]), 0) + first
    return ids == position


def places(index, slot, capacity):
    return index[...] * capacity + slot[...]


def expert_first(k, capacity):
    experts = lax.axis_size("expert")
    return 0 if k is None else lax.rem(lax.axis_index("expert") + k, experts) * capacity


def gate_of(hit, gate):
    return jnp.sum(jnp.where(hit, gate, 0.0), axis=1, keepdims=True)


class Copies:
    def __init__(self, sem):
        self.sem, self.count = sem, 0

    def start(self, src, dst):
        copy = pltpu.make_async_copy(src, dst, self.sem.at[self.count])
        self.count += 1
        copy.start()
        return copy

    def rows(self, src, dst, count, pieces):
        step = count // pieces
        return [self.start(src.at[pl.ds(i * step, step), :], dst.at[pl.ds(i * step, step), :]) for i in range(pieces)]


def wait(copies):
    for copy in copies:
        copy.wait()


def place_kernel(spans, shifts, capacity, index, slot, gate, tokens, grad_output, *refs):
    sends, (index_in, slot_in, gate_in, tok, grad, packed, sem) = refs[: len(spans)], refs[len(spans) :]
    copies = Copies(sem)
    count, share = tok.shape
    columns = pl.ds(pl.multiple_of(lax.axis_index("tensor") * share, share), share)
    small = [copies.start(src, dst) for src, dst in ((index, index_in), (slot, slot_in), (gate, gate_in))]
    arrive = copies.rows(tokens.at[:, columns], tok, count, 4) + copies.rows(grad_output.at[:, columns], grad, count, 4)
    wait(small)
    position = places(index_in, slot_in, capacity)
    found = [hits(position, expert_first(k, capacity), rows) for k, rows in zip(shifts, spans)]
    scales = [gate_of(hit, gate_in[...]) for hit in found]
    hots = [hit.astype(BF16) for hit in found]
    wait(arrive)
    leave = []
    at = 0
    for hot, scale, rows, out in zip(hots, scales, spans, sends):
        packed[at : at + rows, :share] = dot(hot, tok[...]).astype(BF16)
        packed[at : at + rows, share:] = (dot(hot, grad[...]) * scale).astype(BF16)
        leave += copies.rows(packed.at[pl.ds(at, rows), :], out, rows, 2)
        at += rows
    wait(leave)


def place(spans, shifts, capacity, index, slot, gate, tokens, grad_output):
    count, width = tokens.shape
    share = width // 4
    buf = lambda *shape: pltpu.VMEM(shape, BF16)
    return pl.pallas_call(
        functools.partial(place_kernel, spans, shifts, capacity),
        out_shape=[jax.ShapeDtypeStruct((rows, 2 * share), BF16) for rows in spans],
        in_specs=[ANY] * 5,
        out_specs=[ANY] * len(spans),
        scratch_shapes=[
            pltpu.VMEM((1, count), I32), pltpu.VMEM((1, count), I32), pltpu.VMEM((1, count), F32),
            buf(count, share), buf(count, share), buf(sum(spans), 2 * share),
            pltpu.SemaphoreType.DMA((11 + 2 * len(spans),)),
        ],
        compiler_params=pltpu.CompilerParams(vmem_limit_bytes=54 * 2**20),
        cost_estimate=SMALL,
        name="place_rows",
    )(index, slot, gate, tokens, grad_output)


def gelu_parts(pre):
    c = 0.7978845608028654
    square = pre * pre
    th = jnp.tanh(c * (pre + 0.044715 * (pre * square)))
    half = 0.5 * (1.0 + th)
    return pre * half, half + 0.5 * pre * (1.0 - th * th) * (c + (3 * 0.044715 * c) * square)


def expert_kernel(chunks, base, groups, aliased, *refs):
    refs = list(refs)
    take = lambda n: [refs.pop(0) for _ in range(n)]
    slots = take(5) if chunks is None else [take(n) for n in chunks]
    up_halves, down_halves = take(2), take(2)
    take(aliased)
    kept_rows, kept_acts = take(2)
    targets = [take(4 if step is None else 2) for _, step in groups]
    tok, grad, up, down, hidden, slope, back = take(7)
    if chunks is None:
        tok_in, grad_in = take(2)
    copies = Copies(take(1)[0])
    rows, width = tok.shape
    half, share = width // 2, width // 4
    order = lax.axis_index("tensor") ^ (2 * lax.axis_index("dp"))
    arrive = []
    if chunks is None:
        mine = lax.axis_index("dp")
        count = tok_in.shape[0]
        for src, dst in zip(slots[3:], (tok_in, grad_in)):
            for i, start in enumerate((mine * half, (1 - mine) * half)):
                source = src.at[:, pl.ds(pl.multiple_of(start, half), half)]
                arrive += copies.rows(source, dst.at[:, pl.ds(i * half, half)], count, 2)
    else:
        at = 0
        for chunk in slots:
            n = chunk[0].shape[0]
            for j in range(4):
                columns = pl.ds(pl.multiple_of((order ^ j) * share, share), share)
                if j == 3 and len(chunk) == 5:
                    sources = chunk[3:]
                else:
                    sources = [chunk[j].at[:, pl.ds(i * share, share)] for i in range(2)]
                arrive += [copies.start(src, dst.at[pl.ds(at, n), columns]) for src, dst in zip(sources, (tok, grad))]
            at += n
    hid = hidden.shape[1]
    step = 256
    tiles = []
    for n in range(0, hid, step):
        cols = pl.ds(n, step)
        tiles.append([])
        for halves, dst in ((up_halves, up), (down_halves, down)):
            for i in range(2):
                tiles[-1].append(copies.start(halves[i].at[:, cols], dst.at[pl.ds(i * half, half), cols]))
    if chunks is None:
        hit = hits(places(slots[0], slots[1], rows), expert_first(0, rows), rows)
        hot, scale = hit.astype(BF16), gate_of(hit, slots[2][...])
    wait(arrive)
    if chunks is None:
        tok[...] = dot(hot, tok_in[...]).astype(BF16)
        grad[...] = (dot(hot, grad_in[...]) * scale).astype(BF16)
    mine = pl.ds(base, rows)
    leave = [copies.start(src, kept_rows.at[i, mine, :]) for i, src in enumerate((tok, grad))]
    for n, arrived in zip(range(0, hid, step), tiles):
        cols = slice(n, n + step)
        wait(arrived)
        pre = dot(tok[...], up[:, cols])
        hidden_grad = dot(grad[...], down[:, cols])
        act, deriv = gelu_parts(pre)
        hidden[:, cols] = act.astype(BF16)
        slope[:, cols] = (hidden_grad * deriv).astype(BF16)
    leave += [copies.start(src, kept_acts.at[i, mine, :]) for i, src in enumerate((slope, hidden))]
    for j in range(4):
        quarter = pl.ds(pl.multiple_of((order ^ j) * share, share), share)
        back[j] = dot(slope[...], up[quarter, :], 1, 1).astype(BF16)
        at = 0
        for (n, step), outs in zip(groups, targets):
            out = outs[j] if step is None else outs[(j & step) // step].at[(j & (3 - step)) // (3 - step)]
            leave.append(copies.start(back.at[j, pl.ds(at, n), :], out))
            at += n
    wait(leave)


def expert_rows(own, chunks, groups, weights, total_rows, base, kept):
    slots = own or sum(chunks, [])
    counts_in = None if own else [len(c) for c in chunks]
    rows = sum(n for n, _ in groups)
    half, hid = weights[0].shape
    width, share = 2 * half, half // 2
    operands = list(slots) + list(weights) + list(kept or [])
    aliases = {len(slots) + 4 + i: i for i in range(2)} if kept else {}
    shape = lambda *s: jax.ShapeDtypeStruct(s, BF16)
    buf = lambda *s: pltpu.VMEM(s, BF16)
    quarters = [[shape(n, share)] * 4 if step is None else [shape(2, n, share)] * 2 for n, step in groups]
    counts = [len(q) for q in quarters]
    out = pl.pallas_call(
        functools.partial(expert_kernel, counts_in, base, groups, len(aliases)),
        out_shape=[shape(2, total_rows, width), shape(2, total_rows, hid)] + sum(quarters, []),
        in_specs=([VMEM] * 3 if own else [ANY] * 3) + [ANY] * (len(operands) - 3),
        out_specs=[ANY] * (2 + sum(counts)),
        scratch_shapes=[
            buf(rows, width), buf(rows, width), buf(width, hid), buf(width, hid),
            buf(rows, hid), buf(rows, hid), buf(4, rows, share),
        ]
        + ([buf(*own[3].shape)] * 2 if own else [])
        + [pltpu.SemaphoreType.DMA((16 + 4 * (hid // 256) + 4 * len(groups) + 4,))],
        input_output_aliases=aliases,
        compiler_params=pltpu.CompilerParams(vmem_limit_bytes=LIMIT + rows * 2**15),
        cost_estimate=pl.CostEstimate(
            flops=6 * rows * width * hid, bytes_accessed=4 * width * hid + 8 * rows * width, transcendentals=rows * hid
        ),
        name="expert_rows",
    )(*operands)
    starts = [2 + sum(counts[:i]) for i in range(len(counts))]
    return list(out[:2]), [list(out[i : i + n]) for i, n in zip(starts, counts)]


def unplace_kernel(spans, shifts, capacity, index, slot, *refs):
    out = refs[-1]
    position = places(index, slot, capacity)
    total = None
    for k, rows, back in zip(shifts, spans, refs[:-1]):
        hot = hits(position, expert_first(k, capacity), rows).astype(BF16)
        part = dot(hot, back[...], 0, 0)
        total = part if total is None else total + part
    out[...] = total.astype(BF16)


def unplace(shifts, capacity, index, slot, backs):
    spans = [b.shape[0] for b in backs]
    count, share = index.shape[1], backs[0].shape[1]
    return pl.pallas_call(
        functools.partial(unplace_kernel, spans, shifts, capacity),
        out_shape=jax.ShapeDtypeStruct((count, share), BF16),
        in_specs=[VMEM] * (2 + len(backs)),
        out_specs=VMEM,
        compiler_params=pltpu.CompilerParams(vmem_limit_bytes=LIMIT),
        cost_estimate=SMALL,
        name="unplace_rows",
    )(index, slot, *backs)


def weight_grad_kernel(rows, acts, got, up_out, down_out, total, sem):
    copies = Copies(sem)
    half = total.shape[1]
    step = 128
    leave = []
    for i, out in enumerate((up_out, down_out)):
        for n in range(0, half, step):
            mine = dot(rows[i, :, n : n + step], acts[i], 0, 0).astype(BF16).astype(F32)
            total[i, n : n + step, :] = (mine + got[i, n : n + step, :].astype(F32)).astype(BF16)
            leave.append(copies.start(total.at[i, pl.ds(n, step), :], out.at[pl.ds(n, step), :]))
    wait(leave)


def weight_grads(kept_rows, kept_acts, got):
    _, count, width = kept_rows.shape
    hid = kept_acts.shape[2]
    half = width // 2
    return pl.pallas_call(
        weight_grad_kernel,
        out_shape=[jax.ShapeDtypeStruct((half, hid), BF16)] * 2,
        grid=(1,),
        in_specs=[
            pl.BlockSpec((2, count, half), lambda i: (0, 0, 0)),
            pl.BlockSpec((2, count, hid), lambda i: (0, 0, 0)),
            pl.BlockSpec((2, half, hid), lambda i: (0, 0, 0)),
        ],
        out_specs=[ANY] * 2,
        scratch_shapes=[pltpu.VMEM((2, half, hid), BF16), pltpu.SemaphoreType.DMA((2 * (half // 128),))],
        compiler_params=pltpu.CompilerParams(vmem_limit_bytes=40 * 2**20),
        cost_estimate=SMALL,
        name="weight_grads",
    )(kept_rows, kept_acts, got)


def local(tokens, grad_output, gate_prob, expert_index, slot_index, up_weight, down_weight):
    experts = lax.axis_size("expert")
    tensor_size = lax.axis_size("tensor")
    tok_count, width = tokens.shape
    capacity = 2 * tok_count // experts
    share = width // tensor_size

    def swap(x):
        return lax.ppermute(x, "dp", [(0, 1), (1, 0)])

    def across(x, j):
        return lax.ppermute(x, "tensor", [(i, i ^ j) for i in range(tensor_size)])

    def shift(x, k):
        return lax.ppermute(x, "expert", [(i, (i + k) % experts) for i in range(experts)])

    def after(x, *others):
        return lax.optimization_barrier((x,) + others)[0]

    def spread(rows, *before):
        x, y = across(rows, 1), across(rows, 2)
        half_y, half_x = y[:, :share], x[:, share:]
        if before:
            half_y, half_x = after(half_y, *before), after(half_x, *before)
        return [rows, x, y, across(half_y, 1), across(half_x, 2)]

    def collect(blocks):
        got = [across(blocks[j], j) for j in (1, 2, 3)]
        terms = [b.astype(F32) for b in [blocks[0]] + got]
        return (terms[0] + terms[1] + (terms[2] + terms[3])).astype(BF16), got

    def collect_pair(pair, step):
        keep, send = pair
        got = across(send, step)
        last = across((keep[1].astype(F32) + got[1].astype(F32)).astype(BF16), 3 - step)
        return (keep[0].astype(F32) + got[0].astype(F32) + last.astype(F32)).astype(BF16), got

    def other_halves(kept):
        rows, acts = kept
        dims = (((1,), (1,)), ((0,), (0,)))
        return lax.dot_general(rows[:, :, width // 2 :], acts, dims, preferred_element_type=F32).astype(BF16)

    index, slot = expert_index.reshape(1, tok_count), slot_index.reshape(1, tok_count)
    gate = gate_prob.reshape(1, tok_count)
    up_own, down_own = up_weight[0], down_weight[0]
    weights = [up_own, swap(up_own), down_own, swap(down_own)]

    if experts == 4:
        shifts = [1, 3, 2]
        sends = place([capacity] * 3, shifts, capacity, index, slot, gate, tokens, grad_output)
        everything = 4 * capacity
        moved = [shift(rows, k) for rows, k in zip(sends, shifts)]
        own = [index, slot, gate, tokens, grad_output]
        kept, (pair,) = expert_rows(own, None, [(capacity, 1)], weights, everything, 0, None)
        near = spread(jnp.concatenate([after(moved[0], pair[0]), moved[1]], 0))
        far = after(moved[2], *near[1:3])
        far = [far] + [across(far, j) for j in (1, 2, 3)]
        kept, (blocks,) = expert_rows(None, [near], [(2 * capacity, None)], weights, everything, capacity, kept)
        total, got = collect(blocks)
        backs = [shift(total[:capacity], -1), shift(total[capacity:], -3)]
        kept, (blocks,) = expert_rows(None, [far], [(capacity, None)], weights, everything, 3 * capacity, kept)
        others = other_halves(kept)
        grads = weight_grads(*kept, swap(after(others, *got)))
        total, last = collect([blocks[0]] + [after(b, got[0], others) for b in blocks[1:]])
        back, _ = collect_pair([pair[0], after(pair[1], others)], 1)
        backs = [back] + backs + [after(shift(total, -2), *grads)]
        shifts = [0] + shifts
    else:
        rows = experts * capacity
        shifts = [None]

        def exchange(x):
            moved = lax.all_to_all(
                x.reshape(experts, capacity, x.shape[1]), "expert", split_axis=0, concat_axis=0, tiled=True
            )
            return moved.reshape(rows, x.shape[1])

        (send,) = place([rows], shifts, capacity, index, slot, gate, tokens, grad_output)
        kept, (blocks,) = expert_rows(None, [spread(exchange(send))], [(rows, None)], weights, rows, 0, None)
        others = other_halves(kept)
        grads = weight_grads(*kept, swap(others))
        total, _ = collect(blocks)
        backs = [exchange(total)]

    return unplace(shifts, capacity, index, slot, backs), grads[0][None], grads[1][None]


def solution(mesh):
    placed = (
        P(("expert", "dp"), None),
        P(("expert", "dp"), None),
        P(("expert", "dp")),
        P(("expert", "dp"), None),
        P(("expert", "dp"), None),
        P("expert", "dp", "tensor"),
        P("expert", "dp", "tensor"),
    )
    return jax.shard_map(
        local,
        mesh=mesh,
        in_specs=placed,
        out_specs=(
            P(("expert", "dp"), "tensor"),
            P("expert", "dp", "tensor"),
            P("expert", "dp", "tensor"),
        ),
        check_vma=False,
    )
```

```python
import functools

import jax
import jax.numpy as jnp
from jax import lax
from jax.experimental import pallas as pl
from jax.experimental.pallas import tpu as pltpu
from jax.sharding import PartitionSpec as P

F32 = jnp.float32
BF16 = jnp.bfloat16
I32 = jnp.int32
ANY = pl.BlockSpec(memory_space=pl.ANY)
VMEM = pl.BlockSpec(memory_space=pltpu.VMEM)
SMEM = pl.BlockSpec(memory_space=pltpu.SMEM)
HBM = pl.BlockSpec(memory_space=pltpu.HBM)
LIMIT = 22 * 2**20
SMALL = pl.CostEstimate(flops=1000, bytes_accessed=1000, transcendentals=0)


def dot(lhs, rhs, left=1, right=0):
    return lax.dot_general(lhs, rhs, (((left,), (right,)), ((), ())), preferred_element_type=F32)


def hits(position, first, rows):
    ids = lax.broadcasted_iota(I32, (rows, position.shape[1]), 0) + first
    return ids == position


def places(index, slot, capacity):
    return index[...] * capacity + slot[...]


def expert_first(k, capacity):
    experts = lax.axis_size("expert")
    return 0 if k is None else lax.rem(lax.axis_index("expert") + k, experts) * capacity


def gate_of(hit, gate):
    return jnp.sum(jnp.where(hit, gate, 0.0), axis=1, keepdims=True)


class Copies:
    def __init__(self, sem):
        self.sem, self.count = sem, 0

    def start(self, src, dst):
        copy = pltpu.make_async_copy(src, dst, self.sem.at[self.count])
        self.count += 1
        copy.start()
        return copy

    def rows(self, src, dst, count, pieces):
        step = count // pieces
        return [self.start(src.at[pl.ds(i * step, step), :], dst.at[pl.ds(i * step, step), :]) for i in range(pieces)]


def wait(copies):
    for copy in copies:
        copy.wait()


def place_kernel(spans, shifts, capacity, index, slot, gate, tokens, grad_output, *refs):
    sends, (index_in, slot_in, gate_in, tok, grad, packed, sem) = refs[: len(spans)], refs[len(spans) :]
    copies = Copies(sem)
    count, share = tok.shape
    columns = pl.ds(pl.multiple_of(lax.axis_index("tensor") * share, share), share)
    small = [copies.start(src, dst) for src, dst in ((index, index_in), (slot, slot_in), (gate, gate_in))]
    arrive = copies.rows(tokens.at[:, columns], tok, count, 4) + copies.rows(grad_output.at[:, columns], grad, count, 4)
    wait(small)
    position = places(index_in, slot_in, capacity)
    found = [hits(position, expert_first(k, capacity), rows) for k, rows in zip(shifts, spans)]
    scales = [gate_of(hit, gate_in[...]) for hit in found]
    hots = [hit.astype(BF16) for hit in found]
    wait(arrive)
    leave = []
    at = 0
    for hot, scale, rows, out in zip(hots, scales, spans, sends):
        packed[at : at + rows, :share] = dot(hot, tok[...]).astype(BF16)
        packed[at : at + rows, share:] = (dot(hot, grad[...]) * scale).astype(BF16)
        leave += copies.rows(packed.at[pl.ds(at, rows), :], out, rows, 2)
        at += rows
    wait(leave)


def place(spans, shifts, capacity, index, slot, gate, tokens, grad_output):
    count, width = tokens.shape
    share = width // 4
    buf = lambda *shape: pltpu.VMEM(shape, BF16)
    return pl.pallas_call(
        functools.partial(place_kernel, spans, shifts, capacity),
        out_shape=[jax.ShapeDtypeStruct((rows, 2 * share), BF16) for rows in spans],
        in_specs=[ANY] * 5,
        out_specs=[ANY] * len(spans),
        scratch_shapes=[
            pltpu.VMEM((1, count), I32), pltpu.VMEM((1, count), I32), pltpu.VMEM((1, count), F32),
            buf(count, share), buf(count, share), buf(sum(spans), 2 * share),
            pltpu.SemaphoreType.DMA((11 + 2 * len(spans),)),
        ],
        compiler_params=pltpu.CompilerParams(vmem_limit_bytes=54 * 2**20),
        cost_estimate=SMALL,
        name="place_rows",
    )(index, slot, gate, tokens, grad_output)


def gelu_parts(pre):
    c = 0.7978845608028654
    square = pre * pre
    th = jnp.tanh(c * (pre + 0.044715 * (pre * square)))
    half = 0.5 * (1.0 + th)
    return pre * half, half + 0.5 * pre * (1.0 - th * th) * (c + (3 * 0.044715 * c) * square)


def expert_kernel(chunks, base, groups, aliased, *refs):
    refs = list(refs)
    take = lambda n: [refs.pop(0) for _ in range(n)]
    slots = take(5) if chunks is None else [take(n) for n in chunks]
    up_halves, down_halves = take(2), take(2)
    take(aliased)
    kept_rows, kept_acts = take(2)
    targets = [take(4 if step is None else 2) for _, step in groups]
    tok, grad, up, down, hidden, slope, back = take(7)
    if chunks is None:
        tok_in, grad_in = take(2)
    copies = Copies(take(1)[0])
    rows, width = tok.shape
    half, share = width // 2, width // 4
    order = lax.axis_index("tensor") ^ (2 * lax.axis_index("dp"))
    arrive = []
    if chunks is None:
        mine = lax.axis_index("dp")
        count = tok_in.shape[0]
        for src, dst in zip(slots[3:], (tok_in, grad_in)):
            for i, start in enumerate((mine * half, (1 - mine) * half)):
                source = src.at[:, pl.ds(pl.multiple_of(start, half), half)]
                arrive += copies.rows(source, dst.at[:, pl.ds(i * half, half)], count, 2)
    else:
        at = 0
        for chunk in slots:
            n = chunk[0].shape[0]
            for j in range(4):
                columns = pl.ds(pl.multiple_of((order ^ j) * share, share), share)
                if j == 3 and len(chunk) == 5:
                    sources = chunk[3:]
                else:
                    sources = [chunk[j].at[:, pl.ds(i * share, share)] for i in range(2)]
                arrive += [copies.start(src, dst.at[pl.ds(at, n), columns]) for src, dst in zip(sources, (tok, grad))]
            at += n
    hid = hidden.shape[1]
    step = 256
    tiles = []
    for n in range(0, hid, step):
        cols = pl.ds(n, step)
        tiles.append([])
        for halves, dst in ((up_halves, up), (down_halves, down)):
            for i in range(2):
                tiles[-1].append(copies.start(halves[i].at[:, cols], dst.at[pl.ds(i * half, half), cols]))
    if chunks is None:
        hit = hits(places(slots[0], slots[1], rows), expert_first(0, rows), rows)
        hot, scale = hit.astype(BF16), gate_of(hit, slots[2][...])
    wait(arrive)
    if chunks is None:
        tok[...] = dot(hot, tok_in[...]).astype(BF16)
        grad[...] = (dot(hot, grad_in[...]) * scale).astype(BF16)
    mine = pl.ds(base, rows)
    leave = [copies.start(src, kept_rows.at[i, mine, :]) for i, src in enumerate((tok, grad))]
    for n, arrived in zip(range(0, hid, step), tiles):
        cols = slice(n, n + step)
        wait(arrived)
        pre = dot(tok[...], up[:, cols])
        hidden_grad = dot(grad[...], down[:, cols])
        act, deriv = gelu_parts(pre)
        hidden[:, cols] = act.astype(BF16)
        slope[:, cols] = (hidden_grad * deriv).astype(BF16)
    leave += [copies.start(src, kept_acts.at[i, mine, :]) for i, src in enumerate((slope, hidden))]
    for j in range(4):
        quarter = pl.ds(pl.multiple_of((order ^ j) * share, share), share)
        back[j] = dot(slope[...], up[quarter, :], 1, 1).astype(BF16)
        at = 0
        for (n, step), outs in zip(groups, targets):
            out = outs[j] if step is None else outs[(j & step) // step].at[(j & (3 - step)) // (3 - step)]
            leave.append(copies.start(back.at[j, pl.ds(at, n), :], out))
            at += n
    wait(leave)


def expert_rows(own, chunks, groups, weights, total_rows, base, kept):
    slots = own or sum(chunks, [])
    counts_in = None if own else [len(c) for c in chunks]
    rows = sum(n for n, _ in groups)
    half, hid = weights[0].shape
    width, share = 2 * half, half // 2
    operands = list(slots) + list(weights) + list(kept or [])
    aliases = {len(slots) + 4 + i: i for i in range(2)} if kept else {}
    shape = lambda *s: jax.ShapeDtypeStruct(s, BF16)
    buf = lambda *s: pltpu.VMEM(s, BF16)
    quarters = [[shape(n, share)] * 4 if step is None else [shape(2, n, share)] * 2 for n, step in groups]
    counts = [len(q) for q in quarters]
    out = pl.pallas_call(
        functools.partial(expert_kernel, counts_in, base, groups, len(aliases)),
        out_shape=[shape(2, total_rows, width), shape(2, total_rows, hid)] + sum(quarters, []),
        in_specs=([VMEM] * 3 if own else [ANY] * 3) + [ANY] * (len(operands) - 3),
        out_specs=[ANY] * (2 + sum(counts)),
        scratch_shapes=[
            buf(rows, width), buf(rows, width), buf(width, hid), buf(width, hid),
            buf(rows, hid), buf(rows, hid), buf(4, rows, share),
        ]
        + ([buf(*own[3].shape)] * 2 if own else [])
        + [pltpu.SemaphoreType.DMA((16 + 4 * (hid // 256) + 4 * len(groups) + 4,))],
        input_output_aliases=aliases,
        compiler_params=pltpu.CompilerParams(vmem_limit_bytes=LIMIT + rows * 2**15),
        cost_estimate=pl.CostEstimate(
            flops=6 * rows * width * hid, bytes_accessed=4 * width * hid + 8 * rows * width, transcendentals=rows * hid
        ),
        name="expert_rows",
    )(*operands)
    starts = [2 + sum(counts[:i]) for i in range(len(counts))]
    return list(out[:2]), [list(out[i : i + n]) for i, n in zip(starts, counts)]


def unplace_kernel(spans, shifts, capacity, index, slot, *refs):
    out = refs[-1]
    position = places(index, slot, capacity)
    total = None
    for k, rows, back in zip(shifts, spans, refs[:-1]):
        hot = hits(position, expert_first(k, capacity), rows).astype(BF16)
        part = dot(hot, back[...], 0, 0)
        total = part if total is None else total + part
    out[...] = total.astype(BF16)


def unplace(shifts, capacity, index, slot, backs):
    spans = [b.shape[0] for b in backs]
    count, share = index.shape[1], backs[0].shape[1]
    return pl.pallas_call(
        functools.partial(unplace_kernel, spans, shifts, capacity),
        out_shape=jax.ShapeDtypeStruct((count, share), BF16),
        in_specs=[VMEM] * (2 + len(backs)),
        out_specs=VMEM,
        compiler_params=pltpu.CompilerParams(vmem_limit_bytes=LIMIT),
        cost_estimate=SMALL,
        name="unplace_rows",
    )(index, slot, *backs)


def weight_grad_kernel(rows, acts, got, up_out, down_out, total, sem):
    copies = Copies(sem)
    half = total.shape[1]
    step = 128
    leave = []
    for i, out in enumerate((up_out, down_out)):
        for n in range(0, half, step):
            mine = dot(rows[i, :, n : n + step], acts[i], 0, 0).astype(BF16).astype(F32)
            total[i, n : n + step, :] = (mine + got[i, n : n + step, :].astype(F32)).astype(BF16)
            leave.append(copies.start(total.at[i, pl.ds(n, step), :], out.at[pl.ds(n, step), :]))
    wait(leave)


def weight_grads(kept_rows, kept_acts, got):
    _, count, width = kept_rows.shape
    hid = kept_acts.shape[2]
    half = width // 2
    return pl.pallas_call(
        weight_grad_kernel,
        out_shape=[jax.ShapeDtypeStruct((half, hid), BF16)] * 2,
        grid=(1,),
        in_specs=[
            pl.BlockSpec((2, count, half), lambda i: (0, 0, 0)),
            pl.BlockSpec((2, count, hid), lambda i: (0, 0, 0)),
            pl.BlockSpec((2, half, hid), lambda i: (0, 0, 0)),
        ],
        out_specs=[ANY] * 2,
        scratch_shapes=[pltpu.VMEM((2, half, hid), BF16), pltpu.SemaphoreType.DMA((2 * (half // 128),))],
        compiler_params=pltpu.CompilerParams(vmem_limit_bytes=40 * 2**20),
        cost_estimate=SMALL,
        name="weight_grads",
    )(kept_rows, kept_acts, got)


def local(tokens, grad_output, gate_prob, expert_index, slot_index, up_weight, down_weight):
    experts = lax.axis_size("expert")
    tensor_size = lax.axis_size("tensor")
    tok_count, width = tokens.shape
    capacity = 2 * tok_count // experts
    share = width // tensor_size

    def swap(x):
        return lax.ppermute(x, "dp", [(0, 1), (1, 0)])

    def across(x, j):
        return lax.ppermute(x, "tensor", [(i, i ^ j) for i in range(tensor_size)])

    def shift(x, k):
        return lax.ppermute(x, "expert", [(i, (i + k) % experts) for i in range(experts)])

    def after(x, *others):
        return lax.optimization_barrier((x,) + others)[0]

    def spread(rows, *before):
        x, y = across(rows, 1), across(rows, 2)
        half_y, half_x = y[:, :share], x[:, share:]
        if before:
            half_y, half_x = after(half_y, *before), after(half_x, *before)
        return [rows, x, y, across(half_y, 1), across(half_x, 2)]

    def collect(blocks):
        got = [across(blocks[j], j) for j in (1, 2, 3)]
        terms = [b.astype(F32) for b in [blocks[0]] + got]
        return (terms[0] + terms[1] + (terms[2] + terms[3])).astype(BF16), got

    def collect_pair(pair, step):
        keep, send = pair
        got = across(send, step)
        last = across((keep[1].astype(F32) + got[1].astype(F32)).astype(BF16), 3 - step)
        return (keep[0].astype(F32) + got[0].astype(F32) + last.astype(F32)).astype(BF16), got

    def other_halves(kept):
        rows, acts = kept
        dims = (((1,), (1,)), ((0,), (0,)))
        return lax.dot_general(rows[:, :, width // 2 :], acts, dims, preferred_element_type=F32).astype(BF16)

    index, slot = expert_index.reshape(1, tok_count), slot_index.reshape(1, tok_count)
    gate = gate_prob.reshape(1, tok_count)
    up_own, down_own = up_weight[0], down_weight[0]
    weights = [up_own, swap(up_own), down_own, swap(down_own)]

    if experts == 4:
        shifts = [1, 3, 2]
        sends = place([capacity] * 3, shifts, capacity, index, slot, gate, tokens, grad_output)
        everything = 4 * capacity
        moved = [shift(rows, k) for rows, k in zip(sends, shifts)]
        own = [index, slot, gate, tokens, grad_output]
        kept, (pair,) = expert_rows(own, None, [(capacity, 1)], weights, everything, 0, None)
        near = spread(jnp.concatenate([after(moved[0], pair[0]), moved[1]], 0))
        far = after(moved[2], *near[1:3])
        far = [far, across(far, 1), across(far, 2), across(after(far, *near[3:]), 3)]
        kept, (blocks,) = expert_rows(None, [near], [(2 * capacity, None)], weights, everything, capacity, kept)
        total, got = collect(blocks)
        backs = [shift(total[:capacity], -1), shift(total[capacity:], -3)]
        kept, (blocks,) = expert_rows(None, [far], [(capacity, None)], weights, everything, 3 * capacity, kept)
        others = other_halves(kept)
        grads = weight_grads(*kept, swap(after(others, *got)))
        total, last = collect([blocks[0]] + [after(b, got[0], others) for b in blocks[1:]])
        back, _ = collect_pair([pair[0], after(pair[1], others)], 1)
        backs = [back] + backs + [after(shift(total, -2), *grads)]
        shifts = [0] + shifts
    else:
        rows = experts * capacity
        shifts = [None]

        def exchange(x):
            moved = lax.all_to_all(
                x.reshape(experts, capacity, x.shape[1]), "expert", split_axis=0, concat_axis=0, tiled=True
            )
            return moved.reshape(rows, x.shape[1])

        (send,) = place([rows], shifts, capacity, index, slot, gate, tokens, grad_output)
        kept, (blocks,) = expert_rows(None, [spread(exchange(send))], [(rows, None)], weights, rows, 0, None)
        others = other_halves(kept)
        grads = weight_grads(*kept, swap(others))
        total, _ = collect(blocks)
        backs = [exchange(total)]

    return unplace(shifts, capacity, index, slot, backs), grads[0][None], grads[1][None]


def solution(mesh):
    placed = (
        P(("expert", "dp"), None),
        P(("expert", "dp"), None),
        P(("expert", "dp")),
        P(("expert", "dp"), None),
        P(("expert", "dp"), None),
        P("expert", "dp", "tensor"),
        P("expert", "dp", "tensor"),
    )
    return jax.shard_map(
        local,
        mesh=mesh,
        in_specs=placed,
        out_specs=(
            P(("expert", "dp"), "tensor"),
            P("expert", "dp", "tensor"),
            P("expert", "dp", "tensor"),
        ),
        check_vma=False,
    )
```

```python
import functools

import jax
import jax.numpy as jnp
from jax import lax
from jax.experimental import pallas as pl
from jax.experimental.pallas import tpu as pltpu
from jax.sharding import PartitionSpec as P

F32 = jnp.float32
BF16 = jnp.bfloat16
I32 = jnp.int32
ANY = pl.BlockSpec(memory_space=pl.ANY)
VMEM = pl.BlockSpec(memory_space=pltpu.VMEM)
SMEM = pl.BlockSpec(memory_space=pltpu.SMEM)
HBM = pl.BlockSpec(memory_space=pltpu.HBM)
LIMIT = 22 * 2**20
SMALL = pl.CostEstimate(flops=1000, bytes_accessed=1000, transcendentals=0)


def dot(lhs, rhs, left=1, right=0):
    return lax.dot_general(lhs, rhs, (((left,), (right,)), ((), ())), preferred_element_type=F32)


def hits(position, first, rows):
    ids = lax.broadcasted_iota(I32, (rows, position.shape[1]), 0) + first
    return ids == position


def places(index, slot, capacity):
    return index[...] * capacity + slot[...]


def expert_first(k, capacity):
    experts = lax.axis_size("expert")
    return 0 if k is None else lax.rem(lax.axis_index("expert") + k, experts) * capacity


def gate_of(hit, gate):
    return jnp.sum(jnp.where(hit, gate, 0.0), axis=1, keepdims=True)


class Copies:
    def __init__(self, sem):
        self.sem, self.count = sem, 0

    def start(self, src, dst):
        copy = pltpu.make_async_copy(src, dst, self.sem.at[self.count])
        self.count += 1
        copy.start()
        return copy

    def rows(self, src, dst, count, pieces):
        step = count // pieces
        return [self.start(src.at[pl.ds(i * step, step), :], dst.at[pl.ds(i * step, step), :]) for i in range(pieces)]


def wait(copies):
    for copy in copies:
        copy.wait()


def place_kernel(spans, shifts, capacity, index, slot, gate, tokens, grad_output, *refs):
    sends, (index_in, slot_in, gate_in, tok, grad, packed, sem) = refs[: len(spans)], refs[len(spans) :]
    copies = Copies(sem)
    count, share = tok.shape
    columns = pl.ds(pl.multiple_of(lax.axis_index("tensor") * share, share), share)
    small = [copies.start(src, dst) for src, dst in ((index, index_in), (slot, slot_in), (gate, gate_in))]
    arrive = copies.rows(tokens.at[:, columns], tok, count, 4) + copies.rows(grad_output.at[:, columns], grad, count, 4)
    wait(small)
    position = places(index_in, slot_in, capacity)
    found = [hits(position, expert_first(k, capacity), rows) for k, rows in zip(shifts, spans)]
    scales = [gate_of(hit, gate_in[...]) for hit in found]
    hots = [hit.astype(BF16) for hit in found]
    wait(arrive)
    leave = []
    at = 0
    for hot, scale, rows, out in zip(hots, scales, spans, sends):
        packed[at : at + rows, :share] = dot(hot, tok[...]).astype(BF16)
        packed[at : at + rows, share:] = (dot(hot, grad[...]) * scale).astype(BF16)
        leave += copies.rows(packed.at[pl.ds(at, rows), :], out, rows, 2)
        at += rows
    wait(leave)


def place(spans, shifts, capacity, index, slot, gate, tokens, grad_output):
    count, width = tokens.shape
    share = width // 4
    buf = lambda *shape: pltpu.VMEM(shape, BF16)
    return pl.pallas_call(
        functools.partial(place_kernel, spans, shifts, capacity),
        out_shape=[jax.ShapeDtypeStruct((rows, 2 * share), BF16) for rows in spans],
        in_specs=[ANY] * 5,
        out_specs=[ANY] * len(spans),
        scratch_shapes=[
            pltpu.VMEM((1, count), I32), pltpu.VMEM((1, count), I32), pltpu.VMEM((1, count), F32),
            buf(count, share), buf(count, share), buf(sum(spans), 2 * share),
            pltpu.SemaphoreType.DMA((11 + 2 * len(spans),)),
        ],
        compiler_params=pltpu.CompilerParams(vmem_limit_bytes=54 * 2**20),
        cost_estimate=SMALL,
        name="place_rows",
    )(index, slot, gate, tokens, grad_output)


def gelu_parts(pre):
    c = 0.7978845608028654
    square = pre * pre
    th = jnp.tanh(c * (pre + 0.044715 * (pre * square)))
    half = 0.5 * (1.0 + th)
    return pre * half, half + 0.5 * pre * (1.0 - th * th) * (c + (3 * 0.044715 * c) * square)


def expert_kernel(chunks, base, groups, aliased, *refs):
    refs = list(refs)
    take = lambda n: [refs.pop(0) for _ in range(n)]
    slots = take(5) if chunks is None else [take(n) for n in chunks]
    up_halves, down_halves = take(2), take(2)
    take(aliased)
    kept_rows, kept_acts = take(2)
    targets = [take(4 if step is None else 2) for _, step in groups]
    tok, grad, up, down, hidden, slope, back = take(7)
    if chunks is None:
        tok_in, grad_in = take(2)
    copies = Copies(take(1)[0])
    rows, width = tok.shape
    half, share = width // 2, width // 4
    order = lax.axis_index("tensor") ^ (2 * lax.axis_index("dp"))
    arrive = []
    if chunks is None:
        mine = lax.axis_index("dp")
        count = tok_in.shape[0]
        for src, dst in zip(slots[3:], (tok_in, grad_in)):
            for i, start in enumerate((mine * half, (1 - mine) * half)):
                source = src.at[:, pl.ds(pl.multiple_of(start, half), half)]
                arrive += copies.rows(source, dst.at[:, pl.ds(i * half, half)], count, 2)
    else:
        at = 0
        for chunk in slots:
            n = chunk[0].shape[0]
            for j in range(4):
                columns = pl.ds(pl.multiple_of((order ^ j) * share, share), share)
                if j == 3 and len(chunk) == 5:
                    sources = chunk[3:]
                else:
                    sources = [chunk[j].at[:, pl.ds(i * share, share)] for i in range(2)]
                arrive += [copies.start(src, dst.at[pl.ds(at, n), columns]) for src, dst in zip(sources, (tok, grad))]
            at += n
    hid = hidden.shape[1]
    step = 256
    tiles = []
    for n in range(0, hid, step):
        cols = pl.ds(n, step)
        tiles.append([])
        for halves, dst in ((up_halves, up), (down_halves, down)):
            for i in range(2):
                tiles[-1].append(copies.start(halves[i].at[:, cols], dst.at[pl.ds(i * half, half), cols]))
    if chunks is None:
        hit = hits(places(slots[0], slots[1], rows), expert_first(0, rows), rows)
        hot, scale = hit.astype(BF16), gate_of(hit, slots[2][...])
    wait(arrive)
    if chunks is None:
        tok[...] = dot(hot, tok_in[...]).astype(BF16)
        grad[...] = (dot(hot, grad_in[...]) * scale).astype(BF16)
    mine = pl.ds(base, rows)
    leave = [copies.start(src, kept_rows.at[i, mine, :]) for i, src in enumerate((tok, grad))]
    for n, arrived in zip(range(0, hid, step), tiles):
        cols = slice(n, n + step)
        wait(arrived)
        pre = dot(tok[...], up[:, cols])
        hidden_grad = dot(grad[...], down[:, cols])
        act, deriv = gelu_parts(pre)
        hidden[:, cols] = act.astype(BF16)
        slope[:, cols] = (hidden_grad * deriv).astype(BF16)
    leave += [copies.start(src, kept_acts.at[i, mine, :]) for i, src in enumerate((slope, hidden))]
    for j in range(4):
        quarter = pl.ds(pl.multiple_of((order ^ j) * share, share), share)
        back[j] = dot(slope[...], up[quarter, :], 1, 1).astype(BF16)
        at = 0
        for (n, step), outs in zip(groups, targets):
            out = outs[j] if step is None else outs[(j & step) // step].at[(j & (3 - step)) // (3 - step)]
            leave.append(copies.start(back.at[j, pl.ds(at, n), :], out))
            at += n
    wait(leave)


def expert_rows(own, chunks, groups, weights, total_rows, base, kept):
    slots = own or sum(chunks, [])
    counts_in = None if own else [len(c) for c in chunks]
    rows = sum(n for n, _ in groups)
    half, hid = weights[0].shape
    width, share = 2 * half, half // 2
    operands = list(slots) + list(weights) + list(kept or [])
    aliases = {len(slots) + 4 + i: i for i in range(2)} if kept else {}
    shape = lambda *s: jax.ShapeDtypeStruct(s, BF16)
    buf = lambda *s: pltpu.VMEM(s, BF16)
    quarters = [[shape(n, share)] * 4 if step is None else [shape(2, n, share)] * 2 for n, step in groups]
    counts = [len(q) for q in quarters]
    out = pl.pallas_call(
        functools.partial(expert_kernel, counts_in, base, groups, len(aliases)),
        out_shape=[shape(2, total_rows, width), shape(2, total_rows, hid)] + sum(quarters, []),
        in_specs=([VMEM] * 3 if own else [ANY] * 3) + [ANY] * (len(operands) - 3),
        out_specs=[ANY] * (2 + sum(counts)),
        scratch_shapes=[
            buf(rows, width), buf(rows, width), buf(width, hid), buf(width, hid),
            buf(rows, hid), buf(rows, hid), buf(4, rows, share),
        ]
        + ([buf(*own[3].shape)] * 2 if own else [])
        + [pltpu.SemaphoreType.DMA((16 + 4 * (hid // 256) + 4 * len(groups) + 4,))],
        input_output_aliases=aliases,
        compiler_params=pltpu.CompilerParams(vmem_limit_bytes=LIMIT + rows * 2**15),
        cost_estimate=pl.CostEstimate(
            flops=6 * rows * width * hid, bytes_accessed=4 * width * hid + 8 * rows * width, transcendentals=rows * hid
        ),
        name="expert_rows",
    )(*operands)
    starts = [2 + sum(counts[:i]) for i in range(len(counts))]
    return list(out[:2]), [list(out[i : i + n]) for i, n in zip(starts, counts)]


def unplace_kernel(spans, shifts, capacity, index, slot, *refs):
    out = refs[-1]
    position = places(index, slot, capacity)
    total = None
    for k, rows, back in zip(shifts, spans, refs[:-1]):
        hot = hits(position, expert_first(k, capacity), rows).astype(BF16)
        part = dot(hot, back[...], 0, 0)
        total = part if total is None else total + part
    out[...] = total.astype(BF16)


def unplace(shifts, capacity, index, slot, backs):
    spans = [b.shape[0] for b in backs]
    count, share = index.shape[1], backs[0].shape[1]
    return pl.pallas_call(
        functools.partial(unplace_kernel, spans, shifts, capacity),
        out_shape=jax.ShapeDtypeStruct((count, share), BF16),
        in_specs=[VMEM] * (2 + len(backs)),
        out_specs=VMEM,
        compiler_params=pltpu.CompilerParams(vmem_limit_bytes=LIMIT),
        cost_estimate=SMALL,
        name="unplace_rows",
    )(index, slot, *backs)


def weight_grad_kernel(rows, acts, got, up_out, down_out, total, sem):
    copies = Copies(sem)
    half = total.shape[1]
    step = 256
    leave = []
    for i, out in enumerate((up_out, down_out)):
        for n in range(0, half, step):
            mine = dot(rows[i, :, n : n + step], acts[i], 0, 0).astype(BF16).astype(F32)
            total[i, n : n + step, :] = (mine + got[i, n : n + step, :].astype(F32)).astype(BF16)
            leave.append(copies.start(total.at[i, pl.ds(n, step), :], out.at[pl.ds(n, step), :]))
    wait(leave)


def weight_grads(kept_rows, kept_acts, got):
    _, count, width = kept_rows.shape
    hid = kept_acts.shape[2]
    half = width // 2
    return pl.pallas_call(
        weight_grad_kernel,
        out_shape=[jax.ShapeDtypeStruct((half, hid), BF16)] * 2,
        grid=(1,),
        in_specs=[
            pl.BlockSpec((2, count, half), lambda i: (0, 0, 0)),
            pl.BlockSpec((2, count, hid), lambda i: (0, 0, 0)),
            pl.BlockSpec((2, half, hid), lambda i: (0, 0, 0)),
        ],
        out_specs=[ANY] * 2,
        scratch_shapes=[pltpu.VMEM((2, half, hid), BF16), pltpu.SemaphoreType.DMA((2 * (half // 128),))],
        compiler_params=pltpu.CompilerParams(vmem_limit_bytes=40 * 2**20),
        cost_estimate=SMALL,
        name="weight_grads",
    )(kept_rows, kept_acts, got)


def local(tokens, grad_output, gate_prob, expert_index, slot_index, up_weight, down_weight):
    experts = lax.axis_size("expert")
    tensor_size = lax.axis_size("tensor")
    tok_count, width = tokens.shape
    capacity = 2 * tok_count // experts
    share = width // tensor_size

    def swap(x):
        return lax.ppermute(x, "dp", [(0, 1), (1, 0)])

    def across(x, j):
        return lax.ppermute(x, "tensor", [(i, i ^ j) for i in range(tensor_size)])

    def shift(x, k):
        return lax.ppermute(x, "expert", [(i, (i + k) % experts) for i in range(experts)])

    def after(x, *others):
        return lax.optimization_barrier((x,) + others)[0]

    def spread(rows, *before):
        x, y = across(rows, 1), across(rows, 2)
        half_y, half_x = y[:, :share], x[:, share:]
        if before:
            half_y, half_x = after(half_y, *before), after(half_x, *before)
        return [rows, x, y, across(half_y, 1), across(half_x, 2)]

    def collect(blocks):
        got = [across(blocks[j], j) for j in (1, 2, 3)]
        terms = [b.astype(F32) for b in [blocks[0]] + got]
        return (terms[0] + terms[1] + (terms[2] + terms[3])).astype(BF16), got

    def collect_pair(pair, step):
        keep, send = pair
        got = across(send, step)
        last = across((keep[1].astype(F32) + got[1].astype(F32)).astype(BF16), 3 - step)
        return (keep[0].astype(F32) + got[0].astype(F32) + last.astype(F32)).astype(BF16), got

    def other_halves(kept):
        rows, acts = kept
        dims = (((1,), (1,)), ((0,), (0,)))
        return lax.dot_general(rows[:, :, width // 2 :], acts, dims, preferred_element_type=F32).astype(BF16)

    index, slot = expert_index.reshape(1, tok_count), slot_index.reshape(1, tok_count)
    gate = gate_prob.reshape(1, tok_count)
    up_own, down_own = up_weight[0], down_weight[0]
    weights = [up_own, swap(up_own), down_own, swap(down_own)]

    if experts == 4:
        shifts = [1, 3, 2]
        sends = place([capacity] * 3, shifts, capacity, index, slot, gate, tokens, grad_output)
        everything = 4 * capacity
        moved = [shift(rows, k) for rows, k in zip(sends, shifts)]
        own = [index, slot, gate, tokens, grad_output]
        kept, (pair,) = expert_rows(own, None, [(capacity, 1)], weights, everything, 0, None)
        near = spread(jnp.concatenate([after(moved[0], pair[0]), moved[1]], 0))
        far = after(moved[2], *near[1:3])
        far = [far, across(far, 1), across(far, 2), across(after(far, *near[3:]), 3)]
        kept, (blocks,) = expert_rows(None, [near], [(2 * capacity, None)], weights, everything, capacity, kept)
        total, got = collect(blocks)
        backs = [shift(total[:capacity], -1), shift(total[capacity:], -3)]
        kept, (blocks,) = expert_rows(None, [far], [(capacity, None)], weights, everything, 3 * capacity, kept)
        others = other_halves(kept)
        grads = weight_grads(*kept, swap(after(others, *got)))
        total, last = collect([blocks[0]] + [after(b, got[0], others) for b in blocks[1:]])
        back, _ = collect_pair([pair[0], after(pair[1], others)], 1)
        backs = [back] + backs + [after(shift(total, -2), *grads)]
        shifts = [0] + shifts
    else:
        rows = experts * capacity
        shifts = [None]

        def exchange(x):
            moved = lax.all_to_all(
                x.reshape(experts, capacity, x.shape[1]), "expert", split_axis=0, concat_axis=0, tiled=True
            )
            return moved.reshape(rows, x.shape[1])

        (send,) = place([rows], shifts, capacity, index, slot, gate, tokens, grad_output)
        kept, (blocks,) = expert_rows(None, [spread(exchange(send))], [(rows, None)], weights, rows, 0, None)
        others = other_halves(kept)
        grads = weight_grads(*kept, swap(others))
        total, _ = collect(blocks)
        backs = [exchange(total)]

    return unplace(shifts, capacity, index, slot, backs), grads[0][None], grads[1][None]


def solution(mesh):
    placed = (
        P(("expert", "dp"), None),
        P(("expert", "dp"), None),
        P(("expert", "dp")),
        P(("expert", "dp"), None),
        P(("expert", "dp"), None),
        P("expert", "dp", "tensor"),
        P("expert", "dp", "tensor"),
    )
    return jax.shard_map(
        local,
        mesh=mesh,
        in_specs=placed,
        out_specs=(
            P(("expert", "dp"), "tensor"),
            P("expert", "dp", "tensor"),
            P("expert", "dp", "tensor"),
        ),
        check_vma=False,
    )
```
